128 devices in a mesh: pts: 32 (over z, x, core), exp: 4 (over y).
Axes of the slice: x: 4, y: 4, z: 4, core: 2. Of those that a mesh axis runs over, the one named last changes fastest.
Arguments:
- tokens: bfloat16 [32768, 256], P('pts'), may hold values from -6 to 6
- coords: float32 [3, 32768], P(None, 'pts'), may hold values from -1 to 1
- keep: int32 [32768], P('pts'), may hold values 0 or 1
- cotangent: bfloat16 [32768, 256], P('pts'), may hold values from -6 to 6
- w_query: bfloat16 [256, 256], replicated, may hold values from -0.375 to 0.375
- w_key: bfloat16 [256, 256], replicated, may hold values from -0.375 to 0.375
- w_value: bfloat16 [256, 256], replicated, may hold values from -0.375 to 0.375
- w_geo: float32 [3, 64], replicated, may hold values from -3.5 to 3.5
- b_geo: float32 [64], replicated, may hold values from -1 to 1
- w_route: float32 [64, 8], replicated, may hold values from -0.25 to 0.25
- w_in: bfloat16 [8, 256, 1024], P('exp'), may hold values from -0.375 to 0.375
- w_out: bfloat16 [8, 1024, 256], P('exp'), may hold values from -0.1875 to 0.1875
Outputs:
- grad_x: bfloat16 [32768, 256], P('pts')
- grad_wq: float32 [256, 256], replicated
- grad_wk: float32 [256, 256], replicated
- grad_wv: float32 [256, 256], replicated
- grad_w_in: float32 [8, 256, 1024], P('exp')
- grad_w_out: float32 [8, 1024, 256], P('exp')
- grad_route: float32 [64, 8], P(None, 'exp')
The draws below stay inside these ranges and needn't reach their ends.
All inputs are finite; a program needn't handle non-finite values. No bound on the sum of `keep` on one device may be relied on, other than what follows from the above.
Results may differ from the reference program's by a relative error of at most 0.0064.
Values may be sent and summed in bfloat16 or wider, within the bound.
No kernel may reach another device: no remote copies, remote signals or barrier semaphores. Data moves between devices by JAX's collectives and lax.ppermute only.
A program may use at most 128 MiB of HBM per device.

```python
import jax
import jax.numpy as jnp
from jax import lax

D = 256
HEADS = 8
HEAD_DIM = 32
FH = 1024
GH = 64
EXPERTS = 8
TOK_DEV = 1024
TOKENS = 32768


def draw_tokens(key, part):
    key = jax.random.fold_in(key, 11)
    keys = jax.random.split(key, 3)
    blocks = TOKENS // TOK_DEV
    common = jax.random.normal(keys[0], (1, D), jnp.float32)
    per_block = jax.random.normal(keys[1], (blocks, D), jnp.float32)
    offset = jnp.repeat(0.35 * (common + per_block), TOK_DEV, axis=0)
    jitter = jax.random.normal(keys[2], (TOKENS, D), jnp.float32)
    return jnp.clip(offset + jitter, -6.0, 6.0).astype(jnp.bfloat16)


def place_ends(values, stream_key, low, largest):
    longest = values.shape.index(max(values.shape))
    spots = []
    for shift in (0, 1):
        where = [jax.random.randint(jax.random.fold_in(stream_key, axis), (), 0, length) for axis, length in enumerate(values.shape)]
        where[longest] = (where[longest] + shift) % values.shape[longest]
        spots.append(tuple(where))
    return values.at[spots[0]].set(low).at[spots[1]].set(largest)


def level_of(key, dims, cuts, least, largest):
    def one(axis_at, parts):
        heights = jax.random.uniform(jax.random.fold_in(jax.random.fold_in(key, 6), axis_at), (parts,), jnp.float32, least / len(cuts), largest / len(cuts))
        return jnp.repeat(jnp.exp(heights), dims[axis_at] // parts).reshape((-1,) + (1,) * (len(dims) - axis_at - 1))

    factor_of = one(*cuts[0])
    for cut in cuts[1:]:
        factor_of = factor_of * one(*cut)
    return factor_of


def scatter_about(stream_key, dims, width, bound, pieces=(), held_as=jnp.bfloat16):
    loudness = level_of(stream_key, dims, pieces, -0.22, 0.18) if pieces else 1.0
    values = jax.random.normal(stream_key, dims, jnp.float32) * width * loudness
    return jnp.minimum(jnp.maximum(values, -bound), bound).astype(held_as)


def setup_inputs(seed: int = 0) -> dict:
    key_list = jax.random.split(jax.random.key(seed), 13)
    return {
        "tokens": draw_tokens(jax.random.fold_in(key_list[12], 71), 0),
        "coords": jnp.clip(jax.random.uniform(key_list[1], (3, TOKENS), jnp.float32, -1.0, 1.0) * level_of(key_list[1], (3, TOKENS), ((1, 32),), -0.4, 0.0), -1.0, 1.0),
        "keep": place_ends((jax.random.randint(key_list[2], (TOKENS,), 0, 8) < 7).astype(jnp.int32), jax.random.fold_in(key_list[2], 1), 0, 1),
        "cotangent": scatter_about(key_list[3], (TOKENS, D), 1.0, 6.0, ((0, 32),)),
        "w_query": scatter_about(key_list[4], (D, D), D ** -0.5, 0.375),
        "w_key": scatter_about(key_list[5], (D, D), D ** -0.5, 0.375),
        "w_value": scatter_about(key_list[6], (D, D), D ** -0.5, 0.375),
        "w_geo": scatter_about(key_list[7], (3, GH), 3 ** -0.5, 3.5, (), jnp.float32),
        "b_geo": jnp.clip(jax.random.uniform(key_list[8], (GH,), jnp.float32, -1.0, 1.0), -1.0, 1.0),
        "w_route": jnp.clip(jax.random.uniform(key_list[9], (GH, EXPERTS), jnp.float32, -0.25, 0.25), -0.25, 0.25),
        "w_in": scatter_about(key_list[10], (EXPERTS, D, FH), D ** -0.5, 0.375, ((0, 4),)),
        "w_out": scatter_about(key_list[11], (EXPERTS, FH, D), FH ** -0.5, 0.1875, ((0, 4),)),
    }


HIGH = lax.Precision.HIGHEST

def phi(z):
    return jnp.where(z > 0, z + 1.0, jnp.exp(jnp.minimum(z, 0.0)))

def phi_slope(z):
    return jnp.where(z > 0, 1.0, jnp.exp(jnp.minimum(z, 0.0)))

def gelu_tanh(u):
    return jax.nn.gelu(u, approximate=True)

def reference(tokens, coords, keep, cotangent, w_query, w_key, w_value, w_geo, b_geo, w_route, w_in, w_out):
    count = tokens.shape[0]
    keepf = keep.astype(jnp.float32)
    qpre = jnp.dot(tokens, w_query, preferred_element_type=jnp.float32)
    kpre = jnp.dot(tokens, w_key, preferred_element_type=jnp.float32)
    vpre = jnp.dot(tokens, w_value, preferred_element_type=jnp.float32)
    query = phi(qpre).astype(jnp.bfloat16)
    keyed = (phi(kpre) * keepf[:, None]).astype(jnp.bfloat16)
    value = vpre.astype(jnp.bfloat16)
    qf = query.astype(jnp.float32).reshape(count, HEADS, HEAD_DIM)
    kf = keyed.astype(jnp.float32).reshape(count, HEADS, HEAD_DIM)
    vf = value.astype(jnp.float32).reshape(count, HEADS, HEAD_DIM)
    kv = jnp.einsum('thi,thj->hij', kf, vf, precision=HIGH)
    ks = lax.optimization_barrier(jnp.sum(kf, axis=0))
    num = jnp.einsum('thi,hij->thj', qf, kv, precision=HIGH)
    den = jnp.einsum('thi,hi->th', qf, ks, precision=HIGH)
    attn = num / den[..., None]
    mid = (tokens.astype(jnp.float32) + attn.reshape(count, D)).astype(jnp.bfloat16)
    hidden_geo = jnp.tanh(jnp.dot(coords.T, w_geo, precision=HIGH) + b_geo[None, :])
    expo = jnp.exp(jnp.dot(hidden_geo, w_route, precision=HIGH))
    gates = expo / lax.optimization_barrier(jnp.sum(expo, axis=1, keepdims=True))
    dyv = cotangent * keep[:, None].astype(jnp.bfloat16)
    dyf = dyv.astype(jnp.float32)
    dmid = dyf
    dg_cols = []
    gw1_list = []
    gw2_list = []
    for expert in range(EXPERTS):
        upre = jnp.dot(mid, w_in[expert], preferred_element_type=jnp.float32)
        act, pull = jax.vjp(gelu_tanh, upre)
        act_b = act.astype(jnp.bfloat16)
        outf = jnp.dot(act_b, w_out[expert], preferred_element_type=jnp.float32)
        dg_cols.append(lax.optimization_barrier(jnp.sum(dyf * outf, axis=1)))
        dfe = (gates[:, expert:expert + 1] * dyf).astype(jnp.bfloat16)
        gw2_list.append(jnp.dot(act_b.T, dfe, preferred_element_type=jnp.float32))
        dact = jnp.dot(dfe, w_out[expert].T, preferred_element_type=jnp.float32)
        due = pull(dact)[0].astype(jnp.bfloat16)
        gw1_list.append(jnp.dot(mid.T, due, preferred_element_type=jnp.float32))
        dmid = dmid + jnp.dot(due, w_in[expert].T, preferred_element_type=jnp.float32)
    dgate = jnp.stack(dg_cols, axis=1)
    gsum = lax.optimization_barrier(jnp.sum(gates * dgate, axis=1, keepdims=True))
    dlogit = gates * (dgate - gsum)
    grad_route = jnp.dot(hidden_geo.T, dlogit, precision=HIGH)
    dmh = dmid.reshape(count, HEADS, HEAD_DIM)
    dnum = dmh / den[..., None]
    dden = -lax.optimization_barrier(jnp.sum(dmh * attn, axis=-1)) / den
    dkv = jnp.einsum('thi,thj->hij', qf, dnum, precision=HIGH)
    dks = jnp.einsum('th,thi->hi', dden, qf, precision=HIGH)
    dq = jnp.einsum('thj,hij->thi', dnum, kv, precision=HIGH) + dden[..., None] * ks[None]
    dk = (jnp.einsum('thj,hij->thi', vf, dkv, precision=HIGH) + dks[None]) * keepf[:, None, None]
    dv = jnp.einsum('thi,hij->thj', kf, dkv, precision=HIGH)
    dqp = (dq.reshape(count, D) * phi_slope(qpre)).astype(jnp.bfloat16)
    dkp = (dk.reshape(count, D) * phi_slope(kpre)).astype(jnp.bfloat16)
    dvp = dv.reshape(count, D).astype(jnp.bfloat16)
    grad_wq = jnp.dot(tokens.T, dqp, preferred_element_type=jnp.float32)
    grad_wk = jnp.dot(tokens.T, dkp, preferred_element_type=jnp.float32)
    grad_wv = jnp.dot(tokens.T, dvp, preferred_element_type=jnp.float32)
    back = jnp.dot(dqp, w_query.T, preferred_element_type=jnp.float32)
    back = back + jnp.dot(dkp, w_key.T, preferred_element_type=jnp.float32)
    back = back + jnp.dot(dvp, w_value.T, preferred_element_type=jnp.float32)
    grad_x = (dmid + back).astype(jnp.bfloat16)
    return (grad_x, grad_wq, grad_wk, grad_wv, jnp.stack(gw1_list), jnp.stack(gw2_list), grad_route)
```

```python
import functools

import jax
import jax.numpy as jnp
from jax import lax
from jax.experimental import pallas as pl
from jax.experimental.pallas import tpu as pltpu
from jax.sharding import PartitionSpec as P


D = 256
HD = 32
FH = 1024
N1 = 1024
N2 = 2048
TB = 512
HC = 256
F32 = jnp.float32
BF = jnp.bfloat16
VMEM_LIMIT = 60 * 1024 * 1024


def mm(a, b):
    return jnp.dot(a, b, preferred_element_type=F32)


def mm_nt(a, b):
    return lax.dot_general(a, b, (((1,), (1,)), ((), ())), preferred_element_type=F32)


def split2(x):
    hi = x.astype(BF)
    return hi, (x - hi.astype(F32)).astype(BF)


def flip(x):
    return x.astype(F32).T


def head_mask(rows, cols):
    r = lax.broadcasted_iota(jnp.int32, (rows, cols), 0) // HD
    c = lax.broadcasted_iota(jnp.int32, (rows, cols), 1) // HD
    return r == c


def pack_heads(full):
    full = jnp.where(head_mask(D, D), full, 0.0)
    parts = []
    for g in range(2):
        cols = full[:, 128 * g : 128 * g + 128]
        parts.append(sum(cols[128 * g + HD * h : 128 * g + HD * h + HD] for h in range(4)))
    return parts


def unpack_heads(packed):
    mask = head_mask(128, 128)
    zero = jnp.zeros((128, 128), F32)
    blocks = []
    for g in range(2):
        piece = packed[HD * g : HD * g + HD]
        blocks.append(jnp.where(mask, jnp.concatenate([piece] * 4, axis=0), 0.0))
    top = jnp.concatenate([blocks[0], zero], axis=1)
    low = jnp.concatenate([zero, blocks[1]], axis=1)
    return jnp.concatenate([top, low], axis=0)


def row_of(packed, first):
    return jnp.concatenate([packed[first : first + 8], packed[first + 8 : first + 16]], axis=1)


def as_column(row):
    r = lax.broadcasted_iota(jnp.int32, (D, D), 0)
    c = lax.broadcasted_iota(jnp.int32, (D, D), 1)
    return jnp.sum(jnp.where(r == c, row, 0.0), axis=1, keepdims=True)


def params():
    return pltpu.CompilerParams(vmem_limit_bytes=VMEM_LIMIT)


def cost(flops, nbytes):
    return pl.CostEstimate(flops=int(flops), bytes_accessed=int(nbytes), transcendentals=0)


def keys_kernel(tok_ref, keep_ref, wk_ref, wv_ref, km_ref, v_ref, slope_ref, msg_ref):
    tok = tok_ref[...]
    kpre = mm_nt(flip(wk_ref[...]).astype(BF), tok)
    val = mm_nt(flip(wv_ref[...]).astype(BF), tok).astype(BF)
    keep = keep_ref[...].astype(F32)
    low = jnp.exp(jnp.minimum(kpre, 0.0))
    km = (keep * jnp.where(kpre > 0, kpre + 1.0, low)).astype(BF)
    km_ref[...] = km
    v_ref[...] = val
    slope_ref[...] = keep * jnp.where(kpre > 0, 1.0, low)
    parts = pack_heads(mm_nt(val, km))
    msg_ref[0:32, :] = parts[0]
    msg_ref[32:64, :] = parts[1]
    ks = mm_nt(jnp.ones((8, N1), BF), km)
    msg_ref[64:72, :] = ks[:, :128]
    msg_ref[72:80, :] = ks[:, 128:]


def keys_call(tokens, keep_row, wk, wv):
    return pl.pallas_call(
        keys_kernel,
        out_shape=(
            jax.ShapeDtypeStruct((D, N1), BF),
            jax.ShapeDtypeStruct((D, N1), BF),
            jax.ShapeDtypeStruct((D, N1), F32),
            jax.ShapeDtypeStruct((80, 128), F32),
        ),
        compiler_params=params(),
        cost_estimate=cost(4e8, 3e6),
        name="keys",
    )(tokens, keep_row, wk, wv)


def query_kernel(tok_ref, oth_ref, wq_ref, tokt_ref, q_ref):
    wqt = flip(wq_ref[...]).astype(BF)
    for half, ref in enumerate((tok_ref, oth_ref)):
        tok = ref[...]
        cols = slice(N1 * half, N1 * half + N1)
        tokt_ref[:, cols] = flip(tok).astype(BF)
        pre = mm_nt(wqt, tok)
        phi = jnp.where(pre > 0, pre + 1.0, jnp.exp(jnp.minimum(pre, 0.0)))
        q_ref[:, cols] = phi.astype(BF)


def query_call(tokens, tokens_o, wq):
    return pl.pallas_call(
        query_kernel,
        out_shape=(jax.ShapeDtypeStruct((D, N2), BF), jax.ShapeDtypeStruct((D, N2), BF)),
        compiler_params=params(),
        cost_estimate=cost(4e8, 3e6),
        name="queries",
    )(tokens, tokens_o, wq)


def back_kernel(at_ref, cot_ref, oth_ref, ck_ref, cko_ref, win_ref, wout_ref, dyt_ref, back_ref, wint_ref):
    for half, (ref, keep_ref) in enumerate(((cot_ref, ck_ref), (oth_ref, cko_ref))):
        cot = ref[...]
        keep = keep_ref[3:4, :]
        cols = slice(N1 * half, N1 * half + N1)
        dyt_ref[:, cols] = (flip(cot) * keep).astype(BF)
        for j in range(0, FH, HC):
            back_ref[j : j + HC, cols] = (mm_nt(wout_ref[0, j : j + HC, :], cot) * keep).astype(BF)
    wint_ref[...] = flip(win_ref[0]).astype(BF)


def back_call(at, cot, cot_o, ck, ck_o, w_in, w_out):
    whole = lambda shape: pl.BlockSpec(shape, lambda i, at: (0,) * len(shape))
    return pl.pallas_call(
        back_kernel,
        grid_spec=pltpu.PrefetchScalarGridSpec(
            num_scalar_prefetch=1,
            grid=(1,),
            in_specs=[
                whole((N1, D)),
                whole((N1, D)),
                whole((4, N1)),
                whole((4, N1)),
                pl.BlockSpec((1, D, FH), lambda i, at: (at[0], 0, 0)),
                pl.BlockSpec((1, FH, D), lambda i, at: (at[0], 0, 0)),
            ],
            out_specs=[whole((D, N2)), whole((FH, N2)), whole((FH, D))],
        ),
        out_shape=(
            jax.ShapeDtypeStruct((D, N2), BF),
            jax.ShapeDtypeStruct((FH, N2), BF),
            jax.ShapeDtypeStruct((FH, D), BF),
        ),
        compiler_params=params(),
        cost_estimate=cost(11e8, 8e6),
        name="cotangent_back",
    )(at, cot, cot_o, ck, ck_o, w_in, w_out)


def gate_kernel(ck_ref, cko_ref, wgeo_ref, bgeo_ref, wroute_ref, r_ref, g_ref):
    for half, ref in enumerate((ck_ref, cko_ref)):
        cols = slice(N1 * half, N1 * half + N1)
        pre = bgeo_ref[...]
        for k in range(3):
            pre = pre + wgeo_ref[:, k : k + 1] * ref[k : k + 1, :]
        r = jnp.tanh(pre)
        r_ref[:, cols] = r
        logit = jnp.dot(wroute_ref[...], r, precision=lax.Precision.HIGHEST, preferred_element_type=F32)
        expo = jnp.exp(logit)
        g_ref[:, cols] = expo / jnp.sum(expo, axis=0, keepdims=True)


def gate_call(ck, ck_o, wgeo_t, bgeo, wroute_t):
    return pl.pallas_call(
        gate_kernel,
        out_shape=(jax.ShapeDtypeStruct((64, N2), F32), jax.ShapeDtypeStruct((8, N2), F32)),
        compiler_params=params(),
        cost_estimate=cost(1e7, 1e6),
        name="gate",
    )(ck, ck_o, wgeo_t, bgeo, wroute_t)


GELU_A = 0.7978845608028654
GELU_B = 0.7978845608028654 * 0.044715


def expert_kernel(
    at_ref, msg_ref, tokt_ref, q_ref, dyt_ref, back_ref, g_ref, r_ref, win_ref, wint_ref,
    own_ref, oth_ref, msg2_ref, p0_ref, p1_ref, p2_ref, p3_ref,
    kvh, kvl, ksh, ksl, gw1, gw2, dkv, dks, route,
):
    step = pl.program_id(0)
    expert = at_ref[1]

    @pl.when(step == 0)
    def _():
        hi, lo = split2(unpack_heads(msg_ref[0:64, :]))
        kvh[...] = hi
        kvl[...] = lo
        ks = row_of(msg_ref, 64)[0:1]
        hi, lo = split2(jnp.where(head_mask(D, D), ks, 0.0))
        ksh[...] = hi
        ksl[...] = lo
        gw1[...] = jnp.zeros_like(gw1)
        gw2[...] = jnp.zeros_like(gw2)
        dkv[...] = jnp.zeros_like(dkv)
        dks[...] = jnp.zeros_like(dks)
        route[...] = jnp.zeros_like(route)

    q = q_ref[...]
    num = mm(kvh[...], q) + mm(kvl[...], q)
    rden = 1.0 / (mm(ksh[...], q) + mm(ksl[...], q))
    attn = num * rden
    mid = (tokt_ref[...].astype(F32) + attn).astype(BF)
    gates = g_ref[...]
    mine = lax.broadcasted_iota(jnp.int32, gates.shape, 0) == expert
    gate = jnp.sum(jnp.where(mine, gates, 0.0), axis=0, keepdims=True)
    dyt = dyt_ref[...].astype(F32)
    df = (dyt * gate).astype(BF)
    first = jnp.logical_and(at_ref[2] == 0, step < N1 // TB)
    dmid = dyt * jnp.where(first, 1.0, 0.0)
    stat = jnp.zeros((1, TB), F32)
    for j in range(0, FH, HC):
        rows = slice(j, j + HC)
        u = mm(wint_ref[rows, :], mid)
        u2 = u * u
        t = jnp.tanh(u * (GELU_A + GELU_B * u2))
        half = 0.5 + 0.5 * t
        act = (u * half).astype(BF)
        slope = half + 0.5 * u * (1.0 - t * t) * (GELU_A + 3.0 * GELU_B * u2)
        back = back_ref[rows, :].astype(F32)
        stat = stat + jnp.sum(act.astype(F32) * back, axis=0, keepdims=True)
        du = (back * gate * slope).astype(BF)
        gw2[rows, :] += mm_nt(act, df)
        gw1[rows, :] += mm_nt(du, mid)
        dmid = dmid + mm(win_ref[0, :, rows], du)
    stat = stat * gate
    turn = (jnp.where(mine, 1.0, 0.0) - gates) * stat
    route[...] += lax.dot_general(
        turn, r_ref[...], (((1,), (1,)), ((), ())), precision=lax.Precision.HIGHEST, preferred_element_type=F32
    )
    dnum = dmid * rden
    dden = -jnp.sum((dnum * attn).reshape(8, HD, TB), axis=1)
    hi, lo = split2(dnum)
    dkv[...] += mm_nt(q, hi) + mm_nt(q, lo)
    hi, lo = split2(dden)
    dks[...] += mm_nt(hi, q) + mm_nt(lo, q)

    @pl.when(step < N1 // TB)
    def _():
        own_ref[...] = dmid.astype(BF)

    @pl.when(step >= N1 // TB)
    def _():
        oth_ref[...] = dmid.astype(BF)

    @pl.when(step == N2 // TB - 1)
    def _():
        x, z = at_ref[3], at_ref[4]
        for d, ref in enumerate((p0_ref, p1_ref, p2_ref, p3_ref)):
            for e in range(4):
                piece = lax.rem(x + d, 4) * 4 + lax.rem(z + e, 4)
                rows = pl.ds(pl.multiple_of(piece * 64, 64), 64)
                ref[e, 0:64, :] = gw1[rows, :].astype(BF)
                ref[e, 64:128, :] = gw2[rows, :].astype(BF)
        parts = pack_heads(dkv[...])
        msg2_ref[0:32, :] = parts[0]
        msg2_ref[32:64, :] = parts[1]
        r = lax.broadcasted_iota(jnp.int32, (8, D), 0)
        c = lax.broadcasted_iota(jnp.int32, (8, D), 1) // HD
        sums = jnp.where(r == c, dks[...], 0.0)
        msg2_ref[64:72, :] = sums[:, :128]
        msg2_ref[72:80, :] = sums[:, 128:]
        msg2_ref[80:88, :] = jnp.concatenate([route[...], jnp.zeros((8, 64), F32)], axis=1)


def expert_call(at, msg, tokt, q, dyt, back, g, r, w_in, wint):
    steps, own = N2 // TB, N1 // TB
    whole = lambda shape: pl.BlockSpec(shape, lambda i, at: (0,) * len(shape))
    by_points = lambda rows: pl.BlockSpec((rows, TB), lambda i, at: (0, i))
    return pl.pallas_call(
        expert_kernel,
        grid_spec=pltpu.PrefetchScalarGridSpec(
            num_scalar_prefetch=1,
            grid=(steps,),
            in_specs=[
                whole((80, 128)),
                by_points(D),
                by_points(D),
                by_points(D),
                by_points(FH),
                by_points(8),
                by_points(64),
                pl.BlockSpec((1, D, FH), lambda i, at: (at[0], 0, 0)),
                whole((FH, D)),
            ],
            out_specs=[
                pl.BlockSpec((D, TB), lambda i, at: (0, jnp.minimum(i, own - 1))),
                pl.BlockSpec((D, TB), lambda i, at: (0, jnp.maximum(i - own, 0))),
                whole((88, 128)),
            ]
            + [whole((4, 128, D))] * 4,
            scratch_shapes=[pltpu.VMEM((D, D), BF)] * 4
            + [
                pltpu.VMEM((FH, D), F32),
                pltpu.VMEM((FH, D), F32),
                pltpu.VMEM((D, D), F32),
                pltpu.VMEM((8, D), F32),
                pltpu.VMEM((8, 64), F32),
            ],
        ),
        out_shape=(
            jax.ShapeDtypeStruct((D, N1), BF),
            jax.ShapeDtypeStruct((D, N1), BF),
            jax.ShapeDtypeStruct((88, 128), F32),
        )
        + (jax.ShapeDtypeStruct((4, 128, D), BF),) * 4,
        compiler_params=params(),
        cost_estimate=cost(6e9, 12e6),
        name="expert",
    )(at, msg, tokt, q, dyt, back, g, r, w_in, wint)


def back_query_kernel(at_ref, d0, d1, d2, d3, msg_ref, tokt_ref, q_ref, wq_ref, gx_ref, gq_ref):
    dmid = (d0[...].astype(F32) + d1[...].astype(F32)) + (d2[...].astype(F32) + d3[...].astype(F32))
    q = q_ref[...]
    tokt = tokt_ref[...]
    kvt = unpack_heads(msg_ref[0:64, :])
    kvth, kvtl = split2(kvt)
    kvh, kvl = split2(kvt.T)
    ks = row_of(msg_ref, 64)[0:1]
    mask = head_mask(D, D)
    ksh, ksl = split2(jnp.where(mask, ks, 0.0))
    kch, kcl = split2(jnp.where(mask, as_column(ks), 0.0))
    num = mm(kvth, q) + mm(kvtl, q)
    rden = 1.0 / (mm(ksh, q) + mm(ksl, q))
    attn = num * rden
    dnum = dmid * rden
    nh, nl = split2(dnum)
    zh, zl = split2(dnum * attn)
    dq = (mm(kvh, nh) - mm(kch, zh)) + (mm(kvl, nh) - mm(kcl, zh)) + (mm(kvh, nl) - mm(kch, zl))
    wq = wq_ref[...]
    pre = mm(flip(wq).astype(BF), tokt)
    dqp = (dq * jnp.where(pre > 0, 1.0, jnp.exp(jnp.minimum(pre, 0.0)))).astype(BF)
    gx_ref[...] = dmid + mm(wq, dqp)
    rows = pl.ds(pl.multiple_of(at_ref[2] * 64, 64), 64)
    gq_ref[...] = mm_nt(tokt_ref[rows, :], dqp)


def back_query_call(at, dm, msg, tokt, q, wq):
    whole = lambda shape: pl.BlockSpec(shape, lambda i, at: (0,) * len(shape))
    return pl.pallas_call(
        back_query_kernel,
        grid_spec=pltpu.PrefetchScalarGridSpec(
            num_scalar_prefetch=1,
            grid=(1,),
            in_specs=[whole((D, N1))] * 4
            + [whole((80, 128)), whole((D, N1)), whole((D, N1)), whole((D, D))],
            out_specs=[whole((D, N1)), whole((64, D))],
        ),
        out_shape=(jax.ShapeDtypeStruct((D, N1), F32), jax.ShapeDtypeStruct((64, D), F32)),
        compiler_params=params(),
        cost_estimate=cost(2e9, 5e6),
        name="back_query",
    )(at, *dm, msg, tokt, q, wq)


def back_keys_kernel(at_ref, msg_ref, km_ref, v_ref, slope_ref, tokt_ref, gq_ref, dk_ref, dv_ref, keep_ref, send_ref):
    dkv = unpack_heads(msg_ref[0:64, :])
    dks = jnp.sum(row_of(msg_ref, 64), axis=0, keepdims=True)
    hi, lo = split2(dkv)
    v = v_ref[...]
    dk = mm(hi, v) + mm(lo, v) + as_column(dks)
    dk = (dk * slope_ref[...]).astype(BF)
    hi, lo = split2(dkv.T)
    km = km_ref[...]
    dv = (mm(hi, km) + mm(lo, km)).astype(BF)
    dk_ref[...] = dk
    dv_ref[...] = dv
    core, y = at_ref[0], at_ref[2]
    for ref, part in ((keep_ref, core), (send_ref, 1 - core)):
        tok = tokt_ref[pl.ds(pl.multiple_of(y * 64 + part * 32, 32), 32), :]
        ref[:, 0:D] = gq_ref[pl.ds(pl.multiple_of(part * 32, 32), 32), :].astype(BF)
        ref[:, D : 2 * D] = mm_nt(tok, dk).astype(BF)
        ref[:, 2 * D : 3 * D] = mm_nt(tok, dv).astype(BF)


def back_keys_call(at, msg, km, v, slope, tokt, gq):
    whole = lambda shape: pl.BlockSpec(shape, lambda i, at: (0,) * len(shape))
    return pl.pallas_call(
        back_keys_kernel,
        grid_spec=pltpu.PrefetchScalarGridSpec(
            num_scalar_prefetch=1,
            grid=(1,),
            in_specs=[whole((88, 128))] + [whole((D, N1))] * 4 + [whole((64, D))],
            out_specs=[whole((D, N1)), whole((D, N1)), whole((32, 3 * D)), whole((32, 3 * D))],
        ),
        out_shape=(
            jax.ShapeDtypeStruct((D, N1), BF),
            jax.ShapeDtypeStruct((D, N1), BF),
            jax.ShapeDtypeStruct((32, 3 * D), BF),
            jax.ShapeDtypeStruct((32, 3 * D), BF),
        ),
        compiler_params=params(),
        cost_estimate=cost(1e9, 4e6),
        name="back_keys",
    )(at, msg, km, v, slope, tokt, gq)


def grad_x_kernel(gx_ref, dk_ref, dv_ref, wk_ref, wv_ref, out_ref):
    total = gx_ref[...] + mm(wk_ref[...], dk_ref[...]) + mm(wv_ref[...], dv_ref[...])
    out_ref[...] = total.T.astype(BF)


def grad_x_call(gx, dk, dv, wk, wv):
    return pl.pallas_call(
        grad_x_kernel,
        out_shape=jax.ShapeDtypeStruct((N1, D), BF),
        compiler_params=params(),
        cost_estimate=cost(3e8, 3e6),
        name="grad_x",
    )(gx, dk, dv, wk, wv)


def place_kernel(at_ref, *refs):
    ins, (gin_ref, gout_ref, buf) = refs[:8], refs[8:]
    core, x, z = at_ref[0], at_ref[3], at_ref[4]
    for side in range(2):
        expert = core if side == 0 else 1 - core
        for d in range(4):
            ref = ins[4 * side + d]
            for e in range(4):
                piece = lax.rem(x + 4 - d, 4) * 4 + lax.rem(z + 4 - e, 4)
                rows = pl.ds(pl.multiple_of(piece * 64, 64), 64)
                buf[rows, :] = ref[e, 0:64, :].astype(F32)
                gout_ref[expert, rows, :] = ref[e, 64:128, :].astype(F32)
        gin_ref[expert] = buf[...].T


def place_call(at, pieces):
    whole = lambda shape: pl.BlockSpec(shape, lambda i, at: (0,) * len(shape))
    return pl.pallas_call(
        place_kernel,
        grid_spec=pltpu.PrefetchScalarGridSpec(
            num_scalar_prefetch=1,
            grid=(1,),
            in_specs=[whole((4, 128, D))] * 8,
            out_specs=[whole((2, D, FH)), whole((2, FH, D))],
            scratch_shapes=[pltpu.VMEM((FH, D), F32)],
        ),
        out_shape=(jax.ShapeDtypeStruct((2, D, FH), F32), jax.ShapeDtypeStruct((2, FH, D), F32)),
        compiler_params=params(),
        cost_estimate=cost(1e6, 7e6),
        name="place_experts",
    )(at, *pieces)


def place_proj_kernel(at_ref, *refs):
    ins, outs = refs[:4], refs[4:]
    core, y = at_ref[0], at_ref[2]
    for d, ref in enumerate(ins):
        for side in range(2):
            part = core if side == 0 else 1 - core
            rows = pl.ds(pl.multiple_of(lax.rem(y + 4 - d, 4) * 64 + part * 32, 32), 32)
            for k, out in enumerate(outs):
                out[rows, :] = ref[side, :, D * k : D * k + D].astype(F32)


def place_proj_call(at, pieces):
    whole = lambda shape: pl.BlockSpec(shape, lambda i, at: (0,) * len(shape))
    return pl.pallas_call(
        place_proj_kernel,
        grid_spec=pltpu.PrefetchScalarGridSpec(
            num_scalar_prefetch=1,
            grid=(1,),
            in_specs=[whole((2, 32, 3 * D))] * 4,
            out_specs=[whole((D, D))] * 3,
        ),
        out_shape=(jax.ShapeDtypeStruct((D, D), F32),) * 3,
        compiler_params=params(),
        cost_estimate=cost(1e6, 1e6),
        name="place_projections",
    )(at, *pieces)


def swap_core(v):
    return lax.ppermute(v, "pts", [(i, i ^ 1) for i in range(32)])


def to_x(v, d):
    return lax.ppermute(v, "pts", [(i, (i & ~6) | ((i + 2 * d) & 6)) for i in range(32)])


def to_z(v, d):
    return lax.ppermute(v, "pts", [(i, (i + 8 * d) % 32) for i in range(32)])


def to_y(v, d):
    return lax.ppermute(v, "exp", [(i, (i + d) % 4) for i in range(4)])


def star(v, to):
    return [to(v, d) for d in (1, 2, 3)]


def star_sum(v, to):
    a, b, c = star(v, to)
    if v.dtype == BF:
        return ((v.astype(F32) + a.astype(F32)) + (b.astype(F32) + c.astype(F32))).astype(BF)
    return (v + a) + (b + c)


def on_device(
    tokens, coords, keep, cotangent, w_query, w_key, w_value, w_geo, b_geo, w_route, w_in, w_out
):
    pts = lax.axis_index("pts")
    y = lax.axis_index("exp")
    core, x, z = pts % 2, (pts // 2) % 4, pts // 8
    at = jnp.stack([core, 2 * y + core, y, x, z]).astype(jnp.int32)
    keep_row = keep[None, :]
    ck = jnp.concatenate([coords, keep_row.astype(F32)], axis=0)

    km, v, slope, msg = keys_call(tokens, keep_row, w_key, w_value)
    tokens_o, cot_o, ck_o = swap_core(tokens), swap_core(cotangent), swap_core(ck)

    msg = msg + swap_core(msg)
    msg = star_sum(msg, to_x)
    msg = star_sum(msg, to_z)

    tokt, q = query_call(tokens, tokens_o, w_query)
    dyt, back, wint = back_call(at, cotangent, cot_o, ck, ck_o, w_in, w_out)
    r, g = gate_call(ck, ck_o, w_geo.T, b_geo[:, None], w_route.T)

    own, oth, msg2, p0, p1, p2, p3 = expert_call(at, msg, tokt, q, dyt, back, g, r, w_in, wint)

    msg2 = msg2 + swap_core(msg2)
    msg2 = star_sum(msg2, to_y)
    msg2 = star_sum(msg2, to_z)
    msg2 = star_sum(msg2, to_x)

    a, b, c = to_x(p1, 1), to_x(p2, 2), to_x(p3, 3)
    s = (p0.astype(F32) + a.astype(F32)) + (b.astype(F32) + c.astype(F32))
    s = [s[e].astype(BF) for e in range(4)]
    a, b, c = to_z(s[1], 1), to_z(s[2], 2), to_z(s[3], 3)
    s = ((s[0].astype(F32) + a.astype(F32)) + (b.astype(F32) + c.astype(F32))).astype(BF)

    own = (own.astype(F32) + swap_core(oth).astype(F32)).astype(BF)
    dm = [own] + star(own, to_y)

    gx, gq = back_query_call(at, dm, msg, tokt, q, w_query)
    dk, dv, part, away = back_keys_call(at, msg2, km, v, slope, tokt, gq)

    s = jnp.stack([s] + star(s, to_z))
    pieces = [s] + star(s, to_x)
    pieces = pieces + [swap_core(piece) for piece in pieces]
    grad_w_in, grad_w_out = place_call(at, pieces)

    part = (part.astype(F32) + swap_core(away).astype(F32)).astype(BF)
    part = star_sum(part, to_x)
    part = star_sum(part, to_z)
    part = jnp.stack([part, swap_core(part)])
    grad_wq, grad_wk, grad_wv = place_proj_call(at, [part] + star(part, to_y))

    grad_x = grad_x_call(gx, dk, dv, w_key, w_value)
    grad_route = lax.dynamic_slice_in_dim(msg2[80:88, :64], 2 * y, 2, 0).T
    return (grad_x, grad_wq, grad_wk, grad_wv, grad_w_in, grad_w_out, grad_route)


def solution(mesh):
    in_specs = (
        P("pts", None),
        P(None, "pts"),
        P("pts"),
        P("pts", None),
        P(),
        P(),
        P(),
        P(),
        P(),
        P(),
        P("exp", None, None),
        P("exp", None, None),
    )
    out_specs = (
        P("pts", None),
        P(),
        P(),
        P(),
        P("exp", None, None),
        P("exp", None, None),
        P(None, "exp"),
    )
    return jax.shard_map(
        on_device, mesh=mesh, in_specs=in_specs, out_specs=out_specs, check_vma=False
    )
```

```python
import functools

import jax
import jax.numpy as jnp
from jax import lax
from jax.experimental import pallas as pl
from jax.experimental.pallas import tpu as pltpu
from jax.sharding import PartitionSpec as P


D = 256
HD = 32
FH = 1024
N1 = 1024
N2 = 2048
TB = 512
HC = 256
F32 = jnp.float32
BF = jnp.bfloat16
VMEM_LIMIT = 60 * 1024 * 1024


def mm(a, b):
    return jnp.dot(a, b, preferred_element_type=F32)


def mm_nt(a, b):
    return lax.dot_general(a, b, (((1,), (1,)), ((), ())), preferred_element_type=F32)


def split2(x):
    hi = x.astype(BF)
    return hi, (x - hi.astype(F32)).astype(BF)


def flip(x):
    return x.astype(F32).T


def head_mask(rows, cols):
    r = lax.broadcasted_iota(jnp.int32, (rows, cols), 0) // HD
    c = lax.broadcasted_iota(jnp.int32, (rows, cols), 1) // HD
    return r == c


def pack_heads(full):
    full = jnp.where(head_mask(D, D), full, 0.0)
    parts = []
    for g in range(2):
        cols = full[:, 128 * g : 128 * g + 128]
        parts.append(sum(cols[128 * g + HD * h : 128 * g + HD * h + HD] for h in range(4)))
    return parts


def unpack_heads(packed):
    mask = head_mask(128, 128)
    zero = jnp.zeros((128, 128), F32)
    blocks = []
    for g in range(2):
        piece = packed[HD * g : HD * g + HD]
        blocks.append(jnp.where(mask, jnp.concatenate([piece] * 4, axis=0), 0.0))
    top = jnp.concatenate([blocks[0], zero], axis=1)
    low = jnp.concatenate([zero, blocks[1]], axis=1)
    return jnp.concatenate([top, low], axis=0)


def ordered(core, own, other):
    first = core == 0
    return jnp.where(first, own, other), jnp.where(first, other, own)


def row_of(halves):
    return jnp.concatenate([half[HD : HD + 8] for half in halves], axis=1)


def heads_of(halves):
    return unpack_heads(jnp.concatenate([half[:HD] for half in halves], axis=0))


def column_of(row):
    n = row.shape[1]
    r = lax.broadcasted_iota(jnp.int32, (n, n), 0)
    c = lax.broadcasted_iota(jnp.int32, (n, n), 1)
    return jnp.sum(jnp.where(r == c, row, 0.0), axis=1, keepdims=True)


def whole(*shape):
    return pl.BlockSpec(shape, lambda i, at: (0,) * len(shape))


def call(kernel, grid, in_specs, out_specs, out_shape, flops, nbytes, name, scratch=()):
    return pl.pallas_call(
        kernel,
        grid_spec=pltpu.PrefetchScalarGridSpec(
            num_scalar_prefetch=1,
            grid=grid,
            in_specs=in_specs,
            out_specs=out_specs,
            scratch_shapes=list(scratch),
        ),
        out_shape=out_shape,
        compiler_params=pltpu.CompilerParams(vmem_limit_bytes=VMEM_LIMIT),
        cost_estimate=pl.CostEstimate(flops=int(flops), bytes_accessed=int(nbytes), transcendentals=0),
        name=name,
    )


def struct(shape, dtype):
    return jax.ShapeDtypeStruct(shape, dtype)


def keys_kernel(at_ref, tok_ref, keep_ref, coords_ref, wk_ref, wv_ref, km_ref, v_ref, slope_ref, ck_ref, keep_msg, send_msg, keep_m, send_m):
    core = at_ref[0]
    tok = tok_ref[...]
    tokt = flip(tok).astype(BF)
    kpre = mm(flip(wk_ref[...]).astype(BF), tokt)
    val = mm(flip(wv_ref[...]).astype(BF), tokt).astype(BF)
    keep = keep_ref[...].astype(F32)
    ck_ref[0:3, :] = coords_ref[...]
    ck_ref[3:4, :] = keep
    low = jnp.exp(jnp.minimum(kpre, 0.0))
    km = (keep * jnp.where(kpre > 0, kpre + 1.0, low)).astype(BF)
    km_ref[...] = km
    v_ref[...] = val
    slope_ref[...] = keep * jnp.where(kpre > 0, 1.0, low)
    parts = pack_heads(mm_nt(val, km))
    ks = mm_nt(jnp.ones((8, N1), BF), km)
    halves = [jnp.concatenate([parts[g], ks[:, 128 * g : 128 * g + 128]], axis=0) for g in range(2)]
    keep_msg[...], send_msg[...] = ordered(core, *halves)
    for ref, half in ((keep_m, core), (send_m, 1 - core)):
        rows = pl.ds(pl.multiple_of(half * 128, 128), 128)
        ref[...] = mm_nt(tokt, km_ref[rows, :]).astype(BF)


def keys_call(at, tokens, keep_row, coords, wk, wv):
    return call(
        keys_kernel,
        (1,),
        [whole(N1, D), whole(1, N1), whole(3, N1), whole(D, D), whole(D, D)],
        [whole(D, N1), whole(D, N1), whole(D, N1), whole(4, N1), whole(40, 128), whole(40, 128), whole(D, 128), whole(D, 128)],
        (
            struct((D, N1), BF), struct((D, N1), BF), struct((D, N1), F32), struct((4, N1), F32),
            struct((40, 128), F32), struct((40, 128), F32), struct((D, 128), BF), struct((D, 128), BF),
        ),
        4e8, 3e6, "keys",
    )(at, tokens, keep_row, coords, wk, wv)


def query_kernel(at_ref, tok_ref, oth_ref, wq_ref, tokt_ref, q_ref):
    wqt = flip(wq_ref[...]).astype(BF)
    for half, ref in enumerate((tok_ref, oth_ref)):
        tokt = flip(ref[...]).astype(BF)
        cols = slice(N1 * half, N1 * half + N1)
        tokt_ref[:, cols] = tokt
        pre = mm(wqt, tokt)
        q_ref[:, cols] = jnp.where(pre > 0, pre + 1.0, jnp.exp(jnp.minimum(pre, 0.0))).astype(BF)


def query_call(at, tokens, tokens_o, wq):
    return call(
        query_kernel, (1,), [whole(N1, D), whole(N1, D), whole(D, D)], [whole(D, N2), whole(D, N2)],
        (struct((D, N2), BF), struct((D, N2), BF)), 4e8, 3e6, "queries",
    )(at, tokens, tokens_o, wq)


def gate_kernel(at_ref, ck_ref, cko_ref, wgeo_ref, bgeo_ref, wroute_ref, r_ref, g_ref):
    geo = [column_of(wgeo_ref[k : k + 1, :]) for k in range(3)]
    bias = column_of(bgeo_ref[...])
    for half, ref in enumerate((ck_ref, cko_ref)):
        cols = slice(N1 * half, N1 * half + N1)
        pre = bias
        for k in range(3):
            pre = pre + geo[k] * ref[k : k + 1, :]
        r = jnp.tanh(pre)
        r_ref[:, cols] = r
        logit = lax.dot_general(
            wroute_ref[...], r, (((0,), (0,)), ((), ())), precision=lax.Precision.HIGHEST, preferred_element_type=F32
        )
        expo = jnp.exp(logit)
        g_ref[:, cols] = expo / jnp.sum(expo, axis=0, keepdims=True)


def gate_call(at, ck, ck_o, wgeo, bgeo, wroute):
    return call(
        gate_kernel, (1,), [whole(4, N1), whole(4, N1), whole(3, 64), whole(1, 64), whole(64, 8)],
        [whole(64, N2), whole(8, N2)], (struct((64, N2), F32), struct((8, N2), F32)), 1e8, 1e6, "gate",
    )(at, ck, ck_o, wgeo, bgeo, wroute)


def back_kernel(at_ref, cot_ref, oth_ref, ck_ref, cko_ref, win_ref, wout_ref, dyt_ref, back_ref, wint_ref):
    for half, (ref, keep_ref) in enumerate(((cot_ref, ck_ref), (oth_ref, cko_ref))):
        cot = ref[...]
        keep = keep_ref[3:4, :]
        cols = slice(N1 * half, N1 * half + N1)
        dyt_ref[:, cols] = (flip(cot) * keep).astype(BF)
        for j in range(0, FH, HC):
            back_ref[j : j + HC, cols] = (mm_nt(wout_ref[0, j : j + HC, :], cot) * keep).astype(BF)
    wint_ref[...] = flip(win_ref[0]).astype(BF)


def back_call(at, cot, cot_o, ck, ck_o, w_in, w_out):
    return call(
        back_kernel, (1,),
        [
            whole(N1, D), whole(N1, D), whole(4, N1), whole(4, N1),
            pl.BlockSpec((1, D, FH), lambda i, at: (at[0], 0, 0)),
            pl.BlockSpec((1, FH, D), lambda i, at: (at[0], 0, 0)),
        ],
        [whole(D, N2), whole(FH, N2), whole(FH, D)],
        (struct((D, N2), BF), struct((FH, N2), BF), struct((FH, D), BF)), 11e8, 8e6, "cotangent_back",
    )(at, cot, cot_o, ck, ck_o, w_in, w_out)


GELU_A = 0.7978845608028654
GELU_B = 0.7978845608028654 * 0.044715


def expert_kernel(
    at_ref, msg_ref, msgo_ref, m_ref, mo_ref, tokt_ref, q_ref, dyt_ref, back_ref, g_ref, r_ref, win_ref, wint_ref,
    own_ref, oth_ref, keep_msg, send_msg, pieces_ref,
    kvh, kvl, ksh, ksl, gw1, gw2, dkv, dks, route,
):
    step = pl.program_id(0)
    core, expert = at_ref[0], at_ref[1]

    @pl.when(step == 0)
    def _():
        halves = ordered(core, msg_ref[...], msgo_ref[...])
        hi, lo = split2(heads_of(halves))
        kvh[...] = hi
        kvl[...] = lo
        hi, lo = split2(jnp.where(head_mask(D, D), row_of(halves)[0:1], 0.0))
        ksh[...] = hi
        ksl[...] = lo
        gw1[...] = jnp.zeros_like(gw1)
        gw2[...] = jnp.zeros_like(gw2)
        dkv[...] = jnp.zeros_like(dkv)
        dks[...] = jnp.zeros_like(dks)
        route[...] = jnp.zeros_like(route)

    q = q_ref[...]
    num = mm(kvh[...], q) + mm(kvl[...], q)
    rden = 1.0 / (mm(ksh[...], q) + mm(ksl[...], q))
    attn = num * rden
    mid = (tokt_ref[...].astype(F32) + attn).astype(BF)
    gates = g_ref[...]
    mine = lax.broadcasted_iota(jnp.int32, gates.shape, 0) == expert
    gate = jnp.sum(jnp.where(mine, gates, 0.0), axis=0, keepdims=True)
    dyt = dyt_ref[...].astype(F32)
    df = (dyt * gate).astype(BF)
    first = jnp.logical_and(at_ref[2] == 0, step < N1 // TB)
    dmid = dyt * jnp.where(first, 1.0, 0.0)
    stat = jnp.zeros((1, TB), F32)
    for j in range(0, FH, HC):
        rows = slice(j, j + HC)
        u = mm(wint_ref[rows, :], mid)
        u2 = u * u
        t = jnp.tanh(u * (GELU_A + GELU_B * u2))
        half = 0.5 + 0.5 * t
        act = (u * half).astype(BF)
        slope = half + 0.5 * u * (1.0 - t * t) * (GELU_A + 3.0 * GELU_B * u2)
        back = back_ref[rows, :].astype(F32)
        stat = stat + jnp.sum(act.astype(F32) * back, axis=0, keepdims=True)
        du = (back * gate * slope).astype(BF)
        gw2[rows, :] += mm_nt(act, df)
        gw1[rows, :] += mm_nt(du, mid)
        dmid = dmid + mm(win_ref[0, :, rows], du)
    stat = stat * gate
    turn = (jnp.where(mine, 1.0, 0.0) - gates) * stat
    route[...] += lax.dot_general(
        turn, r_ref[...], (((1,), (1,)), ((), ())), precision=lax.Precision.HIGHEST, preferred_element_type=F32
    )
    dnum = dmid * rden
    dden = -jnp.sum((dnum * attn).reshape(8, HD, TB), axis=1)
    hi, lo = split2(dnum)
    dkv[...] += mm_nt(q, hi) + mm_nt(q, lo)
    hi, lo = split2(dden)
    dks[...] += mm_nt(hi, q) + mm_nt(lo, q)

    @pl.when(step < N1 // TB)
    def _():
        own_ref[...] = dmid.astype(BF)

    @pl.when(step >= N1 // TB)
    def _():
        oth_ref[...] = dmid.astype(BF)

    @pl.when(step == N2 // TB - 1)
    def _():
        m = (m_ref[...].astype(F32) + mo_ref[...].astype(F32)).astype(BF)
        for k in range(16):
            rows = slice(64 * k, 64 * k + 64)
            pieces_ref[k, 0:64, :] = gw1[rows, :].astype(BF)
            pieces_ref[k, 64:128, :] = gw2[rows, :].astype(BF)
            pieces_ref[k, 128:144, 0:128] = m[16 * k : 16 * k + 16]
            pieces_ref[k, 128:144, 128:256] = jnp.zeros((16, 128), BF)
        parts = pack_heads(dkv[...])
        r = lax.broadcasted_iota(jnp.int32, (8, D), 0)
        c = lax.broadcasted_iota(jnp.int32, (8, D), 1) // HD
        sums = jnp.where(r == c, dks[...], 0.0)
        last = [jnp.concatenate([route[...], jnp.zeros((8, 64), F32)], axis=1), jnp.zeros((8, 128), F32)]
        halves = [jnp.concatenate([parts[g], sums[:, 128 * g : 128 * g + 128], last[g]], axis=0) for g in range(2)]
        keep_msg[...], send_msg[...] = ordered(core, *halves)


def expert_call(at, msg, msg_o, m, m_o, tokt, q, dyt, back, g, r, w_in, wint):
    steps, own = N2 // TB, N1 // TB
    by_points = lambda rows: pl.BlockSpec((rows, TB), lambda i, at: (0, i))
    return call(
        expert_kernel, (steps,),
        [whole(40, 128), whole(40, 128), whole(D, 128), whole(D, 128)]
        + [by_points(rows) for rows in (D, D, D, FH, 8, 64)]
        + [pl.BlockSpec((1, D, FH), lambda i, at: (at[0], 0, 0)), whole(FH, D)],
        [
            pl.BlockSpec((D, TB), lambda i, at: (0, jnp.minimum(i, own - 1))),
            pl.BlockSpec((D, TB), lambda i, at: (0, jnp.maximum(i - own, 0))),
            whole(48, 128), whole(48, 128), whole(16, 144, D),
        ],
        (
            struct((D, N1), BF), struct((D, N1), BF), struct((48, 128), F32), struct((48, 128), F32),
            struct((16, 144, D), BF),
        ),
        6e9, 12e6, "expert",
        [pltpu.VMEM((D, D), BF)] * 4
        + [pltpu.VMEM((FH, D), F32)] * 2
        + [pltpu.VMEM((D, D), F32), pltpu.VMEM((8, D), F32), pltpu.VMEM((8, 64), F32)],
    )(at, msg, msg_o, m, m_o, tokt, q, dyt, back, g, r, w_in, wint)


def back_query_kernel(at_ref, d0, d1, d2, d3, msg_ref, msgo_ref, tokt_ref, q_ref, wq_ref, gx_ref, gq_ref):
    dmid = (d0[...].astype(F32) + d1[...].astype(F32)) + (d2[...].astype(F32) + d3[...].astype(F32))
    q = q_ref[...]
    tokt = tokt_ref[...]
    halves = ordered(at_ref[0], msg_ref[...], msgo_ref[...])
    kvt = heads_of(halves)
    kvth, kvtl = split2(kvt)
    kvh, kvl = split2(kvt.T)
    ks = row_of(halves)[0:1]
    mask = head_mask(D, D)
    ksh, ksl = split2(jnp.where(mask, ks, 0.0))
    kch, kcl = split2(jnp.where(mask, column_of(ks), 0.0))
    num = mm(kvth, q) + mm(kvtl, q)
    rden = 1.0 / (mm(ksh, q) + mm(ksl, q))
    attn = num * rden
    dnum = dmid * rden
    nh, nl = split2(dnum)
    zh, zl = split2(dnum * attn)
    dq = (mm(kvh, nh) - mm(kch, zh)) + (mm(kvl, nh) - mm(kcl, zh)) + (mm(kvh, nl) - mm(kch, zl))
    wq = wq_ref[...]
    pre = mm(flip(wq).astype(BF), tokt)
    dqp = (dq * jnp.where(pre > 0, 1.0, jnp.exp(jnp.minimum(pre, 0.0)))).astype(BF)
    gx_ref[...] = dmid + mm(wq, dqp)
    gq_ref[...] = mm_nt(tokt, dqp)


def back_query_call(at, dm, msg, msg_o, tokt, q, wq):
    return call(
        back_query_kernel, (1,),
        [whole(D, N1)] * 4 + [whole(40, 128), whole(40, 128), whole(D, N1), whole(D, N1), whole(D, D)],
        [whole(D, N1), whole(D, D)], (struct((D, N1), F32), struct((D, D), F32)), 2e9, 5e6, "back_query",
    )(at, *dm, msg, msg_o, tokt, q, wq)


def back_keys_kernel(at_ref, msg_ref, msgo_ref, km_ref, v_ref, slope_ref, tokt_ref, gq_ref, dk_ref, dv_ref, keep_ref, send_ref):
    core = at_ref[0]
    halves = ordered(core, msg_ref[...], msgo_ref[...])
    dkv = heads_of(halves)
    dks = jnp.sum(row_of(halves), axis=0, keepdims=True)
    hi, lo = split2(dkv)
    v = v_ref[...]
    dk = mm(hi, v) + mm(lo, v) + column_of(dks)
    dk = (dk * slope_ref[...]).astype(BF)
    hi, lo = split2(dkv.T)
    km = km_ref[...]
    dk_ref[...] = dk
    dv_ref[...] = (mm(hi, km) + mm(lo, km)).astype(BF)
    for ref, part in ((keep_ref, core), (send_ref, 1 - core)):
        rows = pl.ds(pl.multiple_of(part * 128, 128), 128)
        ref[:, 0:D] = gq_ref[rows, :].astype(BF)
        ref[:, D : 2 * D] = mm_nt(tokt_ref[rows, :], dk).astype(BF)


def back_keys_call(at, msg, msg_o, km, v, slope, tokt, gq):
    return call(
        back_keys_kernel, (1,), [whole(48, 128)] * 2 + [whole(D, N1)] * 4 + [whole(D, D)],
        [whole(D, N1), whole(D, N1), whole(128, 2 * D), whole(128, 2 * D)],
        (struct((D, N1), BF), struct((D, N1), BF), struct((128, 2 * D), BF), struct((128, 2 * D), BF)),
        1e9, 4e6, "back_keys",
    )(at, msg, msg_o, km, v, slope, tokt, gq)


def grad_x_kernel(at_ref, gx_ref, dk_ref, dv_ref, wk_ref, wv_ref, out_ref):
    total = gx_ref[...] + mm(wk_ref[...], dk_ref[...]) + mm(wv_ref[...], dv_ref[...])
    out_ref[...] = total.T.astype(BF)


def grad_x_call(at, gx, dk, dv, wk, wv):
    return call(
        grad_x_kernel, (1,), [whole(D, N1)] * 3 + [whole(D, D)] * 2, [whole(N1, D)], (struct((N1, D), BF),),
        3e8, 3e6, "grad_x",
    )(at, gx, dk, dv, wk, wv)[0]


def place_kernel(at_ref, own_ref, oth_ref, gin_ref, gout_ref):
    def put(ref):
        parts = [ref[k, 0:64, :].astype(F32) for k in range(4)]
        gin_ref[0] = jnp.concatenate(parts, axis=0).T
        for k in range(4):
            gout_ref[0, 64 * k : 64 * k + 64, :] = ref[k, 64:128, :].astype(F32)

    step = pl.program_id(0)
    pl.when(step < 4)(lambda: put(own_ref))
    pl.when(step >= 4)(lambda: put(oth_ref))


def place_call(at, own, oth):
    expert = lambda i, at: jnp.where(i < 4, at[0], 1 - at[0])
    return call(
        place_kernel, (8,),
        [
            pl.BlockSpec((4, 144, D), lambda i, at: (jnp.minimum(i, 3), 0, 0)),
            pl.BlockSpec((4, 144, D), lambda i, at: (jnp.maximum(i - 4, 0), 0, 0)),
        ],
        [
            pl.BlockSpec((1, D, 256), lambda i, at: (expert(i, at), 0, lax.rem(i, 4))),
            pl.BlockSpec((1, 256, D), lambda i, at: (expert(i, at), lax.rem(i, 4), 0)),
        ],
        (struct((2, D, FH), F32), struct((2, FH, D), F32)), 1e6, 7e6, "place_experts",
    )(at, own, oth)


def place_m_kernel(at_ref, msg_ref, msgo_ref, own_ref, oth_ref, gv_ref, route_ref):
    core, y = at_ref[0], at_ref[2]
    halves = ordered(core, msg_ref[...], msgo_ref[...])
    hi, lo = split2(heads_of(halves))
    own = jnp.concatenate([own_ref[k, :, 0:128].astype(F32) for k in range(16)], axis=0)
    oth = jnp.concatenate([oth_ref[k, :, 0:128].astype(F32) for k in range(16)], axis=0)
    m = jnp.concatenate(ordered(core, own, oth), axis=1).astype(BF)
    gv_ref[...] = mm(m, hi) + mm(m, lo)
    sums = halves[0][40:48, 0:64]
    at_row = lax.broadcasted_iota(jnp.int32, sums.shape, 0)
    cols = [column_of(jnp.sum(jnp.where(at_row == 2 * y + e, sums, 0.0), axis=0, keepdims=True)) for e in range(2)]
    route_ref[...] = jnp.concatenate(cols, axis=1)


def place_m_call(at, msg, msg_o, own, oth):
    last = pl.BlockSpec((16, 16, D), lambda i, at: (0, 8, 0))
    return call(
        place_m_kernel, (1,), [whole(48, 128)] * 2 + [last] * 2, [whole(D, D), whole(64, 2)],
        (struct((D, D), F32), struct((64, 2), F32)), 1e8, 1e6, "grad_wv",
    )(at, msg, msg_o, own, oth)


def place_proj_kernel(at_ref, own_ref, oth_ref, gq_ref, gk_ref):
    core = at_ref[0]
    for ref, part in ((own_ref, core), (oth_ref, 1 - core)):
        rows = pl.ds(pl.multiple_of(part * 128, 128), 128)
        gq_ref[rows, :] = ref[:, 0:D].astype(F32)
        gk_ref[rows, :] = ref[:, D : 2 * D].astype(F32)


def place_proj_call(at, own, oth):
    return call(
        place_proj_kernel, (1,), [whole(128, 2 * D)] * 2, [whole(D, D)] * 2, (struct((D, D), F32),) * 2,
        1e6, 1e6, "place_projections",
    )(at, own, oth)


def swap_core(v):
    return lax.ppermute(v, "pts", [(i, i ^ 1) for i in range(32)])


def to_x(v, d):
    return lax.ppermute(v, "pts", [(i, (i & ~6) | ((i + 2 * d) & 6)) for i in range(32)])


def to_z(v, d):
    return lax.ppermute(v, "pts", [(i, (i + 8 * d) % 32) for i in range(32)])


def to_y(v, d):
    return lax.ppermute(v, "exp", [(i, (i + d) % 4) for i in range(4)])


def star(v, to):
    return [to(v, d) for d in (1, 2, 3)]


def star_sum(v, to):
    a, b, c = star(v, to)
    if v.dtype == BF:
        return ((v.astype(F32) + a.astype(F32)) + (b.astype(F32) + c.astype(F32))).astype(BF)
    return (v + a) + (b + c)


CHIPS = [[2 * k + core for k in range(16)] for core in range(2)]


def exchange(v):
    return lax.all_to_all(v, "pts", 0, 0, axis_index_groups=CHIPS)


def chips_sum(v):
    every = exchange(jnp.broadcast_to(v[None], (16,) + v.shape))
    return jnp.sum(every.astype(F32), axis=0)


def on_device(
    tokens, coords, keep, cotangent, w_query, w_key, w_value, w_geo, b_geo, w_route, w_in, w_out
):
    pts = lax.axis_index("pts")
    y = lax.axis_index("exp")
    core = pts % 2
    at = jnp.stack([core, 2 * y + core, y]).astype(jnp.int32)

    tokens_o, cot_o = swap_core(tokens), swap_core(cotangent)
    km, v, slope, ck, msg, msg_away, m, m_away = keys_call(at, tokens, keep[None, :], coords, w_key, w_value)
    msg = msg + swap_core(msg_away)
    msg = chips_sum(msg)
    msg_o = swap_core(msg)
    ck_o, m_o = swap_core(ck), swap_core(m_away)

    tokt, q = query_call(at, tokens, tokens_o, w_query)
    dyt, back, wint = back_call(at, cotangent, cot_o, ck, ck_o, w_in, w_out)
    r, g = gate_call(at, ck, ck_o, w_geo, b_geo[None, :], w_route)

    own, oth, msg2, msg2_away, pieces = expert_call(
        at, msg, msg_o, m, m_o, tokt, q, dyt, back, g, r, w_in, wint
    )

    pieces = exchange(pieces)
    pieces = jnp.sum(pieces.astype(F32), axis=0).astype(BF)

    msg2 = msg2 + swap_core(msg2_away)
    msg2 = star_sum(msg2, to_y)
    msg2 = chips_sum(msg2)
    msg2_o = swap_core(msg2)

    own = (own.astype(F32) + swap_core(oth).astype(F32)).astype(BF)
    dm = [own] + star(own, to_y)

    gx, gq = back_query_call(at, dm, msg, msg_o, tokt, q, w_query)
    dk, dv, part, away = back_keys_call(at, msg2, msg2_o, km, v, slope, tokt, gq)

    pieces = exchange(jnp.broadcast_to(pieces[None], (16,) + pieces.shape))
    pieces_o = swap_core(pieces)
    grad_w_in, grad_w_out = place_call(at, pieces, pieces_o)
    grad_wv, grad_route = place_m_call(at, msg2, msg2_o, pieces, pieces_o)

    part = (part.astype(F32) + swap_core(away).astype(F32)).astype(BF)
    part = star_sum(part, to_x)
    part = star_sum(part, to_z)
    grad_wq, grad_wk = place_proj_call(at, part, swap_core(part))

    grad_x = grad_x_call(at, gx, dk, dv, w_key, w_value)
    return (grad_x, grad_wq, grad_wk, grad_wv, grad_w_in, grad_w_out, grad_route)


def solution(mesh):
    in_specs = (
        P("pts", None),
        P(None, "pts"),
        P("pts"),
        P("pts", None),
        P(),
        P(),
        P(),
        P(),
        P(),
        P(),
        P("exp", None, None),
        P("exp", None, None),
    )
    out_specs = (
        P("pts", None),
        P(),
        P(),
        P(),
        P("exp", None, None),
        P("exp", None, None),
        P(None, "exp"),
    )
    return jax.shard_map(
        on_device, mesh=mesh, in_specs=in_specs, out_specs=out_specs, check_vma=False
    )
```

```python
import functools

import jax
import jax.numpy as jnp
from jax import lax
from jax.experimental import pallas as pl
from jax.experimental.pallas import tpu as pltpu
from jax.sharding import PartitionSpec as P


D = 256
HD = 32
FH = 1024
N1 = 1024
N2 = 2048
TB = 512
HC = 256
F32 = jnp.float32
BF = jnp.bfloat16


def mm(a, b):
    return jnp.dot(a, b, preferred_element_type=F32)


def mm_nt(a, b):
    return lax.dot_general(a, b, (((1,), (1,)), ((), ())), preferred_element_type=F32)


def split2(x):
    hi = x.astype(BF)
    return hi, (x - hi.astype(F32)).astype(BF)


def flip(x):
    return x.astype(F32).T


def head_mask(rows, cols):
    r = lax.broadcasted_iota(jnp.int32, (rows, cols), 0) // HD
    c = lax.broadcasted_iota(jnp.int32, (rows, cols), 1) // HD
    return r == c


def pack_heads(full):
    full = jnp.where(head_mask(D, D), full, 0.0)
    parts = []
    for g in range(2):
        cols = full[:, 128 * g : 128 * g + 128]
        parts.append(sum(cols[128 * g + HD * h : 128 * g + HD * h + HD] for h in range(4)))
    return parts


def unpack_heads(packed):
    mask = head_mask(128, 128)
    zero = jnp.zeros((128, 128), F32)
    blocks = []
    for g in range(2):
        piece = packed[HD * g : HD * g + HD]
        blocks.append(jnp.where(mask, jnp.concatenate([piece] * 4, axis=0), 0.0))
    top = jnp.concatenate([blocks[0], zero], axis=1)
    low = jnp.concatenate([zero, blocks[1]], axis=1)
    return jnp.concatenate([top, low], axis=0)


def ordered(core, own, other):
    first = core == 0
    return jnp.where(first, own, other), jnp.where(first, other, own)


def row_of(halves):
    return jnp.concatenate([half[HD : HD + 8] for half in halves], axis=1)


def heads_of(halves):
    return unpack_heads(jnp.concatenate([half[:HD] for half in halves], axis=0))


def column_of(row):
    n = row.shape[1]
    r = lax.broadcasted_iota(jnp.int32, (n, n), 0)
    c = lax.broadcasted_iota(jnp.int32, (n, n), 1)
    return jnp.sum(jnp.where(r == c, row, 0.0), axis=1, keepdims=True)


def call(kernel, out_shape, flops, nbytes, name, scratch=(), after=(), limit=8, fetch=0):
    def run(at, *args):
        n_in, n_after = len(args), len(after)

        def body(*refs):
            ins, outs = list(refs[1 : 1 + n_in]), refs[1 + n_in + n_after :]
            if fetch:
                outs, bufs, sems = outs[: -fetch - 1], outs[-fetch - 1 : -1], outs[-1]
                copies = [pltpu.make_async_copy(ins[k], bufs[k], sems.at[k]) for k in range(fetch)]
                for copy in copies:
                    copy.start()
                for copy in copies:
                    copy.wait()
                ins[:fetch] = bufs
            kernel(refs[0], *ins, *outs)

        in_vmem = pl.BlockSpec(memory_space=pltpu.VMEM)
        in_any = pl.BlockSpec(memory_space=pl.ANY)
        more = [pltpu.VMEM(x.shape, x.dtype) for x in args[:fetch]]
        return pl.pallas_call(
            body,
            in_specs=[pl.BlockSpec(memory_space=pltpu.SMEM)]
            + [pl.BlockSpec(memory_space=pltpu.HBM)] * fetch
            + [in_vmem] * (n_in - fetch)
            + [in_any] * n_after,
            out_specs=[in_vmem] * len(out_shape),
            out_shape=out_shape,
            scratch_shapes=list(scratch) + (more + [pltpu.SemaphoreType.DMA((fetch,))] if fetch else []),
            compiler_params=pltpu.CompilerParams(vmem_limit_bytes=limit * 1024 * 1024),
            cost_estimate=pl.CostEstimate(flops=int(flops), bytes_accessed=int(nbytes), transcendentals=0),
            name=name,
        )(at, *args, *after)

    return run


def struct(shape, dtype):
    return jax.ShapeDtypeStruct(shape, dtype)


def add(terms, after=(), dtype=BF):
    if after:
        terms = lax.optimization_barrier((*terms, *after))[: len(terms)]
    total = terms[0].astype(F32)
    for term in terms[1:]:
        total = total + term.astype(F32)
    return total.astype(dtype)


def chips_kernel(at_ref, every_ref, out_ref):
    total = every_ref[0].astype(F32)
    for k in range(1, 16):
        total = total + every_ref[k].astype(F32)
    total = total.astype(out_ref.dtype)
    for k in range(16):
        out_ref[k] = total


def chips_call(at, every, after=()):
    return call(chips_kernel, (struct(every.shape, every.dtype),), 1e6, 1e6, "experts_sum", after=after)(at, every)[0]


def keys_values(tokt, keep, wk, wv):
    kpre = mm(flip(wk).astype(BF), tokt)
    val = mm(flip(wv).astype(BF), tokt).astype(BF)
    low = jnp.exp(jnp.minimum(kpre, 0.0))
    km = (keep * jnp.where(kpre > 0, kpre + 1.0, low)).astype(BF)
    return km, val, keep * jnp.where(kpre > 0, 1.0, low)


def keys_kernel(at_ref, tok_ref, keep_ref, coords_ref, wk_ref, wv_ref, ck_ref, msg_ref, keep_m, send_m, km_buf):
    core = at_ref[0]
    tokt = flip(tok_ref[...]).astype(BF)
    keep = keep_ref[...].astype(F32)
    ck_ref[0:3, :] = coords_ref[...]
    ck_ref[3:4, :] = keep
    km, val, _ = keys_values(tokt, keep, wk_ref[...], wv_ref[...])
    km_buf[...] = km
    parts = pack_heads(mm_nt(val, km))
    ks = mm_nt(jnp.ones((8, N1), BF), km)
    for g in range(2):
        msg_ref[40 * g : 40 * g + 32, :] = parts[g]
        msg_ref[40 * g + 32 : 40 * g + 40, :] = ks[:, 128 * g : 128 * g + 128]
    for ref, half in ((keep_m, core), (send_m, 1 - core)):
        rows = pl.ds(pl.multiple_of(half * 128, 128), 128)
        ref[...] = mm_nt(tokt, km_buf[rows, :]).astype(BF)


def keys_call(at, tokens, keep_row, coords, wk, wv):
    return call(
        keys_kernel,
        (struct((4, N1), F32), struct((80, 128), F32), struct((D, 128), BF), struct((D, 128), BF)),
        4e8, 3e6, "keys", [pltpu.VMEM((D, N1), BF)], fetch=5,
    )(at, tokens, keep_row, coords, wk, wv)


def again_kernel(at_ref, tok_ref, keep_ref, wq_ref, wk_ref, wv_ref, tokt_ref, q_ref, qslope_ref, km_ref, v_ref, slope_ref):
    tokt = flip(tok_ref[...]).astype(BF)
    tokt_ref[...] = tokt
    pre = mm(flip(wq_ref[...]).astype(BF), tokt)
    low = jnp.exp(jnp.minimum(pre, 0.0))
    q_ref[...] = jnp.where(pre > 0, pre + 1.0, low).astype(BF)
    qslope_ref[...] = jnp.where(pre > 0, 1.0, low)
    km_ref[...], v_ref[...], slope_ref[...] = keys_values(tokt, keep_ref[...].astype(F32), wk_ref[...], wv_ref[...])


def again_call(at, tokens, keep_row, wq, wk, wv, after):
    return call(
        again_kernel,
        (
            struct((D, N1), BF), struct((D, N1), BF), struct((D, N1), F32),
            struct((D, N1), BF), struct((D, N1), BF), struct((D, N1), F32),
        ),
        5e8, 3e6, "queries_keys_again", after=after, fetch=5,
    )(at, tokens, keep_row, wq, wk, wv)


def query_kernel(at_ref, tok_ref, oth_ref, wq_ref, tokt_ref, q_ref):
    wqt = flip(wq_ref[...]).astype(BF)
    for half, ref in enumerate((tok_ref, oth_ref)):
        tokt = flip(ref[...]).astype(BF)
        cols = slice(N1 * half, N1 * half + N1)
        tokt_ref[:, cols] = tokt
        pre = mm(wqt, tokt)
        q_ref[:, cols] = jnp.where(pre > 0, pre + 1.0, jnp.exp(jnp.minimum(pre, 0.0))).astype(BF)


def query_call(at, tokens, tokens_o, wq):
    out = (struct((D, N2), BF), struct((D, N2), BF))
    return call(query_kernel, out, 4e8, 3e6, "queries")(at, tokens, tokens_o, wq)


def gate_kernel(at_ref, ck_ref, cko_ref, wgeo_ref, bgeo_ref, wroute_ref, r_ref, g_ref):
    geo = [column_of(wgeo_ref[k : k + 1, :]) for k in range(3)]
    bias = column_of(bgeo_ref[...])
    for half, ref in enumerate((ck_ref, cko_ref)):
        cols = slice(N1 * half, N1 * half + N1)
        pre = bias
        for k in range(3):
            pre = pre + geo[k] * ref[k : k + 1, :]
        r = jnp.tanh(pre)
        r_ref[:, cols] = r
        logit = lax.dot_general(
            wroute_ref[...], r, (((0,), (0,)), ((), ())), precision=lax.Precision.HIGHEST, preferred_element_type=F32
        )
        expo = jnp.exp(logit)
        g_ref[:, cols] = expo / jnp.sum(expo, axis=0, keepdims=True)


def gate_call(at, ck, ck_o, wgeo, bgeo, wroute):
    out = (struct((64, N2), F32), struct((8, N2), F32))
    return call(gate_kernel, out, 1e8, 1e6, "gate")(at, ck, ck_o, wgeo, bgeo, wroute)


def back_kernel(at_ref, cot_ref, oth_ref, ck_ref, cko_ref, win_ref, wout_ref, dyt_ref, back_ref, wint_ref):
    core = at_ref[0]
    for half, (ref, keep_ref) in enumerate(((cot_ref, ck_ref), (oth_ref, cko_ref))):
        cot = ref[...]
        keep = keep_ref[3:4, :]
        cols = slice(N1 * half, N1 * half + N1)
        dyt_ref[:, cols] = (flip(cot) * keep).astype(BF)
        for j in range(0, FH, HC):
            back_ref[j : j + HC, cols] = (mm_nt(wout_ref[core, j : j + HC, :], cot) * keep).astype(BF)
    wint_ref[...] = flip(win_ref[core]).astype(BF)


def back_call(at, cot, cot_o, ck, ck_o, w_in, w_out):
    out = (struct((D, N2), BF), struct((FH, N2), BF), struct((FH, D), BF))
    return call(back_kernel, out, 11e8, 8e6, "cotangent_back")(at, cot, cot_o, ck, ck_o, w_in, w_out)


GELU_A = 0.7978845608028654
GELU_B = 0.7978845608028654 * 0.044715


def expert_kernel(
    at_ref, msg_ref, m_ref, mo_ref, tokt_ref, q_ref, dyt_ref, back_ref, g_ref, r_ref, win_ref, wint_ref,
    own_ref, oth_ref, kvt_ref, ks_ref, keep_msg, send_msg, pieces_ref,
    gw1, gw2, dkv, dks, route,
):
    core, expert, y = at_ref[0], at_ref[1], at_ref[2]
    halves = msg_ref[0:40, :], msg_ref[40:80, :]
    kvt = heads_of(halves)
    ks = row_of(halves)
    kvt_ref[...] = kvt
    ks_ref[...] = ks
    kvh, kvl = split2(kvt)
    ksh, ksl = split2(jnp.where(head_mask(D, D), ks[0:1], 0.0))

    def step(i, first):
        cols = slice(TB * i, TB * i + TB)
        q = q_ref[:, cols]
        num = mm(kvh, q) + mm(kvl, q)
        rden = 1.0 / (mm(ksh, q) + mm(ksl, q))
        attn = num * rden
        mid = (tokt_ref[:, cols].astype(F32) + attn).astype(BF)
        gates = g_ref[:, cols]
        mine = lax.broadcasted_iota(jnp.int32, gates.shape, 0) == expert
        gate = jnp.sum(jnp.where(mine, gates, 0.0), axis=0, keepdims=True)
        dyt = dyt_ref[:, cols].astype(F32)
        df = (dyt * gate).astype(BF)
        dmid = jnp.zeros((D, TB), F32)
        if i < N1 // TB:
            dmid = dyt * jnp.where(y == 0, 1.0, 0.0)
        stat = jnp.zeros((1, TB), F32)
        for j in range(0, FH, HC):
            rows = slice(j, j + HC)
            u = mm(wint_ref[rows, :], mid)
            u2 = u * u
            t = jnp.tanh(u * (GELU_A + GELU_B * u2))
            half = 0.5 + 0.5 * t
            act = (u * half).astype(BF)
            slope = half + 0.5 * u * (1.0 - t * t) * (GELU_A + 3.0 * GELU_B * u2)
            back = back_ref[rows, cols].astype(F32)
            stat = stat + jnp.sum(act.astype(F32) * back, axis=0, keepdims=True)
            du = (back * gate * slope).astype(BF)
            dw2, dw1 = mm_nt(act, df), mm_nt(du, mid)
            gw2[rows, :] = dw2 if first else gw2[rows, :] + dw2
            gw1[rows, :] = dw1 if first else gw1[rows, :] + dw1
            dmid = dmid + mm(win_ref[core, :, rows], du)
        stat = stat * gate
        turn = (jnp.where(mine, 1.0, 0.0) - gates) * stat
        dnum = dmid * rden
        dden = -jnp.sum((dnum * attn).reshape(8, HD, TB), axis=1)
        hi, lo = split2(dnum)
        dkv_part = mm_nt(q, hi) + mm_nt(q, lo)
        hi, lo = split2(dden)
        dks_part = mm_nt(hi, q) + mm_nt(lo, q)
        route_part = lax.dot_general(
            turn, r_ref[:, cols], (((1,), (1,)), ((), ())), precision=lax.Precision.HIGHEST, preferred_element_type=F32
        )
        dkv[...] = dkv_part if first else dkv[...] + dkv_part
        dks[...] = dks_part if first else dks[...] + dks_part
        route[...] = route_part if first else route[...] + route_part
        if i < N1 // TB:
            own_ref[:, cols] = dmid
        else:
            oth_ref[:, TB * i - N1 : TB * i - N1 + TB] = dmid.astype(BF)

    for i in range(N2 // TB):
        step(i, i == 0)

    m = (m_ref[...].astype(F32) + mo_ref[...].astype(F32)).astype(BF)
    for k in range(16):
        rows = slice(64 * k, 64 * k + 64)
        pieces_ref[k, 0:64, :] = gw1[rows, :].astype(BF)
        pieces_ref[k, 64:128, :] = gw2[rows, :].astype(BF)
        pieces_ref[k, 128:144, 0:128] = m[16 * k : 16 * k + 16]
        pieces_ref[k, 128:144, 128:256] = jnp.zeros((16, 128), BF)
    parts = pack_heads(dkv[...])
    r = lax.broadcasted_iota(jnp.int32, (8, D), 0)
    c = lax.broadcasted_iota(jnp.int32, (8, D), 1) // HD
    sums = jnp.where(r == c, dks[...], 0.0)
    last = [jnp.concatenate([route[...], jnp.zeros((8, 64), F32)], axis=1), jnp.zeros((8, 128), F32)]
    halves = [jnp.concatenate([parts[g], sums[:, 128 * g : 128 * g + 128], last[g]], axis=0) for g in range(2)]
    keep_msg[...], send_msg[...] = ordered(core, *halves)


def expert_call(at, msg, m, m_o, tokt, q, dyt, back, g, r, w_in, wint):
    return call(
        expert_kernel,
        (
            struct((D, N1), F32), struct((D, N1), BF), struct((D, D), F32), struct((8, D), F32),
            struct((48, 128), F32), struct((48, 128), F32), struct((16, 144, D), BF),
        ),
        6e9, 12e6, "expert",
        [pltpu.VMEM((FH, D), F32)] * 2
        + [pltpu.VMEM((D, D), F32), pltpu.VMEM((8, D), F32), pltpu.VMEM((8, 64), F32)],
        limit=16,
    )(at, msg, m, m_o, tokt, q, dyt, back, g, r, w_in, wint)


def dmid_kernel(at_ref, own_ref, oth_ref, *out_refs):
    for d, ref in enumerate(out_refs):
        cols = pl.ds(pl.multiple_of(lax.rem(at_ref[2] + d, 4) * 256, 256), 256)
        ref[...] = (own_ref[:, cols] + oth_ref[:, cols].astype(F32)).astype(BF)


def dmid_call(at, own, oth):
    return call(dmid_kernel, (struct((D, 256), BF),) * 4, 1e6, 2e6, "dmid_pieces")(at, own, oth)


def back_query_kernel(
    at_ref, d0, d1, d2, d3, kvt_ref, ks_ref, tokt_ref, q_ref, qslope_ref, wq_ref, gx_ref, gq_ref, dmid_ref
):
    for d, ref in enumerate((d0, d1, d2, d3)):
        cols = pl.ds(pl.multiple_of(lax.rem(at_ref[2] + 4 - d, 4) * 256, 256), 256)
        dmid_ref[:, cols] = ref[...].astype(F32)
    dmid = dmid_ref[...]
    q = q_ref[...]
    tokt = tokt_ref[...]
    kvt = kvt_ref[...]
    kvth, kvtl = split2(kvt)
    kvh, kvl = split2(kvt.T)
    ks = ks_ref[0:1, :]
    mask = head_mask(D, D)
    ksh, ksl = split2(jnp.where(mask, ks, 0.0))
    kch, kcl = split2(jnp.where(mask, column_of(ks), 0.0))
    num = mm(kvth, q) + mm(kvtl, q)
    rden = 1.0 / (mm(ksh, q) + mm(ksl, q))
    attn = num * rden
    dnum = dmid * rden
    nh, nl = split2(dnum)
    zh, zl = split2(dnum * attn)
    dq = (mm(kvh, nh) - mm(kch, zh)) + (mm(kvl, nh) - mm(kcl, zh)) + (mm(kvh, nl) - mm(kch, zl))
    wq = wq_ref[...]
    dqp = (dq * qslope_ref[...]).astype(BF)
    gx_ref[...] = dmid + mm(wq, dqp)
    gq_ref[...] = mm_nt(tokt, dqp)


def back_query_call(at, dm, kvt, ks, tokt, q, qslope, wq):
    out = (struct((D, N1), F32), struct((D, D), F32))
    return call(back_query_kernel, out, 2e9, 5e6, "back_query", [pltpu.VMEM((D, N1), F32)])(
        at, *dm, kvt, ks, tokt, q, qslope, wq
    )


def back_keys_kernel(at_ref, msg_ref, msgo_ref, km_ref, v_ref, slope_ref, tokt_ref, gq_ref, dk_ref, dv_ref, keep_ref, send_ref):
    core = at_ref[0]
    halves = ordered(core, msg_ref[...], msgo_ref[...])
    dkv = heads_of(halves)
    dks = jnp.sum(row_of(halves), axis=0, keepdims=True)
    hi, lo = split2(dkv)
    v = v_ref[...]
    dk = mm(hi, v) + mm(lo, v) + column_of(dks)
    dk = (dk * slope_ref[...]).astype(BF)
    hi, lo = split2(dkv.T)
    km = km_ref[...]
    dk_ref[...] = dk
    dv_ref[...] = (mm(hi, km) + mm(lo, km)).astype(BF)
    for ref, part in ((keep_ref, core), (send_ref, 1 - core)):
        rows = pl.ds(pl.multiple_of(part * 128, 128), 128)
        ref[:, 0:D] = gq_ref[rows, :].astype(ref.dtype)
        ref[:, D : 2 * D] = mm_nt(tokt_ref[rows, 0:N1], dk).astype(ref.dtype)


def back_keys_call(at, msg, msg_o, km, v, slope, tokt, gq):
    out = (struct((D, N1), BF), struct((D, N1), BF), struct((128, 2 * D), F32), struct((128, 2 * D), BF))
    return call(back_keys_kernel, out, 1e9, 4e6, "back_keys")(at, msg, msg_o, km, v, slope, tokt, gq)


def grad_x_kernel(at_ref, gx_ref, dk_ref, dv_ref, wk_ref, wv_ref, out_ref):
    total = gx_ref[...] + mm(wk_ref[...], dk_ref[...]) + mm(wv_ref[...], dv_ref[...])
    out_ref[...] = total.T.astype(BF)


def grad_x_call(at, gx, dk, dv, wk, wv):
    return call(grad_x_kernel, (struct((N1, D), BF),), 3e8, 3e6, "grad_x")(at, gx, dk, dv, wk, wv)[0]


def place_kernel(at_ref, own_ref, oth_ref, gin_ref, gout_ref):
    def put(ref, part):
        cols = slice(128 * part, 128 * part + 128)
        gin_ref[0] = jnp.concatenate([ref[k, 0:64, cols].astype(F32) for k in range(16)], axis=0).T
        for k in range(8):
            gout_ref[0, 64 * k : 64 * k + 64, :] = ref[8 * part + k, 64:128, :].astype(F32)

    step = pl.program_id(0)
    for s in range(4):
        pl.when(step == s)(lambda s=s: put(own_ref if s < 2 else oth_ref, s % 2))


def place_call(at, own, oth):
    expert = lambda i, at: jnp.where(i < 2, at[0], 1 - at[0])
    out = pl.BlockSpec((1, 128, FH), lambda i, at: (expert(i, at), lax.rem(i, 2), 0))
    out2 = pl.BlockSpec((1, 512, D), lambda i, at: (expert(i, at), lax.rem(i, 2), 0))
    return pl.pallas_call(
        place_kernel,
        grid_spec=pltpu.PrefetchScalarGridSpec(
            num_scalar_prefetch=1,
            grid=(4,),
            in_specs=[pl.BlockSpec(memory_space=pltpu.VMEM)] * 2,
            out_specs=[out, out2],
        ),
        out_shape=(struct((2, D, FH), F32), struct((2, FH, D), F32)),
        compiler_params=pltpu.CompilerParams(vmem_limit_bytes=32 * 1024 * 1024),
        cost_estimate=pl.CostEstimate(flops=1000000, bytes_accessed=7000000, transcendentals=0),
        name="place_experts",
    )(at, own, oth)


def place_m_kernel(at_ref, msg_ref, msgo_ref, own_ref, oth_ref, gv_ref, route_ref):
    core, y = at_ref[0], at_ref[2]
    halves = ordered(core, msg_ref[...], msgo_ref[...])
    hi, lo = split2(heads_of(halves))
    own = jnp.concatenate([own_ref[k, 128:144, 0:128].astype(F32) for k in range(16)], axis=0)
    oth = jnp.concatenate([oth_ref[k, 128:144, 0:128].astype(F32) for k in range(16)], axis=0)
    m = jnp.concatenate(ordered(core, own, oth), axis=1).astype(BF)
    gv_ref[...] = mm(m, hi) + mm(m, lo)
    sums = halves[0][40:48, 0:64]
    at_row = lax.broadcasted_iota(jnp.int32, sums.shape, 0)
    cols = [column_of(jnp.sum(jnp.where(at_row == 2 * y + e, sums, 0.0), axis=0, keepdims=True)) for e in range(2)]
    route_ref[...] = jnp.concatenate(cols, axis=1)


def place_m_call(at, msg, msg_o, own, oth):
    out = (struct((D, D), F32), struct((64, 2), F32))
    return call(place_m_kernel, out, 1e8, 1e6, "grad_wv")(at, msg, msg_o, own, oth)


def place_proj_kernel(at_ref, own_ref, oth_ref, gq_ref, gk_ref):
    core = at_ref[0]
    for ref, part in ((own_ref, core), (oth_ref, 1 - core)):
        rows = pl.ds(pl.multiple_of(part * 128, 128), 128)
        gq_ref[rows, :] = ref[:, 0:D].astype(F32)
        gk_ref[rows, :] = ref[:, D : 2 * D].astype(F32)


def place_proj_call(at, own, oth):
    return call(place_proj_kernel, (struct((D, D), F32),) * 2, 1e6, 1e6, "place_projections")(at, own, oth)


def swap_core(v):
    return lax.ppermute(v, "pts", [(i, i ^ 1) for i in range(32)])


def to_x(v, d):
    return lax.ppermute(v, "pts", [(i, (i & ~6) | ((i + 2 * d) & 6)) for i in range(32)])


def to_z(v, d):
    return lax.ppermute(v, "pts", [(i, (i + 8 * d) % 32) for i in range(32)])


def to_y(v, d):
    return lax.ppermute(v, "exp", [(i, (i + d) % 4) for i in range(4)])


def star(v, to):
    return [to(v, d) for d in (1, 2, 3)]


CHIPS = [[2 * k + core for k in range(16)] for core in range(2)]


def exchange(v):
    return lax.all_to_all(v, "pts", 0, 0, axis_index_groups=CHIPS)


def on_device(
    tokens, coords, keep, cotangent, w_query, w_key, w_value, w_geo, b_geo, w_route, w_in, w_out
):
    pts = lax.axis_index("pts")
    y = lax.axis_index("exp")
    core = pts % 2
    at = jnp.stack([core, 2 * y + core, y]).astype(jnp.int32)

    tokens_o, cot_o = swap_core(tokens), swap_core(cotangent)
    ck, msg, m, m_away = keys_call(at, tokens, keep[None, :], coords, w_key, w_value)
    ck_o, m_o = swap_core(ck), swap_core(m_away)
    tokt, q = query_call(at, tokens, tokens_o, w_query)
    r, g = gate_call(at, ck, ck_o, w_geo, b_geo[None, :], w_route)
    dyt, back, wint = back_call(at, cotangent, cot_o, ck, ck_o, w_in, w_out)

    msg = add([msg, swap_core(msg)], (), F32)
    msg = add([msg] + star(msg, to_x), (q, g), F32)
    msg = add([msg] + star(msg, to_z), (back,), F32)
    own, oth, kvt, ks, msg2, msg2_away, pieces = expert_call(
        at, msg, m, m_o, tokt, q, dyt, back, g, r, w_in, wint
    )

    pieces = exchange(pieces)

    d0, d1, d2, d3 = dmid_call(at, own, swap_core(oth))
    dm = add([d0, to_y(d1, 1), to_y(d2, 2), to_y(d3, 3)])

    msg2 = add([msg2, swap_core(msg2_away)], (d0,), F32)
    msg2 = add([msg2] + star(msg2, to_y), (dm,), F32)
    dm = [dm] + star(dm, to_y)
    msg2 = msg2_z = add([msg2] + star(msg2, to_z), (), F32)

    pieces = chips_call(at, pieces, (msg2_z,))

    tokt, q, qslope, km, v, slope = again_call(at, tokens, keep[None, :], w_query, w_key, w_value, (pieces,))
    gx, gq = back_query_call(at, dm, kvt, ks, tokt, q, qslope, w_query)
    msg2 = add([msg2] + star(msg2, to_x), (gq,), F32)
    msg2_o = swap_core(msg2)
    dk, dv, part, away = back_keys_call(at, msg2, msg2_o, km, v, slope, tokt, gq)

    pieces = exchange(pieces)
    pieces_o = swap_core(pieces)
    grad_x = grad_x_call(at, gx, dk, dv, w_key, w_value)
    grad_w_in, grad_w_out = place_call(at, pieces, pieces_o)
    grad_wv, grad_route = place_m_call(at, msg2, msg2_o, pieces, pieces_o)

    part = add([part, swap_core(away)])
    part = add([part] + star(part, to_x), (grad_x,))
    part = add([part] + star(part, to_z), (grad_w_in, grad_wv))
    grad_wq, grad_wk = place_proj_call(at, part, swap_core(part))
    return (grad_x, grad_wq, grad_wk, grad_wv, grad_w_in, grad_w_out, grad_route)


def solution(mesh):
    in_specs = (
        P("pts", None),
        P(None, "pts"),
        P("pts"),
        P("pts", None),
        P(),
        P(),
        P(),
        P(),
        P(),
        P(),
        P("exp", None, None),
        P("exp", None, None),
    )
    out_specs = (
        P("pts", None),
        P(),
        P(),
        P(),
        P("exp", None, None),
        P("exp", None, None),
        P(None, "exp"),
    )
    return jax.shard_map(
        on_device, mesh=mesh, in_specs=in_specs, out_specs=out_specs, check_vma=False
    )
```

```python
import functools

import jax
import jax.numpy as jnp
from jax import lax
from jax.experimental import pallas as pl
from jax.experimental.pallas import tpu as pltpu
from jax.sharding import PartitionSpec as P


D = 256
HD = 32
FH = 1024
N1 = 1024
N2 = 2048
TB = 1024
HC = 1024
LIMIT = 36
F32 = jnp.float32
BF = jnp.bfloat16


def mm(a, b):
    return jnp.dot(a, b, preferred_element_type=F32)


def mm_nt(a, b):
    return lax.dot_general(a, b, (((1,), (1,)), ((), ())), preferred_element_type=F32)


def split2(x):
    hi = x.astype(BF)
    return hi, (x - hi.astype(F32)).astype(BF)


def flip(x):
    return x.astype(F32).T


def head_mask(rows, cols):
    r = lax.broadcasted_iota(jnp.int32, (rows, cols), 0) // HD
    c = lax.broadcasted_iota(jnp.int32, (rows, cols), 1) // HD
    return r == c


def pack_heads(full):
    full = jnp.where(head_mask(D, D), full, 0.0)
    parts = []
    for g in range(2):
        cols = full[:, 128 * g : 128 * g + 128]
        parts.append(sum(cols[128 * g + HD * h : 128 * g + HD * h + HD] for h in range(4)))
    return parts


def unpack_heads(packed):
    mask = head_mask(128, 128)
    zero = jnp.zeros((128, 128), F32)
    blocks = []
    for g in range(2):
        piece = packed[HD * g : HD * g + HD]
        blocks.append(jnp.where(mask, jnp.concatenate([piece] * 4, axis=0), 0.0))
    top = jnp.concatenate([blocks[0], zero], axis=1)
    low = jnp.concatenate([zero, blocks[1]], axis=1)
    return jnp.concatenate([top, low], axis=0)


def ordered(core, own, other):
    first = core == 0
    return jnp.where(first, own, other), jnp.where(first, other, own)


def row_of(halves):
    return jnp.concatenate([half[HD : HD + 8] for half in halves], axis=1)


def heads_of(halves):
    return unpack_heads(jnp.concatenate([half[:HD] for half in halves], axis=0))


def column_of(row):
    n = row.shape[1]
    r = lax.broadcasted_iota(jnp.int32, (n, n), 0)
    c = lax.broadcasted_iota(jnp.int32, (n, n), 1)
    return jnp.sum(jnp.where(r == c, row, 0.0), axis=1, keepdims=True)


def call(kernel, out_shape, flops, nbytes, name, scratch=(), after=(), limit=8, fetch=0):
    def run(at, *args):
        n_in, n_after = len(args), len(after)

        def body(*refs):
            ins, outs = list(refs[1 : 1 + n_in]), refs[1 + n_in + n_after :]
            if fetch:
                outs, bufs, sems = outs[: -fetch - 1], outs[-fetch - 1 : -1], outs[-1]
                copies = [pltpu.make_async_copy(ins[k], bufs[k], sems.at[k]) for k in range(fetch)]
                for copy in copies:
                    copy.start()
                for copy in copies:
                    copy.wait()
                ins[:fetch] = bufs
            kernel(refs[0], *ins, *outs)

        in_vmem = pl.BlockSpec(memory_space=pltpu.VMEM)
        in_any = pl.BlockSpec(memory_space=pl.ANY)
        more = [pltpu.VMEM(x.shape, x.dtype) for x in args[:fetch]]
        return pl.pallas_call(
            body,
            in_specs=[pl.BlockSpec(memory_space=pltpu.SMEM)]
            + [pl.BlockSpec(memory_space=pltpu.HBM)] * fetch
            + [in_vmem] * (n_in - fetch)
            + [in_any] * n_after,
            out_specs=[in_vmem] * len(out_shape),
            out_shape=out_shape,
            scratch_shapes=list(scratch) + (more + [pltpu.SemaphoreType.DMA((fetch,))] if fetch else []),
            compiler_params=pltpu.CompilerParams(vmem_limit_bytes=limit * 1024 * 1024),
            cost_estimate=pl.CostEstimate(flops=int(flops), bytes_accessed=int(nbytes), transcendentals=0),
            name=name,
        )(at, *[pltpu.with_memory_space_constraint(x, pltpu.HBM) for x in args[:fetch]], *args[fetch:], *after)

    return run


def struct(shape, dtype):
    return jax.ShapeDtypeStruct(shape, dtype)


def add(terms, after=(), dtype=BF):
    if after:
        terms = lax.optimization_barrier((*terms, *after))[: len(terms)]
    total = terms[0].astype(F32)
    for term in terms[1:]:
        total = total + term.astype(F32)
    return total.astype(dtype)


def chips_kernel(at_ref, every_ref, out_ref):
    total = every_ref[0].astype(F32)
    for k in range(1, 16):
        total = total + every_ref[k].astype(F32)
    out_ref[...] = total.astype(out_ref.dtype)


def chips_call(at, every, after=()):
    out = struct(every.shape[1:], every.dtype)
    return call(chips_kernel, (out,), 1e6, 1e6, "experts_sum", after=after)(at, every)[0]


def keys_values(tokt, keep, wk, wv):
    kpre = mm(flip(wk).astype(BF), tokt)
    val = mm(flip(wv).astype(BF), tokt).astype(BF)
    low = jnp.exp(jnp.minimum(kpre, 0.0))
    km = (keep * jnp.where(kpre > 0, kpre + 1.0, low)).astype(BF)
    return km, val, keep * jnp.where(kpre > 0, 1.0, low)


def keys_kernel(at_ref, tok_ref, keep_ref, coords_ref, wk_ref, wv_ref, ck_ref, msg_ref, keep_m, send_m, km_buf):
    core = at_ref[0]
    tokt = flip(tok_ref[...]).astype(BF)
    keep = keep_ref[...].astype(F32)
    ck_ref[0:3, :] = coords_ref[...]
    ck_ref[3:4, :] = keep
    km, val, _ = keys_values(tokt, keep, wk_ref[...], wv_ref[...])
    km_buf[...] = km
    parts = pack_heads(mm_nt(val, km))
    ks = mm_nt(jnp.ones((8, N1), BF), km)
    for g in range(2):
        msg_ref[40 * g : 40 * g + 32, :] = parts[g]
        msg_ref[40 * g + 32 : 40 * g + 40, :] = ks[:, 128 * g : 128 * g + 128]
    for ref, half in ((keep_m, core), (send_m, 1 - core)):
        rows = pl.ds(pl.multiple_of(half * 128, 128), 128)
        ref[...] = mm_nt(tokt, km_buf[rows, :]).astype(BF)


def keys_call(at, tokens, keep_row, coords, wk, wv):
    return call(
        keys_kernel,
        (struct((4, N1), F32), struct((80, 128), F32), struct((D, 128), BF), struct((D, 128), BF)),
        4e8, 3e6, "keys", [pltpu.VMEM((D, N1), BF)], fetch=5,
    )(at, tokens, keep_row, coords, wk, wv)


def again_kernel(at_ref, tok_ref, keep_ref, wq_ref, wk_ref, wv_ref, tokt_ref, q_ref, qslope_ref, km_ref, v_ref, slope_ref):
    tokt = flip(tok_ref[...]).astype(BF)
    tokt_ref[...] = tokt
    pre = mm(flip(wq_ref[...]).astype(BF), tokt)
    low = jnp.exp(jnp.minimum(pre, 0.0))
    q_ref[...] = jnp.where(pre > 0, pre + 1.0, low).astype(BF)
    qslope_ref[...] = jnp.where(pre > 0, 1.0, low)
    km_ref[...], v_ref[...], slope_ref[...] = keys_values(tokt, keep_ref[...].astype(F32), wk_ref[...], wv_ref[...])


def again_call(at, tokens, keep_row, wq, wk, wv, after):
    return call(
        again_kernel,
        (
            struct((D, N1), BF), struct((D, N1), BF), struct((D, N1), F32),
            struct((D, N1), BF), struct((D, N1), BF), struct((D, N1), F32),
        ),
        5e8, 3e6, "queries_keys_again", after=after, fetch=5,
    )(at, tokens, keep_row, wq, wk, wv)


def query_kernel(at_ref, tok_ref, oth_ref, wq_ref, tokt_ref, q_ref):
    wqt = flip(wq_ref[...]).astype(BF)
    for half, ref in enumerate((tok_ref, oth_ref)):
        tokt = flip(ref[...]).astype(BF)
        cols = slice(N1 * half, N1 * half + N1)
        tokt_ref[:, cols] = tokt
        pre = mm(wqt, tokt)
        q_ref[:, cols] = jnp.where(pre > 0, pre + 1.0, jnp.exp(jnp.minimum(pre, 0.0))).astype(BF)


def query_call(at, tokens, tokens_o, wq):
    out = (struct((D, N2), BF), struct((D, N2), BF))
    return call(query_kernel, out, 4e8, 3e6, "queries")(at, tokens, tokens_o, wq)


def gate_kernel(at_ref, ck_ref, cko_ref, wgeo_ref, bgeo_ref, wroute_ref, r_ref, g_ref):
    geo = [column_of(wgeo_ref[k : k + 1, :]) for k in range(3)]
    bias = column_of(bgeo_ref[...])
    for half, ref in enumerate((ck_ref, cko_ref)):
        cols = slice(N1 * half, N1 * half + N1)
        pre = bias
        for k in range(3):
            pre = pre + geo[k] * ref[k : k + 1, :]
        r = jnp.tanh(pre)
        r_ref[:, cols] = r
        logit = lax.dot_general(
            wroute_ref[...], r, (((0,), (0,)), ((), ())), precision=lax.Precision.HIGHEST, preferred_element_type=F32
        )
        expo = jnp.exp(logit)
        g_ref[:, cols] = expo / jnp.sum(expo, axis=0, keepdims=True)


def gate_call(at, ck, ck_o, wgeo, bgeo, wroute):
    out = (struct((64, N2), F32), struct((8, N2), F32))
    return call(gate_kernel, out, 1e8, 1e6, "gate")(at, ck, ck_o, wgeo, bgeo, wroute)


def own_gate(at_ref, gates):
    mine = lax.broadcasted_iota(jnp.int32, gates.shape, 0) == at_ref[1]
    return jnp.sum(jnp.where(mine, gates, 0.0), axis=0, keepdims=True), mine


def back_kernel(at_ref, cot_ref, oth_ref, ck_ref, cko_ref, g_ref, win_ref, wout_ref, dy_ref, df_ref, back_ref, wint_ref):
    core = at_ref[0]
    dy_ref[...] = (flip(cot_ref[...]) * ck_ref[3:4, :] * jnp.where(at_ref[2] == 0, 1.0, 0.0)).astype(BF)
    for half, (ref, keep_ref) in enumerate(((cot_ref, ck_ref), (oth_ref, cko_ref))):
        cot = ref[...]
        keep = keep_ref[3:4, :]
        cols = slice(N1 * half, N1 * half + N1)
        gate = keep * own_gate(at_ref, g_ref[:, cols])[0]
        df_ref[:, cols] = (flip(cot) * gate).astype(BF)
        for j in range(0, FH, 256):
            back_ref[j : j + 256, cols] = (mm_nt(wout_ref[core, j : j + 256, :], cot) * gate).astype(BF)
    wint_ref[...] = flip(win_ref[core]).astype(BF)


def back_call(at, cot, cot_o, ck, ck_o, g, w_in, w_out):
    out = (struct((D, N1), BF), struct((D, N2), BF), struct((FH, N2), BF), struct((FH, D), BF))
    return call(back_kernel, out, 11e8, 8e6, "cotangent_back")(at, cot, cot_o, ck, ck_o, g, w_in, w_out)


GELU_A = 0.7978845608028654
GELU_B = 0.7978845608028654 * 0.044715


def expert_kernel(
    at_ref, msg_ref, m_ref, mo_ref, tokt_ref, q_ref, dy_ref, df_ref, back_ref, g_ref, r_ref, win_ref, wint_ref,
    own_ref, oth_ref, kvt_ref, ks_ref, keep_msg, send_msg, pieces_ref,
    gw1, gw2, dkv, route,
):
    core = at_ref[0]
    halves = msg_ref[0:40, :], msg_ref[40:80, :]
    kvt = heads_of(halves)
    ks = row_of(halves)
    kvt_ref[...] = kvt
    ks_ref[...] = ks
    kvh, kvl = split2(kvt)
    ksh, ksl = split2(jnp.where(head_mask(D, D), ks[0:1], 0.0))
    sums = jnp.concatenate([kvh, kvl, ksh, ksl], axis=0)

    def step(i, first):
        cols = slice(TB * i, TB * i + TB)
        q = q_ref[:, cols]
        both = mm(sums, q)
        rden = 1.0 / (both[2 * D : 3 * D] + both[3 * D :])
        attn = (both[:D] + both[D : 2 * D]) * rden
        mid = (tokt_ref[:, cols].astype(F32) + attn).astype(BF)
        df = df_ref[:, cols]
        dmid = dy_ref[:, cols].astype(F32) if TB * i < N1 else jnp.zeros((D, TB), F32)
        stat = jnp.zeros((1, TB), F32)
        for j in range(0, FH, HC):
            rows = slice(j, j + HC)
            u = mm(wint_ref[rows, :], mid)
            u2 = u * u
            half = 0.5 + 0.5 * jnp.tanh(u * (GELU_A + GELU_B * u2))
            act = u * half
            slope = half + act * (1.0 - half) * (2.0 * GELU_A + 6.0 * GELU_B * u2)
            back = back_ref[rows, cols].astype(F32)
            stat = stat + jnp.sum(act * back, axis=0, keepdims=True)
            act = act.astype(BF)
            du = (back * slope).astype(BF)
            dw2, dw1 = mm_nt(act, df), mm_nt(du, mid)
            gw2[rows, :] = dw2 if first else gw2[rows, :] + dw2
            gw1[rows, :] = dw1 if first else gw1[rows, :] + dw1
            dmid = dmid + mm(win_ref[core, :, rows], du)
        gates = g_ref[:, cols]
        mine = own_gate(at_ref, gates)[1]
        turn = (jnp.where(mine, 1.0, 0.0) - gates) * stat
        dnum = dmid * rden
        dden = -jnp.sum((dnum * attn).reshape(8, HD, TB), axis=1)
        lhs = jnp.concatenate([*split2(dnum), *split2(jnp.concatenate([dden, dden], axis=0))], axis=0)
        dkv_part = mm_nt(lhs, q)
        route_part = lax.dot_general(
            turn, r_ref[:, cols], (((1,), (1,)), ((), ())), precision=lax.Precision.HIGHEST, preferred_element_type=F32
        )
        dkv[...] = dkv_part if first else dkv[...] + dkv_part
        route[...] = route_part if first else route[...] + route_part
        for k in range(TB // 512):
            at_col = TB * i + 512 * k
            piece = dmid[:, 512 * k : 512 * k + 512]
            if at_col < N1:
                own_ref[:, at_col : at_col + 512] = piece
            else:
                oth_ref[:, at_col - N1 : at_col - N1 + 512] = piece.astype(BF)

    for i in range(N2 // TB):
        step(i, i == 0)

    m = (m_ref[...].astype(F32) + mo_ref[...].astype(F32)).astype(BF)
    for k in range(16):
        rows = slice(64 * k, 64 * k + 64)
        pieces_ref[k, 0:64, :] = gw1[rows, :].astype(BF)
        pieces_ref[k, 64:128, :] = gw2[rows, :].astype(BF)
        pieces_ref[k, 128:144, 0:128] = m[16 * k : 16 * k + 16]
        pieces_ref[k, 128:144, 128:256] = jnp.zeros((16, 128), BF)
    parts = pack_heads(dkv[0:D, :] + dkv[D : 2 * D, :])
    r = lax.broadcasted_iota(jnp.int32, (8, D), 0)
    c = lax.broadcasted_iota(jnp.int32, (8, D), 1) // HD
    sums = jnp.where(r == c, dkv[2 * D : 2 * D + 8, :] + dkv[2 * D + 16 : 2 * D + 24, :], 0.0)
    last = [jnp.concatenate([route[...], jnp.zeros((8, 64), F32)], axis=1), jnp.zeros((8, 128), F32)]
    halves = [jnp.concatenate([parts[g], sums[:, 128 * g : 128 * g + 128], last[g]], axis=0) for g in range(2)]
    keep_msg[...], send_msg[...] = ordered(core, *halves)


def expert_call(at, msg, m, m_o, tokt, q, dy, df, back, g, r, w_in, wint):
    return call(
        expert_kernel,
        (
            struct((D, N1), F32), struct((D, N1), BF), struct((D, D), F32), struct((8, D), F32),
            struct((48, 128), F32), struct((48, 128), F32), struct((16, 144, D), BF),
        ),
        6e9, 12e6, "expert",
        [pltpu.VMEM((FH, D), F32)] * 2 + [pltpu.VMEM((2 * D + 32, D), F32), pltpu.VMEM((8, 64), F32)],
        limit=LIMIT,
    )(at, msg, m, m_o, tokt, q, dy, df, back, g, r, w_in, wint)


def dmid_kernel(at_ref, own_ref, oth_ref, msg_ref, msgo_ref, *out_refs):
    hi, lo = split2(msg_ref[...] + msgo_ref[...])
    for d, ref in enumerate(out_refs):
        cols = pl.ds(pl.multiple_of(lax.rem(at_ref[2] + d, 4) * 256, 256), 256)
        ref[0:256, :] = (own_ref[:, cols] + oth_ref[:, cols].astype(F32)).astype(BF)
        ref[256:304, 0:128] = hi
        ref[256:304, 128:256] = lo


def dmid_call(at, own, oth, msg, msg_o):
    return call(dmid_kernel, (struct((304, 256), BF),) * 4, 1e6, 2e6, "dmid_pieces")(at, own, oth, msg, msg_o)


def back_query_kernel(
    at_ref, d0, d1, d2, d3, kvt_ref, ks_ref, tokt_ref, q_ref, qslope_ref, wq_ref, gx_ref, gq_ref, dmid_ref
):
    for d, ref in enumerate((d0, d1, d2, d3)):
        cols = pl.ds(pl.multiple_of(lax.rem(at_ref[2] + 4 - d, 4) * 256, 256), 256)
        dmid_ref[:, cols] = ref[...].astype(F32)
    dmid = dmid_ref[...]
    q = q_ref[...]
    tokt = tokt_ref[...]
    kvt = kvt_ref[...]
    kvth, kvtl = split2(kvt)
    kvh, kvl = split2(kvt.T)
    ks = ks_ref[0:1, :]
    mask = head_mask(D, D)
    ksh, ksl = split2(jnp.where(mask, ks, 0.0))
    kch, kcl = split2(jnp.where(mask, column_of(ks), 0.0))
    num = mm(kvth, q) + mm(kvtl, q)
    rden = 1.0 / (mm(ksh, q) + mm(ksl, q))
    attn = num * rden
    dnum = dmid * rden
    nh, nl = split2(dnum)
    zh, zl = split2(dnum * attn)
    dq = (mm(kvh, nh) - mm(kch, zh)) + (mm(kvl, nh) - mm(kcl, zh)) + (mm(kvh, nl) - mm(kch, zl))
    wq = wq_ref[...]
    dqp = (dq * qslope_ref[...]).astype(BF)
    gx_ref[...] = dmid + mm(wq, dqp)
    gq_ref[...] = mm_nt(tokt, dqp)


def back_query_call(at, dm, kvt, ks, tokt, q, qslope, wq):
    out = (struct((D, N1), F32), struct((D, D), F32))
    return call(back_query_kernel, out, 2e9, 5e6, "back_query", [pltpu.VMEM((D, N1), F32)])(
        at, *dm, kvt, ks, tokt, q, qslope, wq
    )


def back_keys_kernel(at_ref, msg_ref, msgo_ref, km_ref, v_ref, slope_ref, tokt_ref, gq_ref, dk_ref, dv_ref, keep_ref, send_ref):
    core = at_ref[0]
    halves = ordered(core, msg_ref[...], msgo_ref[...])
    dkvt = heads_of(halves)
    dks = jnp.sum(row_of(halves), axis=0, keepdims=True)
    hi, lo = split2(dkvt.T)
    v = v_ref[...]
    dk = mm(hi, v) + mm(lo, v) + column_of(dks)
    dk = (dk * slope_ref[...]).astype(BF)
    hi, lo = split2(dkvt)
    km = km_ref[...]
    dk_ref[...] = dk
    dv_ref[...] = (mm(hi, km) + mm(lo, km)).astype(BF)
    for ref, part in ((keep_ref, core), (send_ref, 1 - core)):
        rows = pl.ds(pl.multiple_of(part * 128, 128), 128)
        ref[:, 0:D] = gq_ref[rows, :].astype(ref.dtype)
        ref[:, D : 2 * D] = mm_nt(tokt_ref[rows, 0:N1], dk).astype(ref.dtype)


def back_keys_call(at, msg, msg_o, km, v, slope, tokt, gq):
    out = (struct((D, N1), BF), struct((D, N1), BF), struct((128, 2 * D), F32), struct((128, 2 * D), BF))
    return call(back_keys_kernel, out, 1e9, 4e6, "back_keys")(at, msg, msg_o, km, v, slope, tokt, gq)


def grad_x_kernel(at_ref, gx_ref, dk_ref, dv_ref, wk_ref, wv_ref, out_ref):
    total = gx_ref[...] + mm(wk_ref[...], dk_ref[...]) + mm(wv_ref[...], dv_ref[...])
    out_ref[...] = total.T.astype(BF)


def grad_x_call(at, gx, dk, dv, wk, wv):
    return call(grad_x_kernel, (struct((N1, D), BF),), 3e8, 3e6, "grad_x")(at, gx, dk, dv, wk, wv)[0]


def origin(at_ref, dx, dz):
    return lax.rem(at_ref[4] + 4 - dz, 4) * 4 + lax.rem(at_ref[3] + 4 - dx, 4)


def place_kernel(at_ref, *refs):
    ins, (gin_ref, gout_ref, buf) = refs[:8], refs[8:]

    def put(side):
        for dx in range(4):
            for dz in range(4):
                rows = pl.ds(pl.multiple_of(origin(at_ref, dx, dz) * 64, 64), 64)
                buf[rows, :] = ins[4 * side + dx][dz, 0:64, :].astype(F32)
                gout_ref[0, rows, :] = ins[4 * side + dx][dz, 64:128, :].astype(F32)
        for j in range(0, FH, 256):
            gin_ref[0, :, j : j + 256] = buf[j : j + 256, :].T

    for side in range(2):
        pl.when(pl.program_id(0) == side)(lambda side=side: put(side))


def place_call(at, pieces):
    expert = lambda i, at: (jnp.where(i == 0, at[0], 1 - at[0]), 0, 0)
    return pl.pallas_call(
        place_kernel,
        grid_spec=pltpu.PrefetchScalarGridSpec(
            num_scalar_prefetch=1,
            grid=(2,),
            in_specs=[pl.BlockSpec(memory_space=pltpu.VMEM)] * 8,
            out_specs=[pl.BlockSpec((1, D, FH), expert), pl.BlockSpec((1, FH, D), expert)],
            scratch_shapes=[pltpu.VMEM((FH, D), F32)],
        ),
        out_shape=(struct((2, D, FH), F32), struct((2, FH, D), F32)),
        compiler_params=pltpu.CompilerParams(vmem_limit_bytes=16 * 1024 * 1024),
        cost_estimate=pl.CostEstimate(flops=1000000, bytes_accessed=7000000, transcendentals=0),
        name="place_experts",
    )(at, *pieces)


def place_m_kernel(at_ref, msg_ref, msgo_ref, *refs):
    ins, (gv_ref, route_ref, buf) = refs[:8], refs[8:]
    core, y = at_ref[0], at_ref[2]
    halves = ordered(core, msg_ref[...], msgo_ref[...])
    hi, lo = split2(heads_of(halves).T)
    for side in range(2):
        for dx in range(4):
            for dz in range(4):
                rows = pl.ds(pl.multiple_of(origin(at_ref, dx, dz) * 16, 16), 16)
                buf[side, rows, :] = ins[4 * side + dx][dz, 128:144, 0:128]
    m = jnp.concatenate(ordered(core, buf[0], buf[1]), axis=1)
    gv_ref[...] = mm(m, hi) + mm(m, lo)
    sums = halves[0][40:48, 0:64]
    at_row = lax.broadcasted_iota(jnp.int32, sums.shape, 0)
    cols = [column_of(jnp.sum(jnp.where(at_row == 2 * y + e, sums, 0.0), axis=0, keepdims=True)) for e in range(2)]
    route_ref[...] = jnp.concatenate(cols, axis=1)


def place_m_call(at, msg, msg_o, pieces):
    out = (struct((D, D), F32), struct((64, 2), F32))
    return call(place_m_kernel, out, 1e8, 1e6, "grad_wv", [pltpu.VMEM((2, D, 128), BF)])(at, msg, msg_o, *pieces)


def place_proj_kernel(at_ref, own_ref, oth_ref, gq_ref, gk_ref):
    core = at_ref[0]
    for ref, part in ((own_ref, core), (oth_ref, 1 - core)):
        rows = pl.ds(pl.multiple_of(part * 128, 128), 128)
        gq_ref[rows, :] = ref[:, 0:D].astype(F32)
        gk_ref[rows, :] = ref[:, D : 2 * D].astype(F32)


def place_proj_call(at, own, oth):
    return call(place_proj_kernel, (struct((D, D), F32),) * 2, 1e6, 1e6, "place_projections")(at, own, oth)


def swap_core(v):
    return lax.ppermute(v, "pts", [(i, i ^ 1) for i in range(32)])


def to_x(v, d):
    return lax.ppermute(v, "pts", [(i, (i & ~6) | ((i + 2 * d) & 6)) for i in range(32)])


def to_z(v, d):
    return lax.ppermute(v, "pts", [(i, (i + 8 * d) % 32) for i in range(32)])


def to_y(v, d):
    return lax.ppermute(v, "exp", [(i, (i + d) % 4) for i in range(4)])


def star(v, to):
    return [to(v, d) for d in (1, 2, 3)]


CHIPS = [[2 * k + core for k in range(16)] for core in range(2)]


def exchange(v):
    return lax.all_to_all(v, "pts", 0, 0, axis_index_groups=CHIPS)


def on_device(
    tokens, coords, keep, cotangent, w_query, w_key, w_value, w_geo, b_geo, w_route, w_in, w_out
):
    pts = lax.axis_index("pts")
    y = lax.axis_index("exp")
    core = pts % 2
    at = jnp.stack([core, 2 * y + core, y, (pts // 2) % 4, pts // 8]).astype(jnp.int32)

    tokens_o, cot_o = swap_core(tokens), swap_core(cotangent)
    ck, msg, m, m_away = keys_call(at, tokens, keep[None, :], coords, w_key, w_value)
    ck_o, m_o = swap_core(ck), swap_core(m_away)
    tokt, q = query_call(at, tokens, tokens_o, w_query)
    r, g = gate_call(at, ck, ck_o, w_geo, b_geo[None, :], w_route)
    dy, df, back, wint = back_call(at, cotangent, cot_o, ck, ck_o, g, w_in, w_out)

    msg = add([msg, swap_core(msg)], (), F32)
    msg = add([msg] + star(msg, to_x), (q, g), F32)
    msg = add([msg] + star(msg, to_z), (back,), F32)
    own, oth, kvt, ks, msg2, msg2_away, pieces = expert_call(
        at, msg, m, m_o, tokt, q, dy, df, back, g, r, w_in, wint
    )

    pieces = exchange(pieces)

    p0, p1, p2, p3 = dmid_call(at, own, swap_core(oth), msg2, swap_core(msg2_away))
    arrived = [p0, to_y(p1, 1), to_y(p2, 2), to_y(p3, 3)]
    msg2 = add([p[256:, :128] for p in arrived] + [p[256:, 128:] for p in arrived], (), F32)
    dm = add([p[:256] for p in arrived])
    dm = [dm] + star(dm, to_y)
    msg2 = msg2_z = add([msg2] + star(msg2, to_z), (), F32)

    pieces = chips_call(at, pieces, (msg2_z,))

    tokt, q, qslope, km, v, slope = again_call(at, tokens, keep[None, :], w_query, w_key, w_value, (pieces,))
    gx, gq = back_query_call(at, dm, kvt, ks, tokt, q, qslope, w_query)
    msg2 = add([msg2] + star(msg2, to_x), (gq,), F32)
    msg2_o = swap_core(msg2)
    dk, dv, part, away = back_keys_call(at, msg2, msg2_o, km, v, slope, tokt, gq)

    pieces = jnp.stack([pieces] + star(pieces, to_z))
    pieces = [pieces] + star(pieces, to_x)
    pieces = pieces + [swap_core(piece) for piece in pieces]
    grad_x = grad_x_call(at, gx, dk, dv, w_key, w_value)
    grad_w_in, grad_w_out = place_call(at, pieces)
    grad_wv, grad_route = place_m_call(at, msg2, msg2_o, pieces)

    part = add([part, swap_core(away)])
    part = add([part] + star(part, to_z), (grad_x,))
    part = add([part] + star(part, to_x), (grad_w_in, grad_wv))
    grad_wq, grad_wk = place_proj_call(at, part, swap_core(part))
    return (grad_x, grad_wq, grad_wk, grad_wv, grad_w_in, grad_w_out, grad_route)


def solution(mesh):
    in_specs = (
        P("pts", None),
        P(None, "pts"),
        P("pts"),
        P("pts", None),
        P(),
        P(),
        P(),
        P(),
        P(),
        P(),
        P("exp", None, None),
        P("exp", None, None),
    )
    out_specs = (
        P("pts", None),
        P(),
        P(),
        P(),
        P("exp", None, None),
        P("exp", None, None),
        P(None, "exp"),
    )
    return jax.shard_map(
        on_device, mesh=mesh, in_specs=in_specs, out_specs=out_specs, check_vma=False
    )
```

```python
import functools

import jax
import jax.numpy as jnp
from jax import lax
from jax.experimental import pallas as pl
from jax.experimental.pallas import tpu as pltpu
from jax.sharding import PartitionSpec as P


D = 256
HD = 32
FH = 1024
N1 = 1024
N2 = 2048
TB = N1
HC = 1024
LIMIT = 36
F32 = jnp.float32
BF = jnp.bfloat16


def mm(a, b):
    return jnp.dot(a, b, preferred_element_type=F32)


def mm_nt(a, b):
    return lax.dot_general(a, b, (((1,), (1,)), ((), ())), preferred_element_type=F32)


def split2(x):
    hi = x.astype(BF)
    return hi, (x - hi.astype(F32)).astype(BF)


def flip(x):
    return x.astype(F32).T


def head_mask(rows, cols):
    r = lax.broadcasted_iota(jnp.int32, (rows, cols), 0) // HD
    c = lax.broadcasted_iota(jnp.int32, (rows, cols), 1) // HD
    return r == c


def pack_heads(full):
    full = jnp.where(head_mask(D, D), full, 0.0)
    parts = []
    for g in range(2):
        cols = full[:, 128 * g : 128 * g + 128]
        parts.append(sum(cols[128 * g + HD * h : 128 * g + HD * h + HD] for h in range(4)))
    return parts


def unpack_heads(packed):
    mask = head_mask(128, 128)
    zero = jnp.zeros((128, 128), F32)
    blocks = []
    for g in range(2):
        piece = packed[HD * g : HD * g + HD]
        blocks.append(jnp.where(mask, jnp.concatenate([piece] * 4, axis=0), 0.0))
    top = jnp.concatenate([blocks[0], zero], axis=1)
    low = jnp.concatenate([zero, blocks[1]], axis=1)
    return jnp.concatenate([top, low], axis=0)


def ordered(core, own, other):
    first = core == 0
    return jnp.where(first, own, other), jnp.where(first, other, own)


def row_of(halves):
    return jnp.concatenate([half[HD : HD + 8] for half in halves], axis=1)


def heads_of(halves):
    return unpack_heads(jnp.concatenate([half[:HD] for half in halves], axis=0))


def column_of(row):
    n = row.shape[1]
    r = lax.broadcasted_iota(jnp.int32, (n, n), 0)
    c = lax.broadcasted_iota(jnp.int32, (n, n), 1)
    return jnp.sum(jnp.where(r == c, row, 0.0), axis=1, keepdims=True)


def call(kernel, out_shape, flops, nbytes, name, scratch=(), after=(), limit=8, fetch=0):
    def run(at, *args):
        n_in, n_after = len(args), len(after)

        def body(*refs):
            ins, outs = list(refs[1 : 1 + n_in]), refs[1 + n_in + n_after :]
            if fetch:
                outs, bufs, sems = outs[: -fetch - 1], outs[-fetch - 1 : -1], outs[-1]
                copies = [pltpu.make_async_copy(ins[k], bufs[k], sems.at[k]) for k in range(fetch)]
                for copy in copies:
                    copy.start()
                for copy in copies:
                    copy.wait()
                ins[:fetch] = bufs
            kernel(refs[0], *ins, *outs)

        in_vmem = pl.BlockSpec(memory_space=pltpu.VMEM)
        in_any = pl.BlockSpec(memory_space=pl.ANY)
        more = [pltpu.VMEM(x.shape, x.dtype) for x in args[:fetch]]
        return pl.pallas_call(
            body,
            in_specs=[pl.BlockSpec(memory_space=pltpu.SMEM)]
            + [pl.BlockSpec(memory_space=pltpu.HBM)] * fetch
            + [in_vmem] * (n_in - fetch)
            + [in_any] * n_after,
            out_specs=[in_vmem] * len(out_shape),
            out_shape=out_shape,
            scratch_shapes=list(scratch) + (more + [pltpu.SemaphoreType.DMA((fetch,))] if fetch else []),
            compiler_params=pltpu.CompilerParams(vmem_limit_bytes=limit * 1024 * 1024),
            cost_estimate=pl.CostEstimate(flops=int(flops), bytes_accessed=int(nbytes), transcendentals=0),
            name=name,
        )(at, *[pltpu.with_memory_space_constraint(x, pltpu.HBM) for x in args[:fetch]], *args[fetch:], *after)

    return run


def struct(shape, dtype):
    return jax.ShapeDtypeStruct(shape, dtype)


def add(terms, after=(), dtype=BF):
    if after:
        terms = lax.optimization_barrier((*terms, *after))[: len(terms)]
    total = terms[0].astype(F32)
    for term in terms[1:]:
        total = total + term.astype(F32)
    return total.astype(dtype)


def chips_kernel(at_ref, every_ref, out_ref):
    total = every_ref[0].astype(F32)
    for k in range(1, 16):
        total = total + every_ref[k].astype(F32)
    out_ref[...] = total.astype(out_ref.dtype)


def chips_call(at, every, after=()):
    out = struct(every.shape[1:], every.dtype)
    return call(chips_kernel, (out,), 1e6, 1e6, "experts_sum", after=after)(at, every)[0]


def keys_values(tokt, keep, wk, wv):
    kpre = mm(flip(wk).astype(BF), tokt)
    val = mm(flip(wv).astype(BF), tokt).astype(BF)
    low = jnp.exp(jnp.minimum(kpre, 0.0))
    km = (keep * jnp.where(kpre > 0, kpre + 1.0, low)).astype(BF)
    return km, val, keep * jnp.where(kpre > 0, 1.0, low)


def keys_kernel(at_ref, tok_ref, keep_ref, coords_ref, wk_ref, wv_ref, ck_ref, msg_ref, keep_m, send_m, km_buf):
    core = at_ref[0]
    tokt = flip(tok_ref[...]).astype(BF)
    keep = keep_ref[...].astype(F32)
    ck_ref[0:3, :] = coords_ref[...]
    ck_ref[3:4, :] = keep
    km, val, _ = keys_values(tokt, keep, wk_ref[...], wv_ref[...])
    km_buf[...] = km
    parts = pack_heads(mm_nt(val, km))
    ks = mm_nt(jnp.ones((8, N1), BF), km)
    for g in range(2):
        msg_ref[40 * g : 40 * g + 32, :] = parts[g]
        msg_ref[40 * g + 32 : 40 * g + 40, :] = ks[:, 128 * g : 128 * g + 128]
    for ref, half in ((keep_m, core), (send_m, 1 - core)):
        rows = pl.ds(pl.multiple_of(half * 128, 128), 128)
        ref[...] = mm_nt(tokt, km_buf[rows, :]).astype(BF)


def keys_call(at, tokens, keep_row, coords, wk, wv):
    return call(
        keys_kernel,
        (struct((4, N1), F32), struct((80, 128), F32), struct((D, 128), BF), struct((D, 128), BF)),
        4e8, 3e6, "keys", [pltpu.VMEM((D, N1), BF)], fetch=5,
    )(at, tokens, keep_row, coords, wk, wv)


def again_kernel(at_ref, tok_ref, keep_ref, wq_ref, wk_ref, wv_ref, tokt_ref, q_ref, qslope_ref, km_ref, v_ref, slope_ref):
    tokt = flip(tok_ref[...]).astype(BF)
    tokt_ref[...] = tokt
    pre = mm(flip(wq_ref[...]).astype(BF), tokt)
    low = jnp.exp(jnp.minimum(pre, 0.0))
    q_ref[...] = jnp.where(pre > 0, pre + 1.0, low).astype(BF)
    qslope_ref[...] = jnp.where(pre > 0, 1.0, low)
    km_ref[...], v_ref[...], slope_ref[...] = keys_values(tokt, keep_ref[...].astype(F32), wk_ref[...], wv_ref[...])


def again_call(at, tokens, keep_row, wq, wk, wv, after):
    return call(
        again_kernel,
        (
            struct((D, N1), BF), struct((D, N1), BF), struct((D, N1), F32),
            struct((D, N1), BF), struct((D, N1), BF), struct((D, N1), F32),
        ),
        5e8, 3e6, "queries_keys_again", after=after, fetch=5,
    )(at, tokens, keep_row, wq, wk, wv)


def query_kernel(at_ref, tok_ref, wq_ref, tokt_ref, q_ref):
    tokt = flip(tok_ref[...]).astype(BF)
    tokt_ref[...] = tokt
    pre = mm(flip(wq_ref[...]).astype(BF), tokt)
    q_ref[...] = jnp.where(pre > 0, pre + 1.0, jnp.exp(jnp.minimum(pre, 0.0))).astype(BF)


def query_call(at, tokens, wq, name):
    out = (struct((D, N1), BF), struct((D, N1), BF))
    return call(query_kernel, out, 2e8, 2e6, name, fetch=2)(at, tokens, wq)


def gate_kernel(at_ref, wgeo_ref, bgeo_ref, wroute_ref, ck_ref, cko_ref, r_ref, g_ref):
    geo = [column_of(wgeo_ref[k : k + 1, :]) for k in range(3)]
    bias = column_of(bgeo_ref[...])
    for half, ref in enumerate((ck_ref, cko_ref)):
        cols = slice(N1 * half, N1 * half + N1)
        pre = bias
        for k in range(3):
            pre = pre + geo[k] * ref[k : k + 1, :]
        r = jnp.tanh(pre)
        r_ref[:, cols] = r
        logit = jnp.dot(wroute_ref[...], r, precision=lax.Precision.HIGHEST, preferred_element_type=F32)
        expo = jnp.exp(logit)
        g_ref[:, cols] = expo / jnp.sum(expo, axis=0, keepdims=True)


def gate_call(at, wgeo, bgeo, wroute, ck, ck_o):
    out = (struct((64, N2), F32), struct((8, N2), F32))
    return call(gate_kernel, out, 1e8, 1e6, "gate", fetch=3)(at, wgeo, bgeo, wroute, ck, ck_o)


def own_gate(at_ref, gates):
    mine = lax.broadcasted_iota(jnp.int32, gates.shape, 0) == at_ref[1]
    return jnp.sum(jnp.where(mine, gates, 0.0), axis=0, keepdims=True), mine


def back_kernel(at_ref, cot_ref, oth_ref, ck_ref, cko_ref, g_ref, win_ref, wout_ref, dy_ref, df_ref, back_ref, wint_ref):
    core = at_ref[0]
    dy_ref[...] = (flip(cot_ref[...]) * ck_ref[3:4, :] * jnp.where(at_ref[2] == 0, 1.0, 0.0)).astype(BF)
    for half, (ref, keep_ref) in enumerate(((cot_ref, ck_ref), (oth_ref, cko_ref))):
        cot = ref[...]
        keep = keep_ref[3:4, :]
        cols = slice(N1 * half, N1 * half + N1)
        gate = keep * own_gate(at_ref, g_ref[:, cols])[0]
        df_ref[:, cols] = (flip(cot) * gate).astype(BF)
        for j in range(0, FH, 256):
            back_ref[j : j + 256, cols] = mm_nt(wout_ref[core, j : j + 256, :], cot) * gate
    wint_ref[...] = flip(win_ref[core]).astype(BF)


def back_call(at, cot, cot_o, ck, ck_o, g, w_in, w_out):
    out = (struct((D, N1), BF), struct((D, N2), BF), struct((FH, N2), F32), struct((FH, D), BF))
    return call(back_kernel, out, 11e8, 8e6, "cotangent_back", limit=12)(at, cot, cot_o, ck, ck_o, g, w_in, w_out)


GELU_A = 0.7978845608028654
GELU_B = 0.7978845608028654 * 0.044715


def expert_kernel(
    at_ref, msg_ref, m_ref, mo_ref, tokt_ref, tokto_ref, q_ref, qo_ref, dy_ref, df_ref, back_ref, g_ref, r_ref, win_ref, wint_ref,
    own_ref, oth_ref, kvt_ref, ks_ref, keep_msg, send_msg, pieces_ref,
    gw1, gw2, dkv, route,
):
    core = at_ref[0]
    halves = msg_ref[0:40, :], msg_ref[40:80, :]
    kvt = heads_of(halves)
    ks = row_of(halves)
    kvt_ref[...] = kvt
    ks_ref[...] = ks
    kvh, kvl = split2(kvt)
    ksh, ksl = split2(jnp.where(head_mask(D, D), ks[0:1], 0.0))
    sums = jnp.concatenate([kvh, kvl, ksh, ksl], axis=0)

    def step(i, first):
        cols = slice(TB * i, TB * i + TB)
        q = (q_ref if i == 0 else qo_ref)[...]
        tokt = (tokt_ref if i == 0 else tokto_ref)[...]
        both = mm(sums, q)
        rden = 1.0 / (both[2 * D : 3 * D] + both[3 * D :])
        attn = (both[:D] + both[D : 2 * D]) * rden
        mid = (tokt.astype(F32) + attn).astype(BF)
        df = df_ref[:, cols]
        dmid = dy_ref[:, cols].astype(F32) if TB * i < N1 else jnp.zeros((D, TB), F32)
        stat = jnp.zeros((1, TB), F32)
        for j in range(0, FH, HC):
            rows = slice(j, j + HC)
            u = mm(wint_ref[rows, :], mid)
            u2 = u * u
            half = 0.5 + 0.5 * jnp.tanh(u * (GELU_A + GELU_B * u2))
            act = u * half
            slope = half + act * (1.0 - half) * (2.0 * GELU_A + 6.0 * GELU_B * u2)
            back = back_ref[rows, cols]
            act = act.astype(BF)
            stat = stat + jnp.sum(act.astype(F32) * back, axis=0, keepdims=True)
            du = (back * slope).astype(BF)
            dw2, dw1 = mm_nt(act, df), mm_nt(du, mid)
            gw2[rows, :] = dw2 if first else gw2[rows, :] + dw2
            gw1[rows, :] = dw1 if first else gw1[rows, :] + dw1
            dmid = dmid + mm(win_ref[core, :, rows], du)
        gates = g_ref[:, cols]
        mine = own_gate(at_ref, gates)[1]
        turn = (jnp.where(mine, 1.0, 0.0) - gates) * stat
        dnum = dmid * rden
        dden = -jnp.sum((dnum * attn).reshape(8, HD, TB), axis=1)
        lhs = jnp.concatenate([*split2(dnum), *split2(jnp.concatenate([dden, dden], axis=0))], axis=0)
        dkv_part = mm_nt(lhs, q)
        route_part = lax.dot_general(
            turn, r_ref[:, cols], (((1,), (1,)), ((), ())), precision=lax.Precision.HIGHEST, preferred_element_type=F32
        )
        dkv[...] = dkv_part if first else dkv[...] + dkv_part
        route[...] = route_part if first else route[...] + route_part
        for k in range(TB // 512):
            at_col = TB * i + 512 * k
            piece = dmid[:, 512 * k : 512 * k + 512]
            if at_col < N1:
                own_ref[:, at_col : at_col + 512] = piece
            else:
                oth_ref[:, at_col - N1 : at_col - N1 + 512] = piece.astype(BF)

    for i in range(N2 // TB):
        step(i, i == 0)

    m = (m_ref[...].astype(F32) + mo_ref[...].astype(F32)).astype(BF)
    for k in range(16):
        rows = slice(64 * k, 64 * k + 64)
        pieces_ref[k, 0:64, :] = gw1[rows, :].astype(BF)
        pieces_ref[k, 64:128, :] = gw2[rows, :].astype(BF)
        pieces_ref[k, 128:144, 0:128] = m[16 * k : 16 * k + 16]
        pieces_ref[k, 128:144, 128:256] = jnp.zeros((16, 128), BF)
    parts = pack_heads(dkv[0:D, :] + dkv[D : 2 * D, :])
    r = lax.broadcasted_iota(jnp.int32, (8, D), 0)
    c = lax.broadcasted_iota(jnp.int32, (8, D), 1) // HD
    sums = jnp.where(r == c, dkv[2 * D : 2 * D + 8, :] + dkv[2 * D + 16 : 2 * D + 24, :], 0.0)
    last = [jnp.concatenate([route[...], jnp.zeros((8, 64), F32)], axis=1), jnp.zeros((8, 128), F32)]
    halves = [jnp.concatenate([parts[g], sums[:, 128 * g : 128 * g + 128], last[g]], axis=0) for g in range(2)]
    keep_msg[...], send_msg[...] = ordered(core, *halves)


def expert_call(at, msg, m, m_o, tokt, tokt_o, q, q_o, dy, df, back, g, r, w_in, wint):
    return call(
        expert_kernel,
        (
            struct((D, N1), F32), struct((D, N1), BF), struct((D, D), F32), struct((8, D), F32),
            struct((48, 128), F32), struct((48, 128), F32), struct((16, 144, D), BF),
        ),
        6e9, 12e6, "expert",
        [pltpu.VMEM((FH, D), F32)] * 2 + [pltpu.VMEM((2 * D + 32, D), F32), pltpu.VMEM((8, 64), F32)],
        limit=LIMIT,
    )(at, msg, m, m_o, tokt, tokt_o, q, q_o, dy, df, back, g, r, w_in, wint)


def dmid_kernel(at_ref, own_ref, oth_ref, msg_ref, msgo_ref, *out_refs):
    hi, lo = split2(msg_ref[...] + msgo_ref[...])
    for d, ref in enumerate(out_refs):
        cols = pl.ds(pl.multiple_of(lax.rem(at_ref[2] + d, 4) * 256, 256), 256)
        ref[0:256, :] = (own_ref[:, cols] + oth_ref[:, cols].astype(F32)).astype(ref.dtype)
        ref[256:304, 0:128] = hi.astype(ref.dtype)
        ref[256:304, 128:256] = lo.astype(ref.dtype)


def dmid_call(at, own, oth, msg, msg_o):
    return call(dmid_kernel, (struct((304, 256), F32),) + (struct((304, 256), BF),) * 3, 1e6, 2e6, "dmid_pieces")(at, own, oth, msg, msg_o)


def back_query_kernel(
    at_ref, d0, d1, d2, d3, kvt_ref, ks_ref, tokt_ref, q_ref, qslope_ref, wq_ref, gx_ref, gq_ref, dmid_ref
):
    for d, ref in enumerate((d0, d1, d2, d3)):
        cols = pl.ds(pl.multiple_of(lax.rem(at_ref[2] + 4 - d, 4) * 256, 256), 256)
        dmid_ref[:, cols] = ref[...].astype(F32)
    dmid = dmid_ref[...]
    q = q_ref[...]
    tokt = tokt_ref[...]
    kvt = kvt_ref[...]
    kvth, kvtl = split2(kvt)
    kvh, kvl = split2(kvt.T)
    ks = ks_ref[0:1, :]
    mask = head_mask(D, D)
    ksh, ksl = split2(jnp.where(mask, ks, 0.0))
    kch, kcl = split2(jnp.where(mask, column_of(ks), 0.0))
    both = mm(jnp.concatenate([kvth, kvtl, ksh, ksl], axis=0), q)
    rden = 1.0 / (both[2 * D : 3 * D] + both[3 * D :])
    attn = (both[:D] + both[D : 2 * D]) * rden
    dnum = dmid * rden
    nh, nl = split2(dnum)
    zh, zl = split2(dnum * attn)
    left = jnp.concatenate([kvh, -kch], axis=1)
    both = mm(jnp.concatenate([left, jnp.concatenate([kvl, -kcl], axis=1)], axis=0), jnp.concatenate([nh, zh], axis=0))
    dq = both[:D] + both[D:] + mm(left, jnp.concatenate([nl, zl], axis=0))
    wq = wq_ref[...]
    dqp = (dq * qslope_ref[...]).astype(BF)
    gx_ref[...] = dmid + mm(wq, dqp)
    gq_ref[...] = mm_nt(tokt, dqp)


def back_query_call(at, dm, kvt, ks, tokt, q, qslope, wq, after):
    out = (struct((D, N1), F32), struct((D, D), F32))
    return call(back_query_kernel, out, 2e9, 5e6, "back_query", [pltpu.VMEM((D, N1), F32)], after)(
        at, *dm, kvt, ks, tokt, q, qslope, wq
    )


def back_keys_kernel(at_ref, msg_ref, msgo_ref, km_ref, v_ref, slope_ref, tokt_ref, gq_ref, dk_ref, dv_ref, keep_ref, send_ref):
    core = at_ref[0]
    halves = ordered(core, msg_ref[...], msgo_ref[...])
    dkvt = heads_of(halves)
    dks = jnp.sum(row_of(halves), axis=0, keepdims=True)
    hi, lo = split2(dkvt.T)
    v = v_ref[...]
    dk = mm(hi, v) + mm(lo, v) + column_of(dks)
    dk = (dk * slope_ref[...]).astype(BF)
    hi, lo = split2(dkvt)
    km = km_ref[...]
    dk_ref[...] = dk
    dv_ref[...] = (mm(hi, km) + mm(lo, km)).astype(BF)
    for ref, part in ((keep_ref, core), (send_ref, 1 - core)):
        rows = pl.ds(pl.multiple_of(part * 128, 128), 128)
        ref[:, 0:D] = gq_ref[rows, :].astype(ref.dtype)
        ref[:, D : 2 * D] = mm_nt(tokt_ref[rows, 0:N1], dk).astype(ref.dtype)


def back_keys_call(at, msg, msg_o, km, v, slope, tokt, gq):
    out = (struct((D, N1), BF), struct((D, N1), BF), struct((128, 2 * D), F32), struct((128, 2 * D), BF))
    return call(back_keys_kernel, out, 1e9, 4e6, "back_keys")(at, msg, msg_o, km, v, slope, tokt, gq)


def grad_x_kernel(at_ref, gx_ref, dk_ref, dv_ref, wk_ref, wv_ref, out_ref):
    total = gx_ref[...] + mm(wk_ref[...], dk_ref[...]) + mm(wv_ref[...], dv_ref[...])
    out_ref[...] = total.T.astype(BF)


def grad_x_call(at, gx, dk, dv, wk, wv):
    return call(grad_x_kernel, (struct((N1, D), BF),), 3e8, 3e6, "grad_x")(at, gx, dk, dv, wk, wv)[0]


def origin(at_ref, dx, dz):
    return lax.rem(at_ref[4] + 4 - dz, 4) * 4 + lax.rem(at_ref[3] + 4 - dx, 4)


def place_kernel(at_ref, *refs):
    ins, (gin_ref, gout_ref, buf) = refs[:8], refs[8:]

    def put(side):
        for dx in range(4):
            for dz in range(4):
                rows = pl.ds(pl.multiple_of(origin(at_ref, dx, dz) * 64, 64), 64)
                buf[rows, :] = ins[4 * side + dx][dz, 0:64, :].astype(F32)
                gout_ref[0, rows, :] = ins[4 * side + dx][dz, 64:128, :].astype(F32)
        for j in range(0, FH, 256):
            gin_ref[0, :, j : j + 256] = buf[j : j + 256, :].T

    for side in range(2):
        pl.when(pl.program_id(0) == side)(lambda side=side: put(side))


def place_call(at, pieces):
    expert = lambda i, at: (jnp.where(i == 0, at[0], 1 - at[0]), 0, 0)
    return pl.pallas_call(
        place_kernel,
        grid_spec=pltpu.PrefetchScalarGridSpec(
            num_scalar_prefetch=1,
            grid=(2,),
            in_specs=[pl.BlockSpec(memory_space=pltpu.VMEM)] * 8,
            out_specs=[pl.BlockSpec((1, D, FH), expert), pl.BlockSpec((1, FH, D), expert)],
            scratch_shapes=[pltpu.VMEM((FH, D), F32)],
        ),
        out_shape=(struct((2, D, FH), F32), struct((2, FH, D), F32)),
        compiler_params=pltpu.CompilerParams(vmem_limit_bytes=16 * 1024 * 1024),
        cost_estimate=pl.CostEstimate(flops=1000000, bytes_accessed=7000000, transcendentals=0),
        name="place_experts",
    )(at, *pieces)


def place_m_kernel(at_ref, msg_ref, msgo_ref, *refs):
    ins, (gv_ref, route_ref, buf) = refs[:8], refs[8:]
    core, y = at_ref[0], at_ref[2]
    halves = ordered(core, msg_ref[...], msgo_ref[...])
    hi, lo = split2(heads_of(halves).T)
    for side in range(2):
        for dx in range(4):
            for dz in range(4):
                rows = pl.ds(pl.multiple_of(origin(at_ref, dx, dz) * 16, 16), 16)
                buf[side, rows, :] = ins[4 * side + dx][dz, 128:144, 0:128]
    m = jnp.concatenate(ordered(core, buf[0], buf[1]), axis=1)
    gv_ref[...] = mm(m, hi) + mm(m, lo)
    sums = halves[0][40:48, 0:64]
    at_row = lax.broadcasted_iota(jnp.int32, sums.shape, 0)
    for e in range(2):
        route_ref[e : e + 1, :] = jnp.sum(jnp.where(at_row == 2 * y + e, sums, 0.0), axis=0, keepdims=True)


def place_m_call(at, msg, msg_o, pieces):
    out = (struct((D, D), F32), struct((2, 64), F32))
    return call(place_m_kernel, out, 1e8, 1e6, "grad_wv", [pltpu.VMEM((2, D, 128), BF)])(at, msg, msg_o, *pieces)


def place_proj_kernel(at_ref, own_ref, oth_ref, gq_ref, gk_ref):
    core = at_ref[0]
    for ref, part in ((own_ref, core), (oth_ref, 1 - core)):
        rows = pl.ds(pl.multiple_of(part * 128, 128), 128)
        gq_ref[rows, :] = ref[:, 0:D].astype(F32)
        gk_ref[rows, :] = ref[:, D : 2 * D].astype(F32)


def place_proj_call(at, own, oth):
    return call(place_proj_kernel, (struct((D, D), F32),) * 2, 1e6, 1e6, "place_projections")(at, own, oth)


def swap_core(v):
    return lax.ppermute(v, "pts", [(i, i ^ 1) for i in range(32)])


def to_x(v, d):
    return lax.ppermute(v, "pts", [(i, (i & ~6) | ((i + 2 * d) & 6)) for i in range(32)])


def to_z(v, d):
    return lax.ppermute(v, "pts", [(i, (i + 8 * d) % 32) for i in range(32)])


def to_y(v, d):
    return lax.ppermute(v, "exp", [(i, (i + d) % 4) for i in range(4)])


def star(v, to):
    return [to(v, d) for d in (1, 2, 3)]


CHIPS = [[2 * k + core for k in range(16)] for core in range(2)]


def exchange(v):
    return lax.all_to_all(v, "pts", 0, 0, axis_index_groups=CHIPS)


def on_device(
    tokens, coords, keep, cotangent, w_query, w_key, w_value, w_geo, b_geo, w_route, w_in, w_out
):
    pts = lax.axis_index("pts")
    y = lax.axis_index("exp")
    core = pts % 2
    at = jnp.stack([core, 2 * y + core, y, (pts // 2) % 4, pts // 8]).astype(jnp.int32)

    tokens_o, cot_o = swap_core(tokens), swap_core(cotangent)
    ck, msg, m, m_away = keys_call(at, tokens, keep[None, :], coords, w_key, w_value)
    ck_o, m_o = swap_core(ck), swap_core(m_away)
    tokt, q = query_call(at, tokens, w_query, "queries")
    tokt_o, q_o = query_call(at, tokens_o, w_query, "queries_other")
    r, g = gate_call(at, w_geo, b_geo[None, :], w_route.T, ck, ck_o)
    dy, df, back, wint = back_call(at, cotangent, cot_o, ck, ck_o, g, w_in, w_out)

    msg = add([msg, swap_core(msg)], (), F32)
    msg = add([msg] + star(msg, to_x), (q, g), F32)
    msg = add([msg] + star(msg, to_z), (back, q_o), F32)
    own, oth, kvt, ks, msg2, msg2_away, pieces = expert_call(
        at, msg, m, m_o, tokt, tokt_o, q, q_o, dy, df, back, g, r, w_in, wint
    )

    pieces = exchange(pieces)

    p0, p1, p2, p3 = dmid_call(at, own, swap_core(oth), msg2, swap_core(msg2_away))
    arrived = [p0, to_y(p1, 1), to_y(p2, 2), to_y(p3, 3)]
    msg2 = add([p[256:, :128] for p in arrived] + [p[256:, 128:] for p in arrived], (), F32)
    dm = add([p[:256] for p in arrived], (), BF)
    dm = [dm] + star(dm, to_y)
    msg2 = msg2_z = add([msg2] + star(msg2, to_z), (), F32)

    pieces = chips_call(at, pieces, (msg2_z,))

    tokt, q, qslope, km, v, slope = again_call(at, tokens, keep[None, :], w_query, w_key, w_value, (pieces,))
    gx, gq = back_query_call(at, dm, kvt, ks, tokt, q, qslope, w_query, ())
    msg2 = add([msg2] + star(msg2, to_x), (gq,), F32)
    msg2_o = swap_core(msg2)
    dk, dv, part, away = back_keys_call(at, msg2, msg2_o, km, v, slope, tokt, gq)

    pieces = jnp.stack([pieces] + star(pieces, to_z))
    pieces = [pieces] + star(pieces, to_x)
    pieces = pieces + [swap_core(piece) for piece in pieces]
    grad_x = grad_x_call(at, gx, dk, dv, w_key, w_value)
    grad_w_in, grad_w_out = place_call(at, pieces)
    grad_wv, grad_route = place_m_call(at, msg2, msg2_o, pieces)

    part = add([part, swap_core(away)])
    part = add([part] + star(part, to_z), (grad_x,))
    part = add([part] + star(part, to_x), (grad_w_in, grad_wv))
    grad_wq, grad_wk = place_proj_call(at, part, swap_core(part))
    return (grad_x, grad_wq, grad_wk, grad_wv, grad_w_in, grad_w_out, grad_route.T)


def solution(mesh):
    in_specs = (
        P("pts", None),
        P(None, "pts"),
        P("pts"),
        P("pts", None),
        P(),
        P(),
        P(),
        P(),
        P(),
        P(),
        P("exp", None, None),
        P("exp", None, None),
    )
    out_specs = (
        P("pts", None),
        P(),
        P(),
        P(),
        P("exp", None, None),
        P("exp", None, None),
        P(None, "exp"),
    )
    return jax.shard_map(
        on_device, mesh=mesh, in_specs=in_specs, out_specs=out_specs, check_vma=False
    )
```

```python
import functools

import jax
import jax.numpy as jnp
from jax import lax
from jax.experimental import pallas as pl
from jax.experimental.pallas import tpu as pltpu
from jax.sharding import PartitionSpec as P


D = 256
HD = 32
FH = 1024
N1 = 1024
N2 = 2048
TB = N1
HC = 1024
LIMIT = 36
F32 = jnp.float32
BF = jnp.bfloat16


def mm(a, b):
    return jnp.dot(a, b, preferred_element_type=F32)


def mm_nt(a, b):
    return lax.dot_general(a, b, (((1,), (1,)), ((), ())), preferred_element_type=F32)


def split2(x):
    hi = x.astype(BF)
    return hi, (x - hi.astype(F32)).astype(BF)


def flip(x):
    return x.astype(F32).T


def head_mask(rows, cols):
    r = lax.broadcasted_iota(jnp.int32, (rows, cols), 0) // HD
    c = lax.broadcasted_iota(jnp.int32, (rows, cols), 1) // HD
    return r == c


def pack_heads(full):
    full = jnp.where(head_mask(D, D), full, 0.0)
    parts = []
    for g in range(2):
        cols = full[:, 128 * g : 128 * g + 128]
        parts.append(sum(cols[128 * g + HD * h : 128 * g + HD * h + HD] for h in range(4)))
    return parts


def unpack_heads(packed):
    mask = head_mask(128, 128)
    zero = jnp.zeros((128, 128), F32)
    blocks = []
    for g in range(2):
        piece = packed[HD * g : HD * g + HD]
        blocks.append(jnp.where(mask, jnp.concatenate([piece] * 4, axis=0), 0.0))
    top = jnp.concatenate([blocks[0], zero], axis=1)
    low = jnp.concatenate([zero, blocks[1]], axis=1)
    return jnp.concatenate([top, low], axis=0)


def ordered(core, own, other):
    first = core == 0
    return jnp.where(first, own, other), jnp.where(first, other, own)


def row_of(halves):
    return jnp.concatenate([half[HD : HD + 8] for half in halves], axis=1)


def heads_of(halves):
    return unpack_heads(jnp.concatenate([half[:HD] for half in halves], axis=0))


def column_of(row):
    n = row.shape[1]
    r = lax.broadcasted_iota(jnp.int32, (n, n), 0)
    c = lax.broadcasted_iota(jnp.int32, (n, n), 1)
    return jnp.sum(jnp.where(r == c, row, 0.0), axis=1, keepdims=True)


def call(kernel, out_shape, flops, nbytes, name, scratch=(), after=(), limit=8, fetch=0):
    def run(at, *args):
        n_in, n_after = len(args), len(after)

        def body(*refs):
            ins, outs = list(refs[1 : 1 + n_in]), refs[1 + n_in + n_after :]
            if fetch:
                outs, bufs, sems = outs[: -fetch - 1], outs[-fetch - 1 : -1], outs[-1]
                copies = [pltpu.make_async_copy(ins[k], bufs[k], sems.at[k]) for k in range(fetch)]
                for copy in copies:
                    copy.start()
                for copy in copies:
                    copy.wait()
                ins[:fetch] = bufs
            kernel(refs[0], *ins, *outs)

        in_vmem = pl.BlockSpec(memory_space=pltpu.VMEM)
        in_any = pl.BlockSpec(memory_space=pl.ANY)
        more = [pltpu.VMEM(x.shape, x.dtype) for x in args[:fetch]]
        return pl.pallas_call(
            body,
            in_specs=[pl.BlockSpec(memory_space=pltpu.SMEM)]
            + [pl.BlockSpec(memory_space=pltpu.HBM)] * fetch
            + [in_vmem] * (n_in - fetch)
            + [in_any] * n_after,
            out_specs=[in_vmem] * len(out_shape),
            out_shape=out_shape,
            scratch_shapes=list(scratch) + (more + [pltpu.SemaphoreType.DMA((fetch,))] if fetch else []),
            compiler_params=pltpu.CompilerParams(vmem_limit_bytes=limit * 1024 * 1024),
            cost_estimate=pl.CostEstimate(flops=int(flops), bytes_accessed=int(nbytes), transcendentals=0),
            name=name,
        )(at, *[pltpu.with_memory_space_constraint(x, pltpu.HBM) for x in args[:fetch]], *args[fetch:], *after)

    return run


def struct(shape, dtype):
    return jax.ShapeDtypeStruct(shape, dtype)


def add(terms, after=(), dtype=BF):
    if after:
        terms = lax.optimization_barrier((*terms, *after))[: len(terms)]
    total = terms[0].astype(F32)
    for term in terms[1:]:
        total = total + term.astype(F32)
    return total.astype(dtype)


def chips_kernel(at_ref, every_ref, out_ref):
    total = every_ref[0].astype(F32)
    for k in range(1, 16):
        total = total + every_ref[k].astype(F32)
    total = total.astype(out_ref.dtype)
    for k in range(16):
        out_ref[k] = total


def chips_call(at, every, after=()):
    return call(chips_kernel, (struct(every.shape, every.dtype),), 1e6, 1e6, "experts_sum", after=after)(at, every)[0]


def keys_values(tokt, keep, wk, wv):
    kpre = mm(flip(wk).astype(BF), tokt)
    val = mm(flip(wv).astype(BF), tokt).astype(BF)
    low = jnp.exp(jnp.minimum(kpre, 0.0))
    km = (keep * jnp.where(kpre > 0, kpre + 1.0, low)).astype(BF)
    return km, val, keep * jnp.where(kpre > 0, 1.0, low)


def keys_kernel(
    at_ref, tok_ref, keep_ref, coords_ref, wk_ref, wv_ref, wq_ref,
    ck_ref, msg_ref, keep_m, send_m, tokt_ref, wqt_ref, km_buf,
):
    core = at_ref[0]
    tokt = flip(tok_ref[...]).astype(BF)
    tokt_ref[...] = tokt
    wqt_ref[...] = flip(wq_ref[...]).astype(BF)
    keep = keep_ref[...].astype(F32)
    ck_ref[0:3, :] = coords_ref[...]
    ck_ref[3:4, :] = keep
    km, val, _ = keys_values(tokt, keep, wk_ref[...], wv_ref[...])
    km_buf[...] = km
    parts = pack_heads(mm_nt(val, km))
    ks = mm_nt(jnp.ones((8, N1), BF), km)
    for g in range(2):
        msg_ref[40 * g : 40 * g + 32, :] = parts[g]
        msg_ref[40 * g + 32 : 40 * g + 40, :] = ks[:, 128 * g : 128 * g + 128]
    for ref, half in ((keep_m, core), (send_m, 1 - core)):
        rows = pl.ds(pl.multiple_of(half * 128, 128), 128)
        ref[...] = mm_nt(tokt, km_buf[rows, :]).astype(BF)


def keys_call(at, tokens, keep_row, coords, wk, wv, wq):
    return call(
        keys_kernel,
        (
            struct((4, N1), F32), struct((80, 128), F32), struct((D, 128), BF), struct((D, 128), BF),
            struct((D, N1), BF), struct((D, D), BF),
        ),
        4e8, 3e6, "keys", [pltpu.VMEM((D, N1), BF)], fetch=6,
    )(at, tokens, keep_row, coords, wk, wv, wq)


def again_kernel(at_ref, tok_ref, keep_ref, wq_ref, wk_ref, wv_ref, tokt_ref, q_ref, qslope_ref, km_ref, v_ref, slope_ref):
    tokt = flip(tok_ref[...]).astype(BF)
    tokt_ref[...] = tokt
    pre = mm(flip(wq_ref[...]).astype(BF), tokt)
    low = jnp.exp(jnp.minimum(pre, 0.0))
    q_ref[...] = jnp.where(pre > 0, pre + 1.0, low).astype(BF)
    qslope_ref[...] = jnp.where(pre > 0, 1.0, low)
    km_ref[...], v_ref[...], slope_ref[...] = keys_values(tokt, keep_ref[...].astype(F32), wk_ref[...], wv_ref[...])


def again_call(at, tokens, keep_row, wq, wk, wv, after):
    return call(
        again_kernel,
        (
            struct((D, N1), BF), struct((D, N1), BF), struct((D, N1), F32),
            struct((D, N1), BF), struct((D, N1), BF), struct((D, N1), F32),
        ),
        5e8, 3e6, "queries_keys_again", after=after, fetch=5,
    )(at, tokens, keep_row, wq, wk, wv)


def query_of(tokt, wqt):
    pre = mm(wqt, tokt)
    return jnp.where(pre > 0, pre + 1.0, jnp.exp(jnp.minimum(pre, 0.0))).astype(BF)


def query_kernel(at_ref, tokt_ref, wqt_ref, q_ref):
    q_ref[...] = query_of(tokt_ref[...], wqt_ref[...])


def query_other_kernel(at_ref, tok_ref, wqt_ref, tokt_ref, q_ref):
    tokt = flip(tok_ref[...]).astype(BF)
    tokt_ref[...] = tokt
    q_ref[...] = query_of(tokt, wqt_ref[...])


def query_call(at, tokt, wqt):
    return call(query_kernel, (struct((D, N1), BF),), 2e8, 2e6, "queries")(at, tokt, wqt)[0]


def query_other_call(at, tokens, wqt):
    out = (struct((D, N1), BF), struct((D, N1), BF))
    return call(query_other_kernel, out, 2e8, 2e6, "queries_other")(at, tokens, wqt)


def gate_kernel(at_ref, wgeo_ref, bgeo_ref, wroute_ref, ck_ref, cko_ref, r_ref, g_ref):
    geo = [column_of(wgeo_ref[k : k + 1, :]) for k in range(3)]
    bias = column_of(bgeo_ref[...])
    for half, ref in enumerate((ck_ref, cko_ref)):
        cols = slice(N1 * half, N1 * half + N1)
        pre = bias
        for k in range(3):
            pre = pre + geo[k] * ref[k : k + 1, :]
        r = jnp.tanh(pre)
        r_ref[0:64, cols], r_ref[64:128, cols] = split2(r)
        logit = jnp.dot(wroute_ref[...], r, precision=lax.Precision.HIGHEST, preferred_element_type=F32)
        expo = jnp.exp(logit)
        g_ref[:, cols] = expo / jnp.sum(expo, axis=0, keepdims=True)


def gate_call(at, wgeo, bgeo, wroute, ck, ck_o):
    out = (struct((128, N2), BF), struct((8, N2), F32))
    return call(gate_kernel, out, 1e8, 1e6, "gate", fetch=3)(at, wgeo, bgeo, wroute, ck, ck_o)


def own_gate(at_ref, gates):
    mine = lax.broadcasted_iota(jnp.int32, gates.shape, 0) == at_ref[1]
    return jnp.sum(jnp.where(mine, gates, 0.0), axis=0, keepdims=True), mine


def back_kernel(at_ref, cot_ref, oth_ref, ck_ref, cko_ref, g_ref, win_ref, wout_ref, dy_ref, df_ref, back_ref, wint_ref):
    core = at_ref[0]
    dy_ref[...] = (flip(cot_ref[...]) * ck_ref[3:4, :] * jnp.where(at_ref[2] == 0, 1.0, 0.0)).astype(BF)
    for half, (ref, keep_ref) in enumerate(((cot_ref, ck_ref), (oth_ref, cko_ref))):
        cot = ref[...]
        keep = keep_ref[3:4, :]
        cols = slice(N1 * half, N1 * half + N1)
        gate = keep * own_gate(at_ref, g_ref[:, cols])[0]
        df_ref[:, cols] = (flip(cot) * gate).astype(BF)
        for j in range(0, FH, 256):
            back_ref[j : j + 256, cols] = mm_nt(wout_ref[core, j : j + 256, :], cot) * gate
    wint_ref[...] = flip(win_ref[core]).astype(BF)


def back_call(at, cot, cot_o, ck, ck_o, g, w_in, w_out):
    out = (struct((D, N1), BF), struct((D, N2), BF), struct((FH, N2), F32), struct((FH, D), BF))
    return call(back_kernel, out, 11e8, 8e6, "cotangent_back", limit=12)(at, cot, cot_o, ck, ck_o, g, w_in, w_out)


GELU_A = 0.7978845608028654
GELU_B = 0.7978845608028654 * 0.044715


def expert_kernel(
    at_ref, msg_ref, m_ref, mo_ref, tokt_ref, tokto_ref, q_ref, qo_ref, dy_ref, df_ref, back_ref, g_ref, r_ref, win_ref, wint_ref,
    own_ref, oth_ref, kvt_ref, ks_ref, keep_msg, send_msg, pieces_ref,
    gw1, gw2, dkv, route,
):
    core = at_ref[0]
    halves = msg_ref[0:40, :], msg_ref[40:80, :]
    kvt = heads_of(halves)
    ks = row_of(halves)
    kvt_ref[...] = kvt
    ks_ref[...] = ks
    kvh, kvl = split2(kvt)
    ksh, ksl = split2(jnp.where(head_mask(D, D), ks[0:1], 0.0))
    sums = jnp.concatenate([kvh, kvl, ksh, ksl], axis=0)

    def step(i, first):
        cols = slice(TB * i, TB * i + TB)
        q = (q_ref if i == 0 else qo_ref)[...]
        tokt = (tokt_ref if i == 0 else tokto_ref)[...]
        both = mm(sums, q)
        rden = 1.0 / (both[2 * D : 3 * D] + both[3 * D :])
        attn = (both[:D] + both[D : 2 * D]) * rden
        mid = (tokt.astype(F32) + attn).astype(BF)
        df = df_ref[:, cols]
        dmid = dy_ref[:, cols].astype(F32) if TB * i < N1 else jnp.zeros((D, TB), F32)
        stat = jnp.zeros((1, TB), F32)
        for j in range(0, FH, HC):
            rows = slice(j, j + HC)
            u = mm(wint_ref[rows, :], mid)
            u2 = u * u
            half = 0.5 + 0.5 * jnp.tanh(u * (GELU_A + GELU_B * u2))
            act = u * half
            slope = half + act * (1.0 - half) * (2.0 * GELU_A + 6.0 * GELU_B * u2)
            back = back_ref[rows, cols]
            act = act.astype(BF)
            stat = stat + jnp.sum(act.astype(F32) * back, axis=0, keepdims=True)
            du = (back * slope).astype(BF)
            dw2, dw1 = mm_nt(act, df), mm_nt(du, mid)
            gw2[rows, :] = dw2 if first else gw2[rows, :] + dw2
            gw1[rows, :] = dw1 if first else gw1[rows, :] + dw1
            dmid = dmid + mm(win_ref[core, :, rows], du)
        gates = g_ref[:, cols]
        mine = own_gate(at_ref, gates)[1]
        turn = (jnp.where(mine, 1.0, 0.0) - gates) * stat
        dnum = dmid * rden
        dden = -jnp.sum((dnum * attn).reshape(8, HD, TB), axis=1)
        lhs = jnp.concatenate([*split2(dnum), *split2(jnp.concatenate([dden, dden], axis=0))], axis=0)
        dkv_part = mm_nt(lhs, q)
        hi, lo = split2(jnp.concatenate([turn, turn], axis=0))
        both = mm_nt(jnp.concatenate([hi, lo], axis=0), r_ref[:, cols])
        route_part = both[0:8, 0:64] + (both[0:8, 64:128] + both[16:24, 0:64])
        dkv[...] = dkv_part if first else dkv[...] + dkv_part
        route[...] = route_part if first else route[...] + route_part
        for k in range(TB // 512):
            at_col = TB * i + 512 * k
            piece = dmid[:, 512 * k : 512 * k + 512]
            if at_col < N1:
                own_ref[:, at_col : at_col + 512] = piece
            else:
                oth_ref[:, at_col - N1 : at_col - N1 + 512] = piece.astype(BF)

    for i in range(N2 // TB):
        step(i, i == 0)

    m = (m_ref[...].astype(F32) + mo_ref[...].astype(F32)).astype(BF)
    for k in range(16):
        rows = slice(64 * k, 64 * k + 64)
        pieces_ref[k, 0:64, :] = gw1[rows, :].astype(BF)
        pieces_ref[k, 64:128, :] = gw2[rows, :].astype(BF)
        pieces_ref[k, 128:144, 0:128] = m[16 * k : 16 * k + 16]
        pieces_ref[k, 128:144, 128:256] = jnp.zeros((16, 128), BF)
    parts = pack_heads(dkv[0:D, :] + dkv[D : 2 * D, :])
    r = lax.broadcasted_iota(jnp.int32, (8, D), 0)
    c = lax.broadcasted_iota(jnp.int32, (8, D), 1) // HD
    sums = jnp.where(r == c, dkv[2 * D : 2 * D + 8, :] + dkv[2 * D + 16 : 2 * D + 24, :], 0.0)
    last = [jnp.concatenate([route[...], jnp.zeros((8, 64), F32)], axis=1), jnp.zeros((8, 128), F32)]
    halves = [jnp.concatenate([parts[g], sums[:, 128 * g : 128 * g + 128], last[g]], axis=0) for g in range(2)]
    keep_msg[...], send_msg[...] = ordered(core, *halves)


def expert_call(at, msg, m, m_o, tokt, tokt_o, q, q_o, dy, df, back, g, r, w_in, wint):
    return call(
        expert_kernel,
        (
            struct((D, N1), F32), struct((D, N1), BF), struct((D, D), F32), struct((8, D), F32),
            struct((48, 128), F32), struct((48, 128), F32), struct((16, 144, D), BF),
        ),
        6e9, 12e6, "expert",
        [pltpu.VMEM((FH, D), F32)] * 2 + [pltpu.VMEM((2 * D + 32, D), F32), pltpu.VMEM((8, 64), F32)],
        limit=LIMIT,
    )(at, msg, m, m_o, tokt, tokt_o, q, q_o, dy, df, back, g, r, w_in, wint)


def dmid_kernel(at_ref, own_ref, oth_ref, msg_ref, msgo_ref, *out_refs):
    hi, lo = split2(msg_ref[...] + msgo_ref[...])
    for d, ref in enumerate(out_refs):
        cols = pl.ds(pl.multiple_of(lax.rem(at_ref[2] + d, 4) * 256, 256), 256)
        ref[0:256, :] = (own_ref[:, cols] + oth_ref[:, cols].astype(F32)).astype(ref.dtype)
        ref[256:304, 0:128] = hi.astype(ref.dtype)
        ref[256:304, 128:256] = lo.astype(ref.dtype)


def dmid_call(at, own, oth, msg, msg_o):
    return call(dmid_kernel, (struct((304, 256), F32),) + (struct((304, 256), BF),) * 3, 1e6, 2e6, "dmid_pieces")(at, own, oth, msg, msg_o)


def back_query_kernel(
    at_ref, d0, d1, d2, d3, kvt_ref, ks_ref, tokt_ref, q_ref, qslope_ref, wq_ref, gx_ref, gq_ref, dmid_ref
):
    for d, ref in enumerate((d0, d1, d2, d3)):
        cols = pl.ds(pl.multiple_of(lax.rem(at_ref[2] + 4 - d, 4) * 256, 256), 256)
        dmid_ref[:, cols] = ref[...].astype(F32)
    dmid = dmid_ref[...]
    q = q_ref[...]
    tokt = tokt_ref[...]
    kvt = kvt_ref[...]
    kvth, kvtl = split2(kvt)
    kvh, kvl = split2(kvt.T)
    ks = ks_ref[0:1, :]
    mask = head_mask(D, D)
    ksh, ksl = split2(jnp.where(mask, ks, 0.0))
    kch, kcl = split2(jnp.where(mask, column_of(ks), 0.0))
    both = mm(jnp.concatenate([kvth, kvtl, ksh, ksl], axis=0), q)
    rden = 1.0 / (both[2 * D : 3 * D] + both[3 * D :])
    attn = (both[:D] + both[D : 2 * D]) * rden
    dnum = dmid * rden
    nh, nl = split2(dnum)
    zh, zl = split2(dnum * attn)
    left = jnp.concatenate([kvh, -kch], axis=1)
    both = mm(jnp.concatenate([left, jnp.concatenate([kvl, -kcl], axis=1)], axis=0), jnp.concatenate([nh, zh], axis=0))
    dq = both[:D] + both[D:] + mm(left, jnp.concatenate([nl, zl], axis=0))
    wq = wq_ref[...]
    dqp = (dq * qslope_ref[...]).astype(BF)
    gx_ref[...] = dmid + mm(wq, dqp)
    gq_ref[...] = mm_nt(tokt, dqp)


def back_query_call(at, dm, kvt, ks, tokt, q, qslope, wq, after):
    out = (struct((D, N1), F32), struct((D, D), F32))
    return call(back_query_kernel, out, 2e9, 5e6, "back_query", [pltpu.VMEM((D, N1), F32)], after)(
        at, *dm, kvt, ks, tokt, q, qslope, wq
    )


def back_keys_kernel(at_ref, msg_ref, msgo_ref, km_ref, v_ref, slope_ref, tokt_ref, gq_ref, dk_ref, dv_ref, keep_ref, send_ref):
    core = at_ref[0]
    halves = ordered(core, msg_ref[...], msgo_ref[...])
    dkvt = heads_of(halves)
    dks = jnp.sum(row_of(halves), axis=0, keepdims=True)
    hi, lo = split2(dkvt.T)
    v = v_ref[...]
    dk = mm(hi, v) + mm(lo, v) + column_of(dks)
    dk = (dk * slope_ref[...]).astype(BF)
    hi, lo = split2(dkvt)
    km = km_ref[...]
    dk_ref[...] = dk
    dv_ref[...] = (mm(hi, km) + mm(lo, km)).astype(BF)
    for ref, part in ((keep_ref, core), (send_ref, 1 - core)):
        rows = pl.ds(pl.multiple_of(part * 128, 128), 128)
        ref[:, 0:D] = gq_ref[rows, :].astype(ref.dtype)
        ref[:, D : 2 * D] = mm_nt(tokt_ref[rows, 0:N1], dk).astype(ref.dtype)


def back_keys_call(at, msg, msg_o, km, v, slope, tokt, gq):
    out = (struct((D, N1), BF), struct((D, N1), BF), struct((128, 2 * D), F32), struct((128, 2 * D), BF))
    return call(back_keys_kernel, out, 1e9, 4e6, "back_keys")(at, msg, msg_o, km, v, slope, tokt, gq)


def grad_x_kernel(at_ref, gx_ref, dk_ref, dv_ref, wk_ref, wv_ref, out_ref):
    total = gx_ref[...] + mm(wk_ref[...], dk_ref[...]) + mm(wv_ref[...], dv_ref[...])
    out_ref[...] = total.T.astype(BF)


def grad_x_call(at, gx, dk, dv, wk, wv):
    return call(grad_x_kernel, (struct((N1, D), BF),), 3e8, 3e6, "grad_x")(at, gx, dk, dv, wk, wv)[0]


def place_kernel(at_ref, own_ref, oth_ref, gin_ref, gout_ref):
    def put(ref, part):
        cols = slice(128 * part, 128 * part + 128)
        gin_ref[0] = jnp.concatenate([ref[k, 0:64, cols].astype(F32) for k in range(16)], axis=0).T
        for k in range(8):
            gout_ref[0, 64 * k : 64 * k + 64, :] = ref[8 * part + k, 64:128, :].astype(F32)

    step = pl.program_id(0)
    for s in range(4):
        pl.when(step == s)(lambda s=s: put(own_ref if s < 2 else oth_ref, s % 2))


def place_call(at, own, oth):
    expert = lambda i, at: jnp.where(i < 2, at[0], 1 - at[0])
    out = pl.BlockSpec((1, 128, FH), lambda i, at: (expert(i, at), lax.rem(i, 2), 0))
    out2 = pl.BlockSpec((1, 512, D), lambda i, at: (expert(i, at), lax.rem(i, 2), 0))
    return pl.pallas_call(
        place_kernel,
        grid_spec=pltpu.PrefetchScalarGridSpec(
            num_scalar_prefetch=1,
            grid=(4,),
            in_specs=[pl.BlockSpec(memory_space=pltpu.VMEM)] * 2,
            out_specs=[out, out2],
        ),
        out_shape=(struct((2, D, FH), F32), struct((2, FH, D), F32)),
        compiler_params=pltpu.CompilerParams(vmem_limit_bytes=32 * 1024 * 1024),
        cost_estimate=pl.CostEstimate(flops=1000000, bytes_accessed=7000000, transcendentals=0),
        name="place_experts",
    )(at, own, oth)


def place_m_kernel(at_ref, msg_ref, msgo_ref, own_ref, oth_ref, gv_ref, route_ref):
    core, y = at_ref[0], at_ref[2]
    halves = ordered(core, msg_ref[...], msgo_ref[...])
    hi, lo = split2(heads_of(halves).T)
    own = jnp.concatenate([own_ref[k, 128:144, 0:128].astype(F32) for k in range(16)], axis=0)
    oth = jnp.concatenate([oth_ref[k, 128:144, 0:128].astype(F32) for k in range(16)], axis=0)
    m = jnp.concatenate(ordered(core, own, oth), axis=1).astype(BF)
    gv_ref[...] = mm(m, hi) + mm(m, lo)
    sums = halves[0][40:48, 0:64]
    at_row = lax.broadcasted_iota(jnp.int32, sums.shape, 0)
    for e in range(2):
        route_ref[e : e + 1, :] = jnp.sum(jnp.where(at_row == 2 * y + e, sums, 0.0), axis=0, keepdims=True)


def place_m_call(at, msg, msg_o, own, oth):
    out = (struct((D, D), F32), struct((2, 64), F32))
    return call(place_m_kernel, out, 1e8, 1e6, "grad_wv")(at, msg, msg_o, own, oth)


def place_proj_kernel(at_ref, own_ref, oth_ref, gq_ref, gk_ref):
    core = at_ref[0]
    for ref, part in ((own_ref, core), (oth_ref, 1 - core)):
        rows = pl.ds(pl.multiple_of(part * 128, 128), 128)
        gq_ref[rows, :] = ref[:, 0:D].astype(F32)
        gk_ref[rows, :] = ref[:, D : 2 * D].astype(F32)


def place_proj_call(at, own, oth):
    return call(place_proj_kernel, (struct((D, D), F32),) * 2, 1e6, 1e6, "place_projections")(at, own, oth)


def swap_core(v):
    return lax.ppermute(v, "pts", [(i, i ^ 1) for i in range(32)])


def to_x(v, d):
    return lax.ppermute(v, "pts", [(i, (i & ~6) | ((i + 2 * d) & 6)) for i in range(32)])


def to_z(v, d):
    return lax.ppermute(v, "pts", [(i, (i + 8 * d) % 32) for i in range(32)])


def to_y(v, d):
    return lax.ppermute(v, "exp", [(i, (i + d) % 4) for i in range(4)])


def star(v, to):
    return [to(v, d) for d in (1, 2, 3)]


CHIPS = [[2 * k + core for k in range(16)] for core in range(2)]


def exchange(v):
    return lax.all_to_all(v, "pts", 0, 0, axis_index_groups=CHIPS)


def on_device(
    tokens, coords, keep, cotangent, w_query, w_key, w_value, w_geo, b_geo, w_route, w_in, w_out
):
    pts = lax.axis_index("pts")
    y = lax.axis_index("exp")
    core = pts % 2
    at = jnp.stack([core, 2 * y + core, y]).astype(jnp.int32)

    tokens_o, cot_o = swap_core(tokens), swap_core(cotangent)
    ck, msg, m, m_away, tokt, wqt = keys_call(at, tokens, keep[None, :], coords, w_key, w_value, w_query)
    ck_o, m_o = swap_core(ck), swap_core(m_away)
    q = query_call(at, tokt, wqt)
    tokt_o, q_o = query_other_call(at, tokens_o, wqt)
    r, g = gate_call(at, w_geo, b_geo[None, :], w_route.T, ck, ck_o)
    dy, df, back, wint = back_call(at, cotangent, cot_o, ck, ck_o, g, w_in, w_out)

    msg = add([msg, swap_core(msg)], (), F32)
    msg = add([msg] + star(msg, to_x), (q, g), F32)
    msg = add([msg] + star(msg, to_z), (back, q_o), F32)
    own, oth, kvt, ks, msg2, msg2_away, pieces = expert_call(
        at, msg, m, m_o, tokt, tokt_o, q, q_o, dy, df, back, g, r, w_in, wint
    )

    pieces = exchange(pieces)

    p0, p1, p2, p3 = dmid_call(at, own, swap_core(oth), msg2, swap_core(msg2_away))
    arrived = [p0, to_y(p1, 1), to_y(p2, 2), to_y(p3, 3)]
    msg2 = add([p[256:, :128] for p in arrived] + [p[256:, 128:] for p in arrived], (), F32)
    dm = add([p[:256] for p in arrived], (), BF)
    dm = [dm] + star(dm, to_y)
    msg2 = msg2_z = add([msg2] + star(msg2, to_z), (), F32)

    pieces = chips_call(at, pieces, (msg2_z,))
    around = star(msg2, to_x)
    pieces, *around = lax.optimization_barrier((pieces, *around))
    tokt, q, qslope, km, v, slope = again_call(at, tokens, keep[None, :], w_query, w_key, w_value, (pieces,))
    pieces = exchange(pieces)

    gx, gq = back_query_call(at, dm, kvt, ks, tokt, q, qslope, w_query, ())
    msg2 = add([msg2] + around, (), F32)
    msg2_o = swap_core(msg2)
    dk, dv, part, away = back_keys_call(at, msg2, msg2_o, km, v, slope, tokt, gq)
    grad_x = grad_x_call(at, gx, dk, dv, w_key, w_value)

    part = add([part, swap_core(away)])
    part = add([part] + star(part, to_z), (grad_x,))
    pieces, _ = lax.optimization_barrier((pieces, part))
    pieces_o = swap_core(pieces)
    grad_w_in, grad_w_out = place_call(at, pieces, pieces_o)
    grad_wv, grad_route = place_m_call(at, msg2, msg2_o, pieces, pieces_o)
    part = add([part] + star(part, to_x), (grad_w_in, grad_wv))
    grad_wq, grad_wk = place_proj_call(at, part, swap_core(part))
    return (grad_x, grad_wq, grad_wk, grad_wv, grad_w_in, grad_w_out, grad_route.T)


def solution(mesh):
    in_specs = (
        P("pts", None),
        P(None, "pts"),
        P("pts"),
        P("pts", None),
        P(),
        P(),
        P(),
        P(),
        P(),
        P(),
        P("exp", None, None),
        P("exp", None, None),
    )
    out_specs = (
        P("pts", None),
        P(),
        P(),
        P(),
        P("exp", None, None),
        P("exp", None, None),
        P(None, "exp"),
    )
    return jax.shard_map(
        on_device, mesh=mesh, in_specs=in_specs, out_specs=out_specs, check_vma=False
    )
```

```python
import functools

import jax
import jax.numpy as jnp
from jax import lax
from jax.experimental import pallas as pl
from jax.experimental.pallas import tpu as pltpu
from jax.sharding import PartitionSpec as P


D = 256
HD = 32
FH = 1024
N1 = 1024
N2 = 2048
TB = N1
HC = 1024
LIMIT = 36
F32 = jnp.float32
BF = jnp.bfloat16


def mm(a, b):
    return jnp.dot(a, b, preferred_element_type=F32)


def mm_nt(a, b):
    return lax.dot_general(a, b, (((1,), (1,)), ((), ())), preferred_element_type=F32)


def split2(x):
    hi = x.astype(BF)
    return hi, (x - hi.astype(F32)).astype(BF)


def flip(x):
    return x.astype(F32).T


def head_mask(rows, cols):
    r = lax.broadcasted_iota(jnp.int32, (rows, cols), 0) // HD
    c = lax.broadcasted_iota(jnp.int32, (rows, cols), 1) // HD
    return r == c


def pack_heads(full):
    full = jnp.where(head_mask(D, D), full, 0.0)
    parts = []
    for g in range(2):
        cols = full[:, 128 * g : 128 * g + 128]
        parts.append(sum(cols[128 * g + HD * h : 128 * g + HD * h + HD] for h in range(4)))
    return parts


def unpack_heads(packed):
    mask = head_mask(128, 128)
    zero = jnp.zeros((128, 128), F32)
    blocks = []
    for g in range(2):
        piece = packed[HD * g : HD * g + HD]
        blocks.append(jnp.where(mask, jnp.concatenate([piece] * 4, axis=0), 0.0))
    top = jnp.concatenate([blocks[0], zero], axis=1)
    low = jnp.concatenate([zero, blocks[1]], axis=1)
    return jnp.concatenate([top, low], axis=0)


def ordered(core, own, other):
    first = core == 0
    return jnp.where(first, own, other), jnp.where(first, other, own)


def row_of(halves):
    return jnp.concatenate([half[HD : HD + 8] for half in halves], axis=1)


def heads_of(halves):
    return unpack_heads(jnp.concatenate([half[:HD] for half in halves], axis=0))


def column_of(row):
    n = row.shape[1]
    r = lax.broadcasted_iota(jnp.int32, (n, n), 0)
    c = lax.broadcasted_iota(jnp.int32, (n, n), 1)
    return jnp.sum(jnp.where(r == c, row, 0.0), axis=1, keepdims=True)


def call(kernel, out_shape, flops, nbytes, name, scratch=(), after=(), limit=8, fetch=0):
    def run(at, *args):
        n_in, n_after = len(args), len(after)

        def body(*refs):
            ins, outs = list(refs[1 : 1 + n_in]), refs[1 + n_in + n_after :]
            if fetch:
                outs, bufs, sems = outs[: -fetch - 1], outs[-fetch - 1 : -1], outs[-1]
                copies = [pltpu.make_async_copy(ins[k], bufs[k], sems.at[k]) for k in range(fetch)]
                for copy in copies:
                    copy.start()
                for copy in copies:
                    copy.wait()
                ins[:fetch] = bufs
            kernel(refs[0], *ins, *outs)

        in_vmem = pl.BlockSpec(memory_space=pltpu.VMEM)
        in_any = pl.BlockSpec(memory_space=pl.ANY)
        more = [pltpu.VMEM(x.shape, x.dtype) for x in args[:fetch]]
        return pl.pallas_call(
            body,
            in_specs=[pl.BlockSpec(memory_space=pltpu.SMEM)]
            + [pl.BlockSpec(memory_space=pltpu.HBM)] * fetch
            + [in_vmem] * (n_in - fetch)
            + [in_any] * n_after,
            out_specs=[in_vmem] * len(out_shape),
            out_shape=out_shape,
            scratch_shapes=list(scratch) + (more + [pltpu.SemaphoreType.DMA((fetch,))] if fetch else []),
            compiler_params=pltpu.CompilerParams(vmem_limit_bytes=limit * 1024 * 1024),
            cost_estimate=pl.CostEstimate(flops=int(flops), bytes_accessed=int(nbytes), transcendentals=0),
            name=name,
        )(at, *[pltpu.with_memory_space_constraint(x, pltpu.HBM) for x in args[:fetch]], *args[fetch:], *after)

    return run


def struct(shape, dtype):
    return jax.ShapeDtypeStruct(shape, dtype)


def add(terms, after=(), dtype=BF):
    if after:
        terms = lax.optimization_barrier((*terms, *after))[: len(terms)]
    total = terms[0].astype(F32)
    for term in terms[1:]:
        total = total + term.astype(F32)
    return total.astype(dtype)


def chips_kernel(at_ref, every_ref, out_ref):
    total = every_ref[0].astype(F32)
    for k in range(1, 16):
        total = total + every_ref[k].astype(F32)
    total = total.astype(out_ref.dtype)
    for k in range(16):
        out_ref[k] = total


def chips_call(at, every, after=()):
    return call(chips_kernel, (struct(every.shape, every.dtype),), 1e6, 1e6, "experts_sum", after=after)(at, every)[0]


def keys_values(tokt, keep, wk, wv):
    kpre = mm(flip(wk).astype(BF), tokt)
    val = mm(flip(wv).astype(BF), tokt).astype(BF)
    low = jnp.exp(jnp.minimum(kpre, 0.0))
    km = (keep * jnp.where(kpre > 0, kpre + 1.0, low)).astype(BF)
    return km, val, keep * jnp.where(kpre > 0, 1.0, low)


def keys_kernel(
    at_ref, tok_ref, keep_ref, coords_ref, wk_ref, wv_ref, wq_ref,
    ck_ref, msg_ref, keep_m, send_m, tokt_ref, wqt_ref, km_buf,
):
    core = at_ref[0]
    tokt = flip(tok_ref[...]).astype(BF)
    tokt_ref[...] = tokt
    wqt_ref[...] = flip(wq_ref[...]).astype(BF)
    keep = keep_ref[...].astype(F32)
    ck_ref[0:3, :] = coords_ref[...]
    ck_ref[3:4, :] = keep
    km, val, _ = keys_values(tokt, keep, wk_ref[...], wv_ref[...])
    km_buf[...] = km
    parts = pack_heads(mm_nt(val, km))
    ks = mm_nt(jnp.ones((8, N1), BF), km)
    for g in range(2):
        msg_ref[40 * g : 40 * g + 32, :] = parts[g]
        msg_ref[40 * g + 32 : 40 * g + 40, :] = ks[:, 128 * g : 128 * g + 128]
    for ref, half in ((keep_m, core), (send_m, 1 - core)):
        rows = pl.ds(pl.multiple_of(half * 128, 128), 128)
        ref[...] = mm_nt(tokt, km_buf[rows, :]).astype(BF)


def keys_call(at, tokens, keep_row, coords, wk, wv, wq):
    return call(
        keys_kernel,
        (
            struct((4, N1), F32), struct((80, 128), F32), struct((D, 128), BF), struct((D, 128), BF),
            struct((D, N1), BF), struct((D, D), BF),
        ),
        4e8, 3e6, "keys", [pltpu.VMEM((D, N1), BF)], fetch=6,
    )(at, tokens, keep_row, coords, wk, wv, wq)


def again_kernel(at_ref, tok_ref, keep_ref, wq_ref, wk_ref, wv_ref, tokt_ref, q_ref, qslope_ref, km_ref, v_ref, slope_ref):
    tokt = flip(tok_ref[...]).astype(BF)
    tokt_ref[...] = tokt
    pre = mm(flip(wq_ref[...]).astype(BF), tokt)
    low = jnp.exp(jnp.minimum(pre, 0.0))
    q_ref[...] = jnp.where(pre > 0, pre + 1.0, low).astype(BF)
    qslope_ref[...] = jnp.where(pre > 0, 1.0, low)
    km_ref[...], v_ref[...], slope_ref[...] = keys_values(tokt, keep_ref[...].astype(F32), wk_ref[...], wv_ref[...])


def again_call(at, tokens, keep_row, wq, wk, wv, after):
    return call(
        again_kernel,
        (
            struct((D, N1), BF), struct((D, N1), BF), struct((D, N1), F32),
            struct((D, N1), BF), struct((D, N1), BF), struct((D, N1), F32),
        ),
        5e8, 3e6, "queries_keys_again", after=after, fetch=5,
    )(at, tokens, keep_row, wq, wk, wv)


def query_of(tokt, wqt):
    pre = mm(wqt, tokt)
    return jnp.where(pre > 0, pre + 1.0, jnp.exp(jnp.minimum(pre, 0.0))).astype(BF)


def query_kernel(at_ref, tokt_ref, wqt_ref, q_ref):
    q_ref[...] = query_of(tokt_ref[...], wqt_ref[...])


def query_other_kernel(at_ref, tok_ref, wqt_ref, tokt_ref, q_ref):
    tokt = flip(tok_ref[...]).astype(BF)
    tokt_ref[...] = tokt
    q_ref[...] = query_of(tokt, wqt_ref[...])


def query_call(at, tokt, wqt):
    return call(query_kernel, (struct((D, N1), BF),), 2e8, 2e6, "queries")(at, tokt, wqt)[0]


def query_other_call(at, tokens, wqt):
    out = (struct((D, N1), BF), struct((D, N1), BF))
    return call(query_other_kernel, out, 2e8, 2e6, "queries_other")(at, tokens, wqt)


def gate_kernel(at_ref, wgeo_ref, bgeo_ref, wroute_ref, ck_ref, cko_ref, r_ref, g_ref):
    geo = [column_of(wgeo_ref[k : k + 1, :]) for k in range(3)]
    bias = column_of(bgeo_ref[...])
    for half, ref in enumerate((ck_ref, cko_ref)):
        cols = slice(N1 * half, N1 * half + N1)
        pre = bias
        for k in range(3):
            pre = pre + geo[k] * ref[k : k + 1, :]
        r = jnp.tanh(pre)
        r_ref[0:64, cols], r_ref[64:128, cols] = split2(r)
        logit = jnp.dot(wroute_ref[...], r, precision=lax.Precision.HIGHEST, preferred_element_type=F32)
        expo = jnp.exp(logit)
        g_ref[:, cols] = expo / jnp.sum(expo, axis=0, keepdims=True)


def gate_call(at, wgeo, bgeo, wroute, ck, ck_o):
    out = (struct((128, N2), BF), struct((8, N2), F32))
    return call(gate_kernel, out, 1e8, 1e6, "gate", fetch=3)(at, wgeo, bgeo, wroute, ck, ck_o)


def own_gate(at_ref, gates):
    mine = lax.broadcasted_iota(jnp.int32, gates.shape, 0) == at_ref[1]
    return jnp.sum(jnp.where(mine, gates, 0.0), axis=0, keepdims=True), mine


def back_kernel(at_ref, cot_ref, oth_ref, ck_ref, cko_ref, g_ref, win_ref, wout_ref, dy_ref, df_ref, back_ref, wint_ref):
    core = at_ref[0]
    dy_ref[...] = (flip(cot_ref[...]) * ck_ref[3:4, :] * jnp.where(at_ref[2] == 0, 1.0, 0.0)).astype(BF)
    for half, (ref, keep_ref) in enumerate(((cot_ref, ck_ref), (oth_ref, cko_ref))):
        cot = ref[...]
        keep = keep_ref[3:4, :]
        cols = slice(N1 * half, N1 * half + N1)
        gate = keep * own_gate(at_ref, g_ref[:, cols])[0]
        df_ref[:, cols] = (flip(cot) * gate).astype(BF)
        for j in range(0, FH, 256):
            back_ref[j : j + 256, cols] = mm_nt(wout_ref[core, j : j + 256, :], cot) * gate
    wint_ref[...] = flip(win_ref[core]).astype(BF)


def back_call(at, cot, cot_o, ck, ck_o, g, w_in, w_out):
    out = (struct((D, N1), BF), struct((D, N2), BF), struct((FH, N2), F32), struct((FH, D), BF))
    return call(back_kernel, out, 11e8, 8e6, "cotangent_back", limit=12)(at, cot, cot_o, ck, ck_o, g, w_in, w_out)


GELU_A = 0.7978845608028654
GELU_B = 0.7978845608028654 * 0.044715


def expert_kernel(
    at_ref, msg_ref, m_ref, mo_ref, tokt_ref, tokto_ref, q_ref, qo_ref, dy_ref, df_ref, back_ref, g_ref, r_ref, win_ref, wint_ref,
    own_ref, oth_ref, kvt_ref, ks_ref, keep_msg, send_msg, pieces_ref,
    gw1, gw2, dkv, route,
):
    core = at_ref[0]
    halves = msg_ref[0:40, :], msg_ref[40:80, :]
    kvt = heads_of(halves)
    ks = row_of(halves)
    kvt_ref[...] = kvt
    ks_ref[...] = ks
    kvh, kvl = split2(kvt)
    ksh, ksl = split2(jnp.where(head_mask(D, D), ks[0:1], 0.0))
    sums = jnp.concatenate([kvh, kvl, ksh, ksl], axis=0)

    def step(i, first):
        cols = slice(TB * i, TB * i + TB)
        q = (q_ref if i == 0 else qo_ref)[...]
        tokt = (tokt_ref if i == 0 else tokto_ref)[...]
        both = mm(sums, q)
        rden = 1.0 / (both[2 * D : 3 * D] + both[3 * D :])
        attn = (both[:D] + both[D : 2 * D]) * rden
        mid = (tokt.astype(F32) + attn).astype(BF)
        df = df_ref[:, cols]
        dmid = dy_ref[:, cols].astype(F32) if TB * i < N1 else jnp.zeros((D, TB), F32)
        stat = jnp.zeros((1, TB), F32)
        for j in range(0, FH, HC):
            rows = slice(j, j + HC)
            u = mm(wint_ref[rows, :], mid)
            u2 = u * u
            half = 0.5 + 0.5 * jnp.tanh(u * (GELU_A + GELU_B * u2))
            act = u * half
            slope = half + act * (1.0 - half) * (2.0 * GELU_A + 6.0 * GELU_B * u2)
            back = back_ref[rows, cols]
            act = act.astype(BF)
            stat = stat + jnp.sum(act.astype(F32) * back, axis=0, keepdims=True)
            du = (back * slope).astype(BF)
            dw2, dw1 = mm_nt(act, df), mm_nt(du, mid)
            gw2[rows, :] = dw2 if first else gw2[rows, :] + dw2
            gw1[rows, :] = dw1 if first else gw1[rows, :] + dw1
            dmid = dmid + mm(win_ref[core, :, rows], du)
        gates = g_ref[:, cols]
        mine = own_gate(at_ref, gates)[1]
        turn = (jnp.where(mine, 1.0, 0.0) - gates) * stat
        dnum = dmid * rden
        dden = -jnp.sum((dnum * attn).reshape(8, HD, TB), axis=1)
        lhs = jnp.concatenate([*split2(dnum), *split2(jnp.concatenate([dden, dden], axis=0))], axis=0)
        dkv_part = mm_nt(lhs, q)
        hi, lo = split2(jnp.concatenate([turn, turn], axis=0))
        both = mm_nt(jnp.concatenate([hi, lo], axis=0), r_ref[:, cols])
        route_part = both[0:8, 0:64] + (both[0:8, 64:128] + both[16:24, 0:64])
        dkv[...] = dkv_part if first else dkv[...] + dkv_part
        route[...] = route_part if first else route[...] + route_part
        for k in range(TB // 512):
            at_col = TB * i + 512 * k
            piece = dmid[:, 512 * k : 512 * k + 512]
            if at_col < N1:
                own_ref[:, at_col : at_col + 512] = piece
            else:
                oth_ref[:, at_col - N1 : at_col - N1 + 512] = piece.astype(BF)

    for i in range(N2 // TB):
        step(i, i == 0)

    m = (m_ref[...].astype(F32) + mo_ref[...].astype(F32)).astype(BF)
    for k in range(16):
        rows = slice(64 * k, 64 * k + 64)
        pieces_ref[k, 0:64, :] = gw1[rows, :].astype(BF)
        pieces_ref[k, 64:128, :] = gw2[rows, :].astype(BF)
        pieces_ref[k, 128:144, 0:128] = m[16 * k : 16 * k + 16]
        pieces_ref[k, 128:144, 128:256] = jnp.zeros((16, 128), BF)
    parts = pack_heads(dkv[0:D, :] + dkv[D : 2 * D, :])
    r = lax.broadcasted_iota(jnp.int32, (8, D), 0)
    c = lax.broadcasted_iota(jnp.int32, (8, D), 1) // HD
    sums = jnp.where(r == c, dkv[2 * D : 2 * D + 8, :] + dkv[2 * D + 16 : 2 * D + 24, :], 0.0)
    last = [jnp.concatenate([route[...], jnp.zeros((8, 64), F32)], axis=1), jnp.zeros((8, 128), F32)]
    halves = [jnp.concatenate([parts[g], sums[:, 128 * g : 128 * g + 128], last[g]], axis=0) for g in range(2)]
    keep_msg[...], send_msg[...] = ordered(core, *halves)


def expert_call(at, msg, m, m_o, tokt, tokt_o, q, q_o, dy, df, back, g, r, w_in, wint):
    return call(
        expert_kernel,
        (
            struct((D, N1), F32), struct((D, N1), BF), struct((D, D), F32), struct((8, D), F32),
            struct((48, 128), F32), struct((48, 128), F32), struct((16, 144, D), BF),
        ),
        6e9, 12e6, "expert",
        [pltpu.VMEM((FH, D), F32)] * 2 + [pltpu.VMEM((2 * D + 32, D), F32), pltpu.VMEM((8, 64), F32)],
        limit=LIMIT,
    )(at, msg, m, m_o, tokt, tokt_o, q, q_o, dy, df, back, g, r, w_in, wint)


def dmid_kernel(at_ref, own_ref, oth_ref, msg_ref, msgo_ref, *out_refs):
    hi, lo = split2(msg_ref[...] + msgo_ref[...])
    for d, ref in enumerate(out_refs):
        cols = pl.ds(pl.multiple_of(lax.rem(at_ref[2] + d, 4) * 256, 256), 256)
        ref[0:256, :] = (own_ref[:, cols] + oth_ref[:, cols].astype(F32)).astype(ref.dtype)
        ref[256:304, 0:128] = hi.astype(ref.dtype)
        ref[256:304, 128:256] = lo.astype(ref.dtype)


def dmid_call(at, own, oth, msg, msg_o):
    return call(dmid_kernel, (struct((304, 256), F32),) + (struct((304, 256), BF),) * 3, 1e6, 2e6, "dmid_pieces")(at, own, oth, msg, msg_o)


def back_query_kernel(
    at_ref, d0, d1, d2, d3, kvt_ref, ks_ref, tokt_ref, q_ref, qslope_ref, wq_ref, gx_ref, gq_ref, dmid_ref
):
    for d, ref in enumerate((d0, d1, d2, d3)):
        cols = pl.ds(pl.multiple_of(lax.rem(at_ref[2] + 4 - d, 4) * 256, 256), 256)
        dmid_ref[:, cols] = ref[...].astype(F32)
    dmid = dmid_ref[...]
    q = q_ref[...]
    tokt = tokt_ref[...]
    kvt = kvt_ref[...]
    kvth, kvtl = split2(kvt)
    kvh, kvl = split2(kvt.T)
    ks = ks_ref[0:1, :]
    mask = head_mask(D, D)
    ksh, ksl = split2(jnp.where(mask, ks, 0.0))
    kch, kcl = split2(jnp.where(mask, column_of(ks), 0.0))
    both = mm(jnp.concatenate([kvth, kvtl, ksh, ksl], axis=0), q)
    rden = 1.0 / (both[2 * D : 3 * D] + both[3 * D :])
    attn = (both[:D] + both[D : 2 * D]) * rden
    dnum = dmid * rden
    nh, nl = split2(dnum)
    zh, zl = split2(dnum * attn)
    left = jnp.concatenate([kvh, -kch], axis=1)
    both = mm(jnp.concatenate([left, jnp.concatenate([kvl, -kcl], axis=1)], axis=0), jnp.concatenate([nh, zh], axis=0))
    dq = both[:D] + both[D:] + mm(left, jnp.concatenate([nl, zl], axis=0))
    wq = wq_ref[...]
    dqp = (dq * qslope_ref[...]).astype(BF)
    gx_ref[...] = dmid + mm(wq, dqp)
    gq_ref[...] = mm_nt(tokt, dqp)


def back_query_call(at, dm, kvt, ks, tokt, q, qslope, wq, after):
    out = (struct((D, N1), F32), struct((D, D), F32))
    return call(back_query_kernel, out, 2e9, 5e6, "back_query", [pltpu.VMEM((D, N1), F32)], after)(
        at, *dm, kvt, ks, tokt, q, qslope, wq
    )


def back_keys_kernel(at_ref, msg_ref, msgo_ref, km_ref, v_ref, slope_ref, tokt_ref, gq_ref, dk_ref, dv_ref, keep_ref, send_ref):
    core = at_ref[0]
    halves = ordered(core, msg_ref[...], msgo_ref[...])
    dkvt = heads_of(halves)
    dks = jnp.sum(row_of(halves), axis=0, keepdims=True)
    hi, lo = split2(dkvt.T)
    v = v_ref[...]
    dk = mm(hi, v) + mm(lo, v) + column_of(dks)
    dk = (dk * slope_ref[...]).astype(BF)
    hi, lo = split2(dkvt)
    km = km_ref[...]
    dk_ref[...] = dk
    dv_ref[...] = (mm(hi, km) + mm(lo, km)).astype(BF)
    for ref, part in ((keep_ref, core), (send_ref, 1 - core)):
        rows = pl.ds(pl.multiple_of(part * 128, 128), 128)
        ref[:, 0:D] = gq_ref[rows, :].astype(ref.dtype)
        ref[:, D : 2 * D] = mm_nt(tokt_ref[rows, 0:N1], dk).astype(ref.dtype)


def back_keys_call(at, msg, msg_o, km, v, slope, tokt, gq):
    out = (struct((D, N1), BF), struct((D, N1), BF), struct((128, 2 * D), F32), struct((128, 2 * D), BF))
    return call(back_keys_kernel, out, 1e9, 4e6, "back_keys")(at, msg, msg_o, km, v, slope, tokt, gq)


def grad_x_kernel(at_ref, gx_ref, dk_ref, dv_ref, wk_ref, wv_ref, out_ref):
    total = gx_ref[...] + mm(wk_ref[...], dk_ref[...]) + mm(wv_ref[...], dv_ref[...])
    out_ref[...] = total.T.astype(BF)


def grad_x_call(at, gx, dk, dv, wk, wv):
    return call(grad_x_kernel, (struct((N1, D), BF),), 3e8, 3e6, "grad_x")(at, gx, dk, dv, wk, wv)[0]


def place_kernel(at_ref, own_ref, oth_ref, gin_ref, gout_ref):
    def put(ref, part):
        cols = slice(128 * part, 128 * part + 128)
        gin_ref[0] = jnp.concatenate([ref[k, 0:64, cols].astype(F32) for k in range(16)], axis=0).T
        for k in range(8):
            gout_ref[0, 64 * k : 64 * k + 64, :] = ref[8 * part + k, 64:128, :].astype(F32)

    step = pl.program_id(0)
    for s in range(4):
        pl.when(step == s)(lambda s=s: put(own_ref if s < 2 else oth_ref, s % 2))


def place_call(at, own, oth):
    expert = lambda i, at: jnp.where(i < 2, at[0], 1 - at[0])
    out = pl.BlockSpec((1, 128, FH), lambda i, at: (expert(i, at), lax.rem(i, 2), 0))
    out2 = pl.BlockSpec((1, 512, D), lambda i, at: (expert(i, at), lax.rem(i, 2), 0))
    return pl.pallas_call(
        place_kernel,
        grid_spec=pltpu.PrefetchScalarGridSpec(
            num_scalar_prefetch=1,
            grid=(4,),
            in_specs=[pl.BlockSpec(memory_space=pltpu.VMEM)] * 2,
            out_specs=[out, out2],
        ),
        out_shape=(struct((2, D, FH), F32), struct((2, FH, D), F32)),
        compiler_params=pltpu.CompilerParams(vmem_limit_bytes=32 * 1024 * 1024),
        cost_estimate=pl.CostEstimate(flops=1000000, bytes_accessed=7000000, transcendentals=0),
        name="place_experts",
    )(at, own, oth)


def place_m_kernel(at_ref, msg_ref, msgo_ref, own_ref, oth_ref, gv_ref, route_ref):
    core, y = at_ref[0], at_ref[2]
    halves = ordered(core, msg_ref[...], msgo_ref[...])
    hi, lo = split2(heads_of(halves).T)
    own = jnp.concatenate([own_ref[k, 128:144, 0:128].astype(F32) for k in range(16)], axis=0)
    oth = jnp.concatenate([oth_ref[k, 128:144, 0:128].astype(F32) for k in range(16)], axis=0)
    m = jnp.concatenate(ordered(core, own, oth), axis=1).astype(BF)
    gv_ref[...] = mm(m, hi) + mm(m, lo)
    sums = halves[0][40:48, 0:64]
    at_row = lax.broadcasted_iota(jnp.int32, sums.shape, 0)
    for e in range(2):
        route_ref[e : e + 1, :] = jnp.sum(jnp.where(at_row == 2 * y + e, sums, 0.0), axis=0, keepdims=True)


def place_m_call(at, msg, msg_o, own, oth):
    out = (struct((D, D), F32), struct((2, 64), F32))
    return call(place_m_kernel, out, 1e8, 1e6, "grad_wv")(at, msg, msg_o, own, oth)


def place_proj_kernel(at_ref, own_ref, oth_ref, gq_ref, gk_ref):
    core = at_ref[0]
    for ref, part in ((own_ref, core), (oth_ref, 1 - core)):
        rows = pl.ds(pl.multiple_of(part * 128, 128), 128)
        gq_ref[rows, :] = ref[:, 0:D].astype(F32)
        gk_ref[rows, :] = ref[:, D : 2 * D].astype(F32)


def place_proj_call(at, own, oth):
    return call(place_proj_kernel, (struct((D, D), F32),) * 2, 1e6, 1e6, "place_projections")(at, own, oth)


def swap_core(v):
    return lax.ppermute(v, "pts", [(i, i ^ 1) for i in range(32)])


def to_x(v, d):
    return lax.ppermute(v, "pts", [(i, (i & ~6) | ((i + 2 * d) & 6)) for i in range(32)])


def to_z(v, d):
    return lax.ppermute(v, "pts", [(i, (i + 8 * d) % 32) for i in range(32)])


def to_y(v, d):
    return lax.ppermute(v, "exp", [(i, (i + d) % 4) for i in range(4)])


def star(v, to):
    return [to(v, d) for d in (1, 2, 3)]


CHIPS = [[2 * k + core for k in range(16)] for core in range(2)]


def exchange(v):
    return lax.all_to_all(v, "pts", 0, 0, axis_index_groups=CHIPS)


def on_device(
    tokens, coords, keep, cotangent, w_query, w_key, w_value, w_geo, b_geo, w_route, w_in, w_out
):
    pts = lax.axis_index("pts")
    y = lax.axis_index("exp")
    core = pts % 2
    at = jnp.stack([core, 2 * y + core, y]).astype(jnp.int32)

    tokens_o, cot_o = swap_core(tokens), swap_core(cotangent)
    ck, msg, m, m_away, tokt, wqt = keys_call(at, tokens, keep[None, :], coords, w_key, w_value, w_query)
    ck_o, m_o = swap_core(ck), swap_core(m_away)
    q = query_call(at, tokt, wqt)
    tokt_o, q_o = query_other_call(at, tokens_o, wqt)
    r, g = gate_call(at, w_geo, b_geo[None, :], w_route.T, ck, ck_o)
    dy, df, back, wint = back_call(at, cotangent, cot_o, ck, ck_o, g, w_in, w_out)

    msg = add([msg, swap_core(msg)], (), F32)
    msg = add([msg] + star(msg, to_x), (q, g), F32)
    msg = add([msg] + star(msg, to_z), (back, q_o), F32)
    own, oth, kvt, ks, msg2, msg2_away, pieces = expert_call(
        at, msg, m, m_o, tokt, tokt_o, q, q_o, dy, df, back, g, r, w_in, wint
    )

    pieces = exchange(pieces)

    p0, p1, p2, p3 = dmid_call(at, own, swap_core(oth), msg2, swap_core(msg2_away))
    arrived = [p0, to_y(p1, 1), to_y(p2, 2), to_y(p3, 3)]
    msg2 = add([p[256:, :128] for p in arrived] + [p[256:, 128:] for p in arrived], (), F32)
    dm = add([p[:256] for p in arrived], (), BF)
    dm = [dm] + star(dm, to_y)
    msg2 = msg2_z = add([msg2] + star(msg2, to_z), (), F32)

    pieces = chips_call(at, pieces, (msg2_z,))
    around = star(msg2, to_x)
    pieces, *dm = lax.optimization_barrier((pieces, *dm))
    tokt, q, qslope, km, v, slope = again_call(at, tokens, keep[None, :], w_query, w_key, w_value, (pieces,))
    pieces = exchange(pieces)

    gx, gq = back_query_call(at, dm, kvt, ks, tokt, q, qslope, w_query, ())
    msg2 = add([msg2] + around, (), F32)
    msg2_o = swap_core(msg2)
    dk, dv, part, away = back_keys_call(at, msg2, msg2_o, km, v, slope, tokt, gq)
    grad_x = grad_x_call(at, gx, dk, dv, w_key, w_value)

    part = add([part, swap_core(away)])
    part = add([part] + star(part, to_z), (grad_x,))
    pieces, _ = lax.optimization_barrier((pieces, part))
    pieces_o = swap_core(pieces)
    grad_w_in, grad_w_out = place_call(at, pieces, pieces_o)
    grad_wv, grad_route = place_m_call(at, msg2, msg2_o, pieces, pieces_o)
    part = add([part] + star(part, to_x), (grad_w_in, grad_wv))
    grad_wq, grad_wk = place_proj_call(at, part, swap_core(part))
    return (grad_x, grad_wq, grad_wk, grad_wv, grad_w_in, grad_w_out, grad_route.T)


def solution(mesh):
    in_specs = (
        P("pts", None),
        P(None, "pts"),
        P("pts"),
        P("pts", None),
        P(),
        P(),
        P(),
        P(),
        P(),
        P(),
        P("exp", None, None),
        P("exp", None, None),
    )
    out_specs = (
        P("pts", None),
        P(),
        P(),
        P(),
        P("exp", None, None),
        P("exp", None, None),
        P(None, "exp"),
    )
    return jax.shard_map(
        on_device, mesh=mesh, in_specs=in_specs, out_specs=out_specs, check_vma=False
    )
```
